32 devices in a mesh: outer: 8 (over z, core), inner: 4 (over y, x).
Axes of the slice: x: 2, y: 2, z: 4, core: 2. Of those that a mesh axis runs over, the one named last changes fastest.
Arguments:
- queries: bfloat16 [4096, 32, 128], P(('outer', 'inner')), may hold values from -8 to 8
- keys: bfloat16 [4096, 4, 128], P(('outer', 'inner')), may hold values from -8 to 8
- values: bfloat16 [4096, 4, 128], P(('outer', 'inner')), may hold values from -6 to 6
- positions: int32 [4096], P(('outer', 'inner')), may hold values from 0 to 4095, as said below
Outputs:
- attended: bfloat16 [4096, 32, 128], P(('outer', 'inner'))
The draws below stay inside these ranges and needn't reach their ends.
Inputs may be any that keep to these rules, and one draw needn't show every extreme that they name: positions is a permutation of the numbers 0 to 4095 made of runs of 64 consecutive ascending positions starting at multiples of 64; runs are laid out in an order drawn from the seed.
All inputs are finite; a program needn't handle non-finite values.
Results may differ from the reference program's by a relative error of at most 0.0045.
Values may be sent and summed in bfloat16 or wider, within the bound.
No kernel may reach another device: no remote copies, remote signals or barrier semaphores. Data moves between devices by JAX's collectives and lax.ppermute only.
A program may use at most 128 MiB of HBM per device.

```python
import jax
import jax.numpy as jnp
from jax import lax

QH = 32
KVH = 4
HD = 128
RUN = 64
TOKENS = 4096


def draw_queries(key, part):
    key = jax.random.fold_in(key, 11)
    base = jax.random.truncated_normal(key, -8.0, 8.0, (TOKENS, QH, HD), jnp.float32)
    return base.astype(jnp.bfloat16)


def draw_keys(key, part):
    key = jax.random.fold_in(key, 23)
    base = jax.random.truncated_normal(key, -8.0, 8.0, (TOKENS, KVH, HD), jnp.float32)
    return base.astype(jnp.bfloat16)


def draw_positions(key, part):
    key = jax.random.fold_in(key, 37)
    order = jax.random.permutation(key, TOKENS // RUN).astype(jnp.int32)
    steps = jnp.arange(RUN, dtype=jnp.int32)
    return (order[:, None] * RUN + steps[None, :]).reshape(TOKENS).astype(jnp.int32)


def level_of(own_key, extent, cuts, smallest, largest):
    def one(axis_at, shards_of):
        steps = jax.random.uniform(jax.random.fold_in(jax.random.fold_in(own_key, 6), axis_at), (shards_of,), jnp.float32, smallest / len(cuts), largest / len(cuts))
        return jnp.repeat(jnp.exp(steps), extent[axis_at] // shards_of).reshape((-1,) + (1,) * (len(extent) - axis_at - 1))

    gain = one(*cuts[0])
    for cut in cuts[1:]:
        gain = gain * one(*cut)
    return gain


def scatter_about(stream_key, dims, scale, reach, cuts=(), kind=jnp.bfloat16):
    result = scale * jax.random.normal(stream_key, dims, jnp.float32)
    if cuts:
        result = result * level_of(stream_key, dims, cuts, -0.22, 0.18)
    return jnp.clip(result, -reach, reach).astype(kind)


def setup_inputs(seed: int = 0) -> dict:
    key_of = jax.random.split(jax.random.key(seed), 5)
    return {
        "queries": draw_queries(jax.random.fold_in(key_of[4], 71), 0),
        "keys": draw_keys(jax.random.fold_in(key_of[4], 71), 0),
        "values": scatter_about(key_of[2], (TOKENS, KVH, HD), 1.0, 6.0, ((0, 32),)),
        "positions": draw_positions(jax.random.fold_in(key_of[4], 71), 0),
    }


def reference(queries, keys, values, positions):
    whole = queries.shape[0]
    half = whole // 2
    block = min(512, half)
    group = QH // KVH
    scale = 1.0 / (HD ** 0.5)
    order = jnp.zeros((whole,), jnp.int32).at[positions].set(jnp.arange(whole, dtype=jnp.int32))
    sorted_q = queries[order]
    sorted_k = keys[order]
    sorted_v = values[order]

    def one_block(index):
        start = (index * block).astype(jnp.int32)
        base = ((start // half) * half).astype(jnp.int32)
        qblk = lax.dynamic_slice_in_dim(sorted_q, start, block, 0).astype(jnp.float32)
        qblk = qblk.reshape(block, KVH, group, HD)
        kblk = lax.dynamic_slice_in_dim(sorted_k, base, half, 0).astype(jnp.float32)
        vblk = lax.dynamic_slice_in_dim(sorted_v, base, half, 0).astype(jnp.float32)
        qidx = start + jnp.arange(block, dtype=jnp.int32)
        kidx = base + jnp.arange(half, dtype=jnp.int32)
        live = kidx[None, :] <= qidx[:, None]

        def one_head(head):
            qh = qblk[:, head]
            score = jnp.einsum("qjd,kd->jqk", qh, kblk[:, head]) * scale
            score = jnp.where(live[None], score, -1e30)
            top = jnp.max(score, axis=-1, keepdims=True)
            weight = jnp.where(live[None], jnp.exp(score - top), 0.0)
            total = jnp.sum(weight, axis=-1)
            weight_b = lax.optimization_barrier(weight.astype(jnp.bfloat16))
            mixed = jnp.einsum("jqk,kd->jqd", weight_b.astype(jnp.float32), vblk[:, head])
            return mixed / total[..., None]

        heads = lax.map(one_head, jnp.arange(KVH, dtype=jnp.int32))
        return jnp.transpose(heads, (2, 0, 1, 3)).reshape(block, QH, HD).astype(jnp.bfloat16)

    out_sorted = lax.map(one_block, jnp.arange(whole // block, dtype=jnp.int32))
    out_sorted = out_sorted.reshape(whole, QH, HD)
    return out_sorted[positions]
```

```python
import functools
import math

import jax
import jax.numpy as jnp
from jax import lax
from jax.experimental import pallas as pl
from jax.experimental.pallas import tpu as pltpu
from jax.sharding import PartitionSpec as P

RUN = 64
TILE = 4
DEAD = 1 << 20


def flash(q, k, v, state, mask, factor):
    top, total, mixed = state
    score = lax.dot_general(
        q, k, (((1,), (1,)), ((), ())), preferred_element_type=jnp.float32
    )
    score = mask(score)
    parts = [score[:, c : c + 128] for c in range(0, score.shape[1], 128)]
    new = functools.reduce(jnp.maximum, parts)
    new = jnp.max(new, axis=1, keepdims=True)
    if top is None:
        new = jnp.broadcast_to(new, parts[0].shape)
    else:
        new = jnp.maximum(top, new)
    weights = [jnp.exp2((part - new) * factor) for part in parts]
    part_total = functools.reduce(jnp.add, weights)
    part_mixed = lax.dot_general(
        jnp.concatenate([w.astype(jnp.bfloat16) for w in weights], axis=1),
        v,
        (((1,), (0,)), ((), ())),
        preferred_element_type=jnp.float32,
    )
    if top is None:
        return new, part_total, part_mixed
    decay = jnp.exp2((top - new) * factor)
    return new, total * decay + part_total, mixed * decay + part_mixed


def attend_kernel(
    group, factor, runs, half,
    ids, own_ids, q_ref, own_ref, kv_ref, out_ref,
    lists, top_ref, total_ref, mixed_ref, buf, sems,
):
    heads_kv = q_ref.shape[1]
    rows = q_ref.shape[2]
    run_rows = 2 * heads_kv * RUN

    def note(r, counts):
        key_run = ids[r]
        fresh = []
        for a in range(2):
            mine = own_ids[a]
            seen = (key_run < mine) & ((key_run >= half) == (mine >= half))
            lists[a, counts[a]] = r
            fresh.append(counts[a] + seen.astype(jnp.int32))
        return tuple(fresh)

    counts = lax.fori_loop(0, runs, note, (jnp.int32(0), jnp.int32(0)))
    tiles = [(n + TILE - 1) // TILE for n in counts]
    every = tiles[0] + tiles[1]

    def place(item):
        second = item >= tiles[0]
        a = second.astype(jnp.int32)
        first = (item - jnp.where(second, tiles[0], 0)) * TILE
        return a, first, jnp.where(second, counts[1], counts[0])

    def copies(item, slot):
        a, first, n = place(item)
        found = []
        for s in range(TILE):
            r = lists[a, jnp.minimum(first + s, n - 1)]
            start = pl.multiple_of((r % 2) * run_rows, run_rows)
            found.append(
                pltpu.make_async_copy(
                    kv_ref.at[r // 2, pl.ds(start, run_rows), :],
                    buf.at[slot, s],
                    sems.at[slot, s],
                )
            )
        return found

    @pl.when(every > 0)
    def _():
        for copy in copies(jnp.int32(0), 0):
            copy.start()

    row_at = lax.broadcasted_iota(jnp.int32, (rows, 2 * RUN), 0) // group
    col_at = lax.broadcasted_iota(jnp.int32, (rows, 2 * RUN), 1)
    for a in range(2):
        mine, other = own_ids[a], own_ids[1 - a]
        seen = (other < mine) & ((other >= half) == (mine >= half))
        reach = jnp.where(seen, RUN, 0)
        if a == 0:
            live = (col_at <= row_at) | ((col_at >= RUN) & (col_at < RUN + reach))
        else:
            live = (col_at < reach) | ((col_at >= RUN) & (col_at - RUN <= row_at))
        for h in range(heads_kv):
            top, total, mixed = flash(
                q_ref[a, h],
                own_ref[:, h].reshape(2 * RUN, -1),
                own_ref[:, heads_kv + h].reshape(2 * RUN, -1),
                (None, None, None),
                lambda score: jnp.where(live, score, -jnp.inf),
                factor,
            )
            top_ref[a, h], total_ref[a, h], mixed_ref[a, h] = top, total, mixed

    col = lax.broadcasted_iota(jnp.int32, (8, TILE * RUN), 1)

    def step(item, carry):
        slot = item % 2
        for copy in copies(item, slot):
            copy.wait()

        @pl.when(item + 1 < every)
        def _():
            for copy in copies(item + 1, 1 - slot):
                copy.start()

        a, first, n = place(item)
        bias = jnp.where(col < (n - first) * RUN, 0.0, -jnp.inf)[:1]
        for h in range(heads_kv):
            k = buf[slot, :, h * RUN : (h + 1) * RUN, :]
            v = buf[slot, :, (heads_kv + h) * RUN : (heads_kv + h + 1) * RUN, :]
            top, total, mixed = flash(
                q_ref[a, h],
                k.reshape(TILE * RUN, -1),
                v.reshape(TILE * RUN, -1),
                (top_ref[a, h], total_ref[a, h], mixed_ref[a, h]),
                lambda score: score + bias,
                factor,
            )
            top_ref[a, h], total_ref[a, h], mixed_ref[a, h] = top, total, mixed
        return carry

    lax.fori_loop(0, every, step, 0)

    for a in range(2):
        for h in range(0, heads_kv, 2):
            done = []
            for g in (h, h + 1):
                total = jnp.sum(total_ref[a, g], axis=1, keepdims=True)
                done.append((mixed_ref[a, g] / total).reshape(RUN, group, -1))
            out_ref[a * RUN : (a + 1) * RUN, h * group : (h + 2) * group, :] = (
                jnp.concatenate(done, axis=1).astype(out_ref.dtype)
            )


def per_device(queries, keys, values, positions):
    outer, inner = lax.axis_size("outer"), lax.axis_size("inner")
    devices = outer * inner
    tokens, heads_q, head_dim = queries.shape
    heads_kv = keys.shape[1]
    group = heads_q // heads_kv
    runs = tokens // RUN * devices
    me = lax.axis_index("outer") * inner + lax.axis_index("inner")

    kv = jnp.concatenate(
        [x.reshape(2, RUN, heads_kv, head_dim) for x in (keys, values)], axis=2
    ).transpose(0, 2, 1, 3)
    numbers = (positions // RUN).astype(jnp.bfloat16)
    packed = jnp.concatenate(
        [
            kv.reshape(-1, head_dim),
            jnp.broadcast_to(numbers[None, :], (16, head_dim)),
        ]
    )
    gathered = lax.all_gather(packed, ("outer", "inner"), axis=0)
    q = (
        queries.reshape(2, RUN, heads_kv, group, head_dim)
        .transpose(0, 2, 1, 3, 4)
        .reshape(2, heads_kv, RUN * group, head_dim)
    )
    own_ids = (positions[::RUN] // RUN).astype(jnp.int32)
    ids = gathered[:, -16, ::RUN].astype(jnp.int32)
    ids = jnp.where(jnp.arange(devices)[:, None] == me, DEAD, ids).reshape(runs)

    factor = math.log2(math.e) / math.sqrt(head_dim)
    work = 2 * runs * RUN * tokens * heads_q * head_dim // 2
    vmem = pl.BlockSpec(memory_space=pltpu.VMEM)
    return pl.pallas_call(
        functools.partial(attend_kernel, group, factor, runs, runs // 2),
        out_shape=jax.ShapeDtypeStruct(queries.shape, queries.dtype),
        grid_spec=pltpu.PrefetchScalarGridSpec(
            num_scalar_prefetch=2,
            grid=(),
            in_specs=[vmem, vmem, pl.BlockSpec(memory_space=pl.ANY)],
            out_specs=vmem,
            scratch_shapes=[
                pltpu.SMEM((2, runs + 1), jnp.int32),
                pltpu.VMEM((2, heads_kv, RUN * group, 128), jnp.float32),
                pltpu.VMEM((2, heads_kv, RUN * group, 128), jnp.float32),
                pltpu.VMEM((2, heads_kv, RUN * group, head_dim), jnp.float32),
                pltpu.VMEM((2, TILE, 2 * heads_kv * RUN, head_dim), jnp.bfloat16),
                pltpu.SemaphoreType.DMA((2, TILE)),
            ],
        ),
        compiler_params=pltpu.CompilerParams(vmem_limit_bytes=40 * 1024 * 1024),
        cost_estimate=pl.CostEstimate(
            flops=work, bytes_accessed=gathered.size * 2, transcendentals=0
        ),
        name="attend",
    )(ids, own_ids, q, kv, gathered)


def solution(mesh):
    in_specs = (
        P(("outer", "inner"), None, None),
        P(("outer", "inner"), None, None),
        P(("outer", "inner"), None, None),
        P(("outer", "inner")),
    )
    out_specs = P(("outer", "inner"), None, None)
    return jax.shard_map(
        per_device, mesh=mesh, in_specs=in_specs, out_specs=out_specs, check_vma=False
    )
```

```python
import functools
import math

import jax
import jax.numpy as jnp
from jax import lax
from jax.experimental import pallas as pl
from jax.experimental.pallas import tpu as pltpu
from jax.sharding import PartitionSpec as P

RUN = 64
TILE = 4
AXES = ("outer", "inner")


def flash(q, k, v, state, mask, factor):
    top, total, mixed = state
    score = lax.dot_general(
        q, k, (((1,), (1,)), ((), ())), preferred_element_type=jnp.float32
    )
    score = mask(score)
    parts = [score[:, c : c + 128] for c in range(0, score.shape[1], 128)]
    new = functools.reduce(jnp.maximum, parts)
    new = jnp.max(new, axis=1, keepdims=True)
    if top is None:
        new = jnp.broadcast_to(new, parts[0].shape)
    else:
        new = jnp.maximum(top, new)
    weights = [jnp.exp2((part - new) * factor) for part in parts]
    part_total = functools.reduce(jnp.add, weights)
    part_mixed = lax.dot_general(
        jnp.concatenate([w.astype(jnp.bfloat16) for w in weights], axis=1),
        v,
        (((1,), (0,)), ((), ())),
        preferred_element_type=jnp.float32,
    )
    if top is None:
        return new, part_total, part_mixed
    decay = jnp.exp2((top - new) * factor)
    return new, total * decay + part_total, mixed * decay + part_mixed


def attend_kernel(group, factor, half, first, last, blocks, own_ids, q_ref, *refs):
    heads_kv = q_ref.shape[1]
    rows = q_ref.shape[2]
    run_rows = 2 * heads_kv * RUN
    kv_refs, refs = refs[:blocks], refs[blocks:]
    if first:
        own_ref, refs = refs[0], refs[1:]
    else:
        refs = refs[3:]
    if last:
        out_ref, refs = refs[0], refs[1:]
    top_ref, total_ref, mixed_ref, buf = refs

    if first:
        row_at = lax.broadcasted_iota(jnp.int32, (rows, 2 * RUN), 0) // group
        col_at = lax.broadcasted_iota(jnp.int32, (rows, 2 * RUN), 1)
        for a in range(2):
            mine, other = own_ids[a], own_ids[1 - a]
            seen = (other < mine) & ((other >= half) == (mine >= half))
            reach = jnp.where(seen, RUN, 0)
            if a == 0:
                live = (col_at <= row_at) | ((col_at >= RUN) & (col_at < RUN + reach))
            else:
                live = (col_at < reach) | ((col_at >= RUN) & (col_at - RUN <= row_at))
            for h in range(heads_kv):
                k, v = (
                    jnp.concatenate(
                        [
                            own_ref[r * run_rows + g * RUN : r * run_rows + (g + 1) * RUN]
                            for r in range(2)
                        ]
                    )
                    for g in (h, heads_kv + h)
                )
                top_ref[a, h], total_ref[a, h], mixed_ref[a, h] = flash(
                    q_ref[a, h],
                    k,
                    v,
                    (None, None, None),
                    lambda score: jnp.where(live, score, -jnp.inf),
                    factor,
                )

    flags = [[], []]
    for start in range(0, blocks, 8):
        some = kv_refs[start : start + 8]
        ids = jnp.concatenate([ref[2 * run_rows :] for ref in some]).astype(jnp.float32)
        row = lax.broadcasted_iota(jnp.int32, ids.shape, 0)
        lane = lax.broadcasted_iota(jnp.int32, ids.shape, 1)
        bit = jnp.left_shift(1, 2 * (row // 16) + lane // RUN)
        bit = jnp.where((row % 16 == 0) & (lane % RUN == 0), bit, 0).astype(jnp.float32)
        for a in range(2):
            mine = own_ids[a].astype(jnp.float32)
            low = jnp.where(mine >= half, float(half), 0.0)
            seen = (ids < mine) & (ids >= low)
            bits = jnp.sum(jnp.where(seen, bit, 0.0)).astype(jnp.int32)
            flags[a] += [(bits >> n) & 1 for n in range(2 * len(some))]

    col = lax.broadcasted_iota(jnp.int32, (8, TILE * RUN), 1)
    for a in range(2):
        count = jnp.int32(0)
        for n in range(2 * blocks):

            @pl.when(flags[a][n] == 1)
            def _():
                at = (n % 2) * run_rows
                buf[a, count] = kv_refs[n // 2][at : at + run_rows]

            count = count + flags[a][n]
        for s in range(TILE - 1):
            buf[a, count + s] = jnp.zeros(buf.shape[2:], buf.dtype)

        def step(item, carry):
            bias = jnp.where(col < (count - item * TILE) * RUN, 0.0, -jnp.inf)[:1]
            runs = pl.ds(item * TILE, TILE)
            for h in range(heads_kv):
                k = buf[a, runs, h * RUN : (h + 1) * RUN, :]
                v = buf[a, runs, (heads_kv + h) * RUN : (heads_kv + h + 1) * RUN, :]
                top_ref[a, h], total_ref[a, h], mixed_ref[a, h] = flash(
                    q_ref[a, h],
                    k.reshape(TILE * RUN, -1),
                    v.reshape(TILE * RUN, -1),
                    (top_ref[a, h], total_ref[a, h], mixed_ref[a, h]),
                    lambda score: score + bias,
                    factor,
                )
            return carry

        lax.fori_loop(0, (count + TILE - 1) // TILE, step, 0)

    if last:
        for a in range(2):
            for h in range(0, heads_kv, 2):
                done = []
                for g in (h, h + 1):
                    total = jnp.sum(total_ref[a, g], axis=1, keepdims=True)
                    done.append((mixed_ref[a, g] / total).reshape(RUN, group, -1))
                out_ref[a * RUN : (a + 1) * RUN, h * group : (h + 2) * group, :] = (
                    jnp.concatenate(done, axis=1).astype(out_ref.dtype)
                )


def attend(own_ids, q, kvs, own, state, out, group, half, factor):
    first, last, blocks = own is not None, out is not None, len(kvs)
    operands = [q, *kvs] + ([own] if first else list(state))
    lanes = jax.ShapeDtypeStruct(q.shape[:3] + (128,), jnp.float32)
    carried = [lanes, lanes, jax.ShapeDtypeStruct(q.shape, jnp.float32)]
    vmem = pl.BlockSpec(memory_space=pltpu.VMEM)
    shapes = ([out] if last else []) + carried
    aliases = {}
    if not first:
        aliases = {2 + blocks + n: int(last) + n for n in range(3)}
    run_rows = 2 * q.shape[1] * RUN
    results = pl.pallas_call(
        functools.partial(attend_kernel, group, factor, half, first, last, blocks),
        out_shape=shapes,
        grid_spec=pltpu.PrefetchScalarGridSpec(
            num_scalar_prefetch=1,
            grid=(),
            in_specs=[vmem] * len(operands),
            out_specs=[vmem] * len(shapes),
            scratch_shapes=[
                pltpu.VMEM((2, 2 * blocks + TILE - 1, run_rows, q.shape[3]), q.dtype)
            ],
        ),
        input_output_aliases=aliases,
        compiler_params=pltpu.CompilerParams(vmem_limit_bytes=24 * 1024 * 1024),
        cost_estimate=pl.CostEstimate(
            flops=blocks * RUN * q.size * 4, bytes_accessed=q.size * 16, transcendentals=0
        ),
        name="attend",
    )(own_ids, *operands)
    return results[0] if last else results


def per_device(queries, keys, values, positions):
    outer, inner = lax.axis_size("outer"), lax.axis_size("inner")
    tokens, heads_q, head_dim = queries.shape
    heads_kv = keys.shape[1]
    group = heads_q // heads_kv
    half = tokens // RUN * outer * inner // 2
    factor = math.log2(math.e) / math.sqrt(head_dim)

    chips = outer // 2
    ring = list(range(inner // 2)) + list(range(inner - 1, inner // 2 - 1, -1))
    after = {ring[n]: ring[(n + 1) % inner] for n in range(inner)}
    before = {there: here for here, there in after.items()}

    def permute(x, to):
        pairs = []
        for z in range(chips):
            for core in range(2):
                for place in range(inner):
                    nz, ncore, nplace = to(z, core, place)
                    pairs.append(
                        (
                            (2 * z + core) * inner + place,
                            (2 * nz + ncore) * inner + nplace,
                        )
                    )
        return lax.ppermute(x, AXES, pairs)

    def along_z(x, step):
        return permute(x, lambda z, core, place: ((z + step) % chips, core, place))

    def around(x):
        return permute(
            x, lambda z, core, place: (z, core, (before if core else after)[place])
        )

    def other_core(x):
        return permute(x, lambda z, core, place: (z, 1 - core, place))

    kv = jnp.concatenate(
        [x.reshape(2, RUN, heads_kv, head_dim) for x in (keys, values)], axis=2
    ).transpose(0, 2, 1, 3)
    numbers = (positions // RUN).astype(jnp.bfloat16)
    own = jnp.concatenate(
        [
            kv.reshape(-1, head_dim),
            jnp.broadcast_to(numbers[None, :], (16, head_dim)),
        ]
    )
    own_ids = (positions[::RUN] // RUN).astype(jnp.int32)
    q = (
        queries.reshape(2, RUN, heads_kv, group, head_dim)
        .transpose(0, 2, 1, 3, 4)
        .reshape(2, heads_kv, RUN * group, head_dim)
    )

    starts = [own] + [along_z(own, step) for step in range(1, chips)]
    state = None
    for n, start in enumerate(starts):
        mine = [start]
        for _ in range(inner - 1):
            mine.append(around(mine[-1]))
        theirs = [other_core(x) for x in mine]
        kvs = mine[1:] + theirs if n == 0 else mine + theirs
        last = n == chips - 1
        state = attend(
            own_ids,
            q,
            kvs,
            own if n == 0 else None,
            state,
            jax.ShapeDtypeStruct(queries.shape, queries.dtype) if last else None,
            group,
            half,
            factor,
        )
    return state


def solution(mesh):
    in_specs = (
        P(("outer", "inner"), None, None),
        P(("outer", "inner"), None, None),
        P(("outer", "inner"), None, None),
        P(("outer", "inner")),
    )
    out_specs = P(("outer", "inner"), None, None)
    return jax.shard_map(
        per_device, mesh=mesh, in_specs=in_specs, out_specs=out_specs, check_vma=False
    )
```

```python
import functools
import math

import jax
import jax.numpy as jnp
from jax import lax
from jax.experimental import pallas as pl
from jax.experimental.pallas import tpu as pltpu
from jax.sharding import PartitionSpec as P

RUN = 64
TILE = 4
AXES = ("outer", "inner")


def flash(q, k, v, state, mask, factor):
    top, total, mixed = state
    score = lax.dot_general(
        q, k, (((1,), (1,)), ((), ())), preferred_element_type=jnp.float32
    )
    score = mask(score)
    parts = [score[:, c : c + 128] for c in range(0, score.shape[1], 128)]
    new = functools.reduce(jnp.maximum, parts)
    new = jnp.max(new, axis=1, keepdims=True)
    if top is None:
        new = jnp.broadcast_to(new, parts[0].shape)
    else:
        new = jnp.maximum(top, new)
    weights = [jnp.exp2((part - new) * factor) for part in parts]
    part_total = functools.reduce(jnp.add, weights)
    part_mixed = lax.dot_general(
        jnp.concatenate([w.astype(jnp.bfloat16) for w in weights], axis=1),
        v,
        (((1,), (0,)), ((), ())),
        preferred_element_type=jnp.float32,
    )
    if top is None:
        return new, part_total, part_mixed
    decay = jnp.exp2((top - new) * factor)
    return new, total * decay + part_total, mixed * decay + part_mixed


def attend_kernel(group, factor, half, first, last, blocks, own_ids, q_ref, *refs):
    heads_kv = q_ref.shape[1]
    rows = q_ref.shape[2]
    run_rows = 2 * heads_kv * RUN
    block_rows = 2 * run_rows + 16
    kv_refs, refs = refs[: len(blocks)], refs[len(blocks) :]
    if not first:
        refs = refs[3:]
    if last:
        out_ref, refs = refs[0], refs[1:]
    top_ref, total_ref, mixed_ref, buf = refs

    if first:
        own_ref = kv_refs[0]
        row_at = lax.broadcasted_iota(jnp.int32, (rows, 2 * RUN), 0) // group
        col_at = lax.broadcasted_iota(jnp.int32, (rows, 2 * RUN), 1)
        for a in range(2):
            mine, other = own_ids[a], own_ids[1 - a]
            seen = (other < mine) & ((other >= half) == (mine >= half))
            reach = jnp.where(seen, RUN, 0)
            if a == 0:
                live = (col_at <= row_at) | ((col_at >= RUN) & (col_at < RUN + reach))
            else:
                live = (col_at < reach) | ((col_at >= RUN) & (col_at - RUN <= row_at))
            for h in range(heads_kv):
                k, v = (
                    jnp.concatenate(
                        [
                            own_ref[r * run_rows + g * RUN : r * run_rows + (g + 1) * RUN]
                            for r in range(2)
                        ]
                    )
                    for g in (h, heads_kv + h)
                )
                top_ref[a, h], total_ref[a, h], mixed_ref[a, h] = flash(
                    q_ref[a, h],
                    k,
                    v,
                    (None, None, None),
                    lambda score: jnp.where(live, score, -jnp.inf),
                    factor,
                )

    every = [
        (ref, n * block_rows)
        for at, ref in enumerate(kv_refs)
        for n in range(blocks[at])
        if not (first and at == 0 and n == 0)
    ]
    flags = [[], []]
    for start in range(0, len(every), 8):
        some = every[start : start + 8]
        ids = jnp.concatenate(
            [ref[at + 2 * run_rows : at + block_rows] for ref, at in some]
        ).astype(jnp.float32)
        row = lax.broadcasted_iota(jnp.int32, ids.shape, 0)
        lane = lax.broadcasted_iota(jnp.int32, ids.shape, 1)
        bit = jnp.left_shift(1, 2 * (row // 16) + lane // RUN)
        bit = jnp.where((row % 16 == 0) & (lane % RUN == 0), bit, 0).astype(jnp.float32)
        for a in range(2):
            mine = own_ids[a].astype(jnp.float32)
            low = jnp.where(mine >= half, float(half), 0.0)
            seen = (ids < mine) & (ids >= low)
            bits = jnp.sum(jnp.where(seen, bit, 0.0)).astype(jnp.int32)
            flags[a] += [(bits >> n) & 1 for n in range(2 * len(some))]

    col = lax.broadcasted_iota(jnp.int32, (8, TILE * RUN), 1)
    for a in range(2):
        count = jnp.int32(0)
        for n in range(2 * len(every)):

            @pl.when(flags[a][n] == 1)
            def _():
                ref, at = every[n // 2]
                at += (n % 2) * run_rows
                buf[a, count] = ref[at : at + run_rows]

            count = count + flags[a][n]
        for s in range(TILE - 1):
            buf[a, count + s] = jnp.zeros(buf.shape[2:], buf.dtype)

        def step(item, carry):
            bias = jnp.where(col < (count - item * TILE) * RUN, 0.0, -jnp.inf)[:1]
            runs = pl.ds(item * TILE, TILE)
            for h in range(heads_kv):
                k = buf[a, runs, h * RUN : (h + 1) * RUN, :]
                v = buf[a, runs, (heads_kv + h) * RUN : (heads_kv + h + 1) * RUN, :]
                top_ref[a, h], total_ref[a, h], mixed_ref[a, h] = flash(
                    q_ref[a, h],
                    k.reshape(TILE * RUN, -1),
                    v.reshape(TILE * RUN, -1),
                    (top_ref[a, h], total_ref[a, h], mixed_ref[a, h]),
                    lambda score: score + bias,
                    factor,
                )
            return carry

        lax.fori_loop(0, (count + TILE - 1) // TILE, step, 0)

    if last:
        for a in range(2):
            for h in range(0, heads_kv, 2):
                done = []
                for g in (h, h + 1):
                    total = jnp.sum(total_ref[a, g], axis=1, keepdims=True)
                    done.append((mixed_ref[a, g] / total).reshape(RUN, group, -1))
                out_ref[a * RUN : (a + 1) * RUN, h * group : (h + 2) * group, :] = (
                    jnp.concatenate(done, axis=1).astype(out_ref.dtype)
                )


def attend(own_ids, q, kvs, state, out, group, half, factor):
    first, last = state is None, out is not None
    run_rows = 2 * q.shape[1] * RUN
    blocks = [x.shape[0] // (2 * run_rows + 16) for x in kvs]
    count = sum(blocks) - int(first)
    operands = [q, *kvs] + ([] if first else list(state))
    lanes = jax.ShapeDtypeStruct(q.shape[:3] + (128,), jnp.float32)
    carried = [lanes, lanes, jax.ShapeDtypeStruct(q.shape, jnp.float32)]
    vmem = pl.BlockSpec(memory_space=pltpu.VMEM)
    shapes = ([out] if last else []) + carried
    aliases = {}
    if not first:
        aliases = {2 + len(kvs) + n: int(last) + n for n in range(3)}
    results = pl.pallas_call(
        functools.partial(attend_kernel, group, factor, half, first, last, blocks),
        out_shape=shapes,
        grid_spec=pltpu.PrefetchScalarGridSpec(
            num_scalar_prefetch=1,
            grid=(),
            in_specs=[vmem] * len(operands),
            out_specs=[vmem] * len(shapes),
            scratch_shapes=[
                pltpu.VMEM((2, 2 * count + TILE - 1, run_rows, q.shape[3]), q.dtype)
            ],
        ),
        input_output_aliases=aliases,
        compiler_params=pltpu.CompilerParams(vmem_limit_bytes=24 * 1024 * 1024),
        cost_estimate=pl.CostEstimate(
            flops=count * RUN * q.size * 4, bytes_accessed=q.size * 16, transcendentals=0
        ),
        name="attend",
    )(own_ids, *operands)
    return results[0] if last else results


def per_device(queries, keys, values, positions):
    outer, inner = lax.axis_size("outer"), lax.axis_size("inner")
    tokens, heads_q, head_dim = queries.shape
    heads_kv = keys.shape[1]
    group = heads_q // heads_kv
    half = tokens // RUN * outer * inner // 2
    factor = math.log2(math.e) / math.sqrt(head_dim)

    chips = outer // 2
    bits = inner.bit_length() - 1
    ring = list(range(0, chips, 2))[:1] + list(range(1, chips, 2))
    ring += list(range(2, chips, 2))[::-1]
    after = {ring[n]: ring[(n + 1) % chips] for n in range(chips)}

    def permute(x, to):
        pairs = []
        for z in range(chips):
            for core in range(2):
                for place in range(inner):
                    nz, ncore, nplace = to(z, core, place)
                    pairs.append(
                        (
                            (2 * z + core) * inner + place,
                            (2 * nz + ncore) * inner + nplace,
                        )
                    )
        return lax.ppermute(x, AXES, pairs)

    def along_z(x):
        return permute(x, lambda z, core, place: (after[z], core, place))

    def doubled(x, step):
        there = permute(
            x,
            lambda z, core, place: (
                z,
                core,
                place ^ (1 << (bits - 1 - step if core else step)),
            ),
        )
        return jnp.concatenate([x, there])

    def other_core(x):
        return permute(x, lambda z, core, place: (z, 1 - core, place))

    kv = jnp.concatenate(
        [x.reshape(2, RUN, heads_kv, head_dim) for x in (keys, values)], axis=2
    ).transpose(0, 2, 1, 3)
    numbers = (positions // RUN).astype(jnp.bfloat16)
    own = jnp.concatenate(
        [
            kv.reshape(-1, head_dim),
            jnp.broadcast_to(numbers[None, :], (16, head_dim)),
        ]
    )
    own_ids = (positions[::RUN] // RUN).astype(jnp.int32)
    q = (
        queries.reshape(2, RUN, heads_kv, group, head_dim)
        .transpose(0, 2, 1, 3, 4)
        .reshape(2, heads_kv, RUN * group, head_dim)
    )

    stage = own
    state, waiting = None, None
    shape = jax.ShapeDtypeStruct(queries.shape, queries.dtype)

    for n in range(chips):
        later = along_z(stage) if n + 1 < chips else None
        held = stage
        for step in range(bits):
            held = doubled(held, step)
        if waiting is not None:
            state = attend(own_ids, q, waiting, state, None, group, half, factor)
            held, *state = lax.optimization_barrier((held, *state))
        waiting = [held, other_core(held)]
        stage = later
    return attend(own_ids, q, waiting, state, shape, group, half, factor)


def solution(mesh):
    in_specs = (
        P(("outer", "inner"), None, None),
        P(("outer", "inner"), None, None),
        P(("outer", "inner"), None, None),
        P(("outer", "inner")),
    )
    out_specs = P(("outer", "inner"), None, None)
    return jax.shard_map(
        per_device, mesh=mesh, in_specs=in_specs, out_specs=out_specs, check_vma=False
    )
```

```python
import functools
import math

import jax
import jax.numpy as jnp
from jax import lax
from jax.experimental import pallas as pl
from jax.experimental.pallas import tpu as pltpu
from jax.sharding import PartitionSpec as P

RUN = 64
TILE = 4
AXES = ("outer", "inner")


def scores(q, k):
    score = lax.dot_general(
        k, q, (((1,), (1,)), ((), ())), preferred_element_type=jnp.float32
    )
    return score.reshape(-1, 8, score.shape[1])


def flash(score, v, state, factor):
    top, total, mixed = state
    new = jnp.max(jnp.max(score, axis=0), axis=0, keepdims=True)
    new = jnp.broadcast_to(new, score.shape[1:])
    if top is not None:
        new = jnp.maximum(top, new)
    weight = jnp.exp2((score - new[None]) * factor)
    part_total = jnp.sum(weight, axis=0)
    part_mixed = lax.dot_general(
        v.T,
        weight.reshape(-1, weight.shape[2]).astype(jnp.bfloat16),
        (((1,), (0,)), ((), ())),
        preferred_element_type=jnp.float32,
    )
    if top is None:
        return new, part_total, part_mixed
    decay = jnp.exp2((top - new) * factor)
    mixed = mixed.reshape(-1, 8, mixed.shape[1]) * decay[None]
    return new, total * decay + part_total, mixed.reshape(part_mixed.shape) + part_mixed


def attend_kernel(group, factor, half, first, last, blocks, own_ids, q_ref, *refs):
    heads_kv = q_ref.shape[1]
    rows = q_ref.shape[2]
    run_rows = 2 * heads_kv * RUN
    block_rows = 2 * run_rows + 16
    kv_refs, refs = refs[: len(blocks)], refs[len(blocks) :]
    if not first:
        refs = refs[3:]
    if last:
        out_ref, refs = refs[0], refs[1:]
    top_ref, total_ref, mixed_ref, buf = refs

    def tile(a, keys, values, mask=None, fresh=False):
        ahead = scores(q_ref[a, 0], keys(0))
        for h in range(heads_kv):
            score = ahead
            if h + 1 < heads_kv:
                ahead = scores(q_ref[a, h + 1], keys(h + 1))
            if mask is not None:
                score = jnp.where(mask.reshape(score.shape), score, -jnp.inf)
            state = (None, None, None)
            if not fresh:
                state = (top_ref[a, h], total_ref[a, h], mixed_ref[a, h])
            state = flash(score, values(h), state, factor)
            top_ref[a, h], total_ref[a, h], mixed_ref[a, h] = state

    if first:
        own_ref = kv_refs[0]

        def own(g):
            return jnp.concatenate(
                [
                    own_ref[r * run_rows + g * RUN : r * run_rows + (g + 1) * RUN]
                    for r in range(2)
                ]
            )

        key_at = lax.broadcasted_iota(jnp.int32, (2 * RUN, rows), 0)
        row_at = lax.broadcasted_iota(jnp.int32, (2 * RUN, rows), 1) // group
        for a in range(2):
            mine, other = own_ids[a], own_ids[1 - a]
            seen = (other < mine) & ((other >= half) == (mine >= half))
            reach = jnp.where(seen, RUN, 0)
            if a == 0:
                live = (key_at <= row_at) | ((key_at >= RUN) & (key_at < RUN + reach))
            else:
                live = (key_at < reach) | ((key_at >= RUN) & (key_at - RUN <= row_at))
            tile(a, own, lambda h: own(heads_kv + h), live, True)

    every = [
        (ref, n * block_rows)
        for at, ref in enumerate(kv_refs)
        for n in range(blocks[at])
        if not (first and at == 0 and n == 0)
    ]
    flags = [[], []]
    for start in range(0, len(every), 8):
        some = every[start : start + 8]
        ids = jnp.concatenate(
            [ref[at + 2 * run_rows : at + block_rows] for ref, at in some]
        ).astype(jnp.float32)
        row = lax.broadcasted_iota(jnp.int32, ids.shape, 0)
        lane = lax.broadcasted_iota(jnp.int32, ids.shape, 1)
        bit = jnp.left_shift(1, 2 * (row // 16) + lane // RUN)
        bit = jnp.where((row % 16 == 0) & (lane % RUN == 0), bit, 0).astype(jnp.float32)
        for a in range(2):
            mine = own_ids[a].astype(jnp.float32)
            low = jnp.where(mine >= half, float(half), 0.0)
            seen = (ids < mine) & (ids >= low)
            bits = jnp.sum(jnp.where(seen, bit, 0.0)).astype(jnp.int32)
            flags[a] += [(bits >> n) & 1 for n in range(2 * len(some))]

    for a in range(2):
        count = jnp.int32(0)
        for n in range(2 * len(every)):

            @pl.when(flags[a][n] == 1)
            def _():
                ref, at = every[n // 2]
                at += (n % 2) * run_rows
                buf[a, count] = ref[at : at + run_rows]

            count = count + flags[a][n]

        def some_runs(start, runs):
            def rows_of(g):
                found = buf[a, pl.ds(start, runs), g * RUN : (g + 1) * RUN, :]
                return found.reshape(runs * RUN, -1)

            tile(a, rows_of, lambda h: rows_of(heads_kv + h))

        def step(item, carry):
            some_runs(item * TILE, TILE)
            return carry

        whole = count // TILE
        lax.fori_loop(0, whole, step, 0)
        for rest in range(1, TILE):

            @pl.when(count - whole * TILE == rest)
            def _():
                some_runs(whole * TILE, rest)

    if last:
        for a in range(2):
            for h in range(0, heads_kv, 2):
                done = []
                for g in (h, h + 1):
                    total = jnp.sum(total_ref[a, g], axis=0, keepdims=True)
                    part = mixed_ref[a, g] * (1.0 / total)
                    done.append(part.T.reshape(RUN, group, -1))
                out_ref[a * RUN : (a + 1) * RUN, h * group : (h + 2) * group, :] = (
                    jnp.concatenate(done, axis=1).astype(out_ref.dtype)
                )


def attend(own_ids, q, kvs, state, out, group, half, factor):
    first, last = state is None, out is not None
    heads_kv, rows, head_dim = q.shape[1:]
    run_rows = 2 * heads_kv * RUN
    blocks = [x.shape[0] // (2 * run_rows + 16) for x in kvs]
    count = sum(blocks) - int(first)
    operands = [q, *kvs] + ([] if first else list(state))
    carried = [
        jax.ShapeDtypeStruct((2, heads_kv, n, rows), jnp.float32)
        for n in (8, 8, head_dim)
    ]
    vmem = pl.BlockSpec(memory_space=pltpu.VMEM)
    shapes = ([out] if last else []) + carried
    aliases = {}
    if not first:
        aliases = {2 + len(kvs) + n: int(last) + n for n in range(3)}
    results = pl.pallas_call(
        functools.partial(attend_kernel, group, factor, half, first, last, blocks),
        out_shape=shapes,
        grid_spec=pltpu.PrefetchScalarGridSpec(
            num_scalar_prefetch=1,
            grid=(),
            in_specs=[vmem] * len(operands),
            out_specs=[vmem] * len(shapes),
            scratch_shapes=[pltpu.VMEM((2, 2 * count, run_rows, head_dim), q.dtype)],
        ),
        input_output_aliases=aliases,
        compiler_params=pltpu.CompilerParams(vmem_limit_bytes=24 * 1024 * 1024),
        cost_estimate=pl.CostEstimate(
            flops=count * RUN * q.size * 4, bytes_accessed=q.size * 16, transcendentals=0
        ),
        name="attend",
    )(own_ids, *operands)
    return results[0] if last else results


def per_device(queries, keys, values, positions):
    outer, inner = lax.axis_size("outer"), lax.axis_size("inner")
    tokens, heads_q, head_dim = queries.shape
    heads_kv = keys.shape[1]
    group = heads_q // heads_kv
    half = tokens // RUN * outer * inner // 2
    factor = math.log2(math.e) / math.sqrt(head_dim)

    chips = outer // 2
    bits = inner.bit_length() - 1
    ring = list(range(0, chips, 2))[:1] + list(range(1, chips, 2))
    ring += list(range(2, chips, 2))[::-1]
    after = {ring[n]: ring[(n + 1) % chips] for n in range(chips)}

    def permute(x, to):
        pairs = []
        for z in range(chips):
            for core in range(2):
                for place in range(inner):
                    nz, ncore, nplace = to(z, core, place)
                    pairs.append(
                        (
                            (2 * z + core) * inner + place,
                            (2 * nz + ncore) * inner + nplace,
                        )
                    )
        return lax.ppermute(x, AXES, pairs)

    def along_z(x):
        return permute(x, lambda z, core, place: (after[z], core, place))

    def doubled(x, step):
        there = permute(
            x,
            lambda z, core, place: (
                z,
                core,
                place ^ (1 << (bits - 1 - step if core else step)),
            ),
        )
        return jnp.concatenate([x, there])

    def other_core(x):
        return permute(x, lambda z, core, place: (z, 1 - core, place))

    kv = jnp.concatenate(
        [x.reshape(2, RUN, heads_kv, head_dim) for x in (keys, values)], axis=2
    ).transpose(0, 2, 1, 3)
    numbers = (positions // RUN).astype(jnp.bfloat16)
    own = jnp.concatenate(
        [
            kv.reshape(-1, head_dim),
            jnp.broadcast_to(numbers[None, :], (16, head_dim)),
        ]
    )
    own_ids = (positions[::RUN] // RUN).astype(jnp.int32)
    q = (
        queries.reshape(2, RUN, heads_kv, group, head_dim)
        .transpose(0, 2, 1, 3, 4)
        .reshape(2, heads_kv, RUN * group, head_dim)
    )

    stage = own
    state, waiting = None, None
    shape = jax.ShapeDtypeStruct(queries.shape, queries.dtype)

    for n in range(chips):
        later = along_z(stage) if n + 1 < chips else None
        held = stage
        for step in range(bits):
            held = doubled(held, step)
        if waiting is not None:
            state = attend(own_ids, q, waiting, state, None, group, half, factor)
            held, *state = lax.optimization_barrier((held, *state))
        waiting = [held, other_core(held)]
        stage = later
    return attend(own_ids, q, waiting, state, shape, group, half, factor)


def solution(mesh):
    in_specs = (
        P(("outer", "inner"), None, None),
        P(("outer", "inner"), None, None),
        P(("outer", "inner"), None, None),
        P(("outer", "inner")),
    )
    out_specs = P(("outer", "inner"), None, None)
    return jax.shard_map(
        per_device, mesh=mesh, in_specs=in_specs, out_specs=out_specs, check_vma=False
    )
```

```python
import functools
import math

import jax
import jax.numpy as jnp
from jax import lax
from jax.experimental import pallas as pl
from jax.experimental.pallas import tpu as pltpu
from jax.sharding import PartitionSpec as P

RUN = 64
TILE = 4
AXES = ("outer", "inner")


def scores(q, k):
    score = lax.dot_general(
        k, q, (((1,), (1,)), ((), ())), preferred_element_type=jnp.float32
    )
    return score.reshape(-1, 8, score.shape[1])


def flash(score, v, state, factor):
    top, total, mixed = state
    new = jnp.max(jnp.max(score, axis=0), axis=0, keepdims=True)
    new = jnp.broadcast_to(new, score.shape[1:])
    if top is not None:
        new = jnp.maximum(top, new)
    weight = jnp.exp2((score - new[None]) * factor)
    part_total = jnp.sum(weight, axis=0)
    part_mixed = lax.dot_general(
        v.T,
        weight.reshape(-1, weight.shape[2]).astype(jnp.bfloat16),
        (((1,), (0,)), ((), ())),
        preferred_element_type=jnp.float32,
    )
    if top is None:
        return new, part_total, part_mixed
    decay = jnp.exp2((top - new) * factor)
    mixed = mixed.reshape(-1, 8, mixed.shape[1]) * decay[None]
    return new, total * decay + part_total, mixed.reshape(part_mixed.shape) + part_mixed


def head_tile(q_ref, state_refs, a, keys, values, factor, mask=None, fresh=False):
    ahead = scores(q_ref[a, 0], keys(0))
    heads_kv = q_ref.shape[1]
    for h in range(heads_kv):
        score = ahead
        if h + 1 < heads_kv:
            ahead = scores(q_ref[a, h + 1], keys(h + 1))
        if mask is not None:
            score = jnp.where(mask.reshape(score.shape), score, -jnp.inf)
        state = (None, None, None)
        if not fresh:
            state = tuple(ref[a, h] for ref in state_refs)
        state = flash(score, values(h), state, factor)
        for ref, value in zip(state_refs, state):
            ref[a, h] = value


def own_kernel(group, factor, half, info, q_ref, own_ref, info_out, *state_refs):
    heads_kv, rows = q_ref.shape[1:3]
    run_rows = 2 * heads_kv * RUN
    state_refs = state_refs[:3]

    def own(g):
        return jnp.concatenate(
            [
                own_ref[r * run_rows + g * RUN : r * run_rows + (g + 1) * RUN]
                for r in range(2)
            ]
        )

    key_at = lax.broadcasted_iota(jnp.int32, (2 * RUN, rows), 0)
    row_at = lax.broadcasted_iota(jnp.int32, (2 * RUN, rows), 1) // group
    for a in range(2):
        mine, other = info[a], info[1 - a]
        seen = (other < mine) & ((other >= half) == (mine >= half))
        reach = jnp.where(seen, RUN, 0)
        if a == 0:
            live = (key_at <= row_at) | ((key_at >= RUN) & (key_at < RUN + reach))
        else:
            live = (key_at < reach) | ((key_at >= RUN) & (key_at - RUN <= row_at))
        head_tile(
            q_ref, state_refs, a, own, lambda h: own(heads_kv + h), factor, live, True
        )
        info_out[a] = mine
        info_out[2 + a] = 0


def attend_kernel(group, factor, half, last, blocks, info, q_ref, *refs):
    heads_kv = q_ref.shape[1]
    run_rows = 2 * heads_kv * RUN
    block_rows = 2 * run_rows + 16
    kv_refs, refs = refs[: len(blocks)], refs[len(blocks) :]
    refs = refs[4:]
    if last:
        out_ref, refs = refs[0], refs[1:]
    else:
        info_out, refs = refs[0], refs[1:]
    *state_refs, buf = refs

    every = [
        (ref, n * block_rows) for at, ref in enumerate(kv_refs) for n in range(*blocks[at])
    ]
    flags = [[], []]
    for start in range(0, len(every), 8):
        some = every[start : start + 8]
        ids = jnp.concatenate(
            [ref[at + 2 * run_rows : at + block_rows] for ref, at in some]
        ).astype(jnp.float32)
        row = lax.broadcasted_iota(jnp.int32, ids.shape, 0)
        lane = lax.broadcasted_iota(jnp.int32, ids.shape, 1)
        bit = jnp.left_shift(1, 2 * (row // 16) + lane // RUN)
        bit = jnp.where((row % 16 == 0) & (lane % RUN == 0), bit, 0).astype(jnp.float32)
        for a in range(2):
            mine = info[a].astype(jnp.float32)
            low = jnp.where(mine >= half, float(half), 0.0)
            seen = (ids < mine) & (ids >= low)
            bits = jnp.sum(jnp.where(seen, bit, 0.0)).astype(jnp.int32)
            flags[a] += [(bits >> n) & 1 for n in range(2 * len(some))]

    counts = []
    for a in range(2):
        count = info[2 + a]
        for n in range(2 * len(every)):

            @pl.when(flags[a][n] == 1)
            def _():
                ref, at = every[n // 2]
                at += (n % 2) * run_rows
                buf[a, count] = ref[at : at + run_rows]

            count = count + flags[a][n]
        counts.append(count)

    def some_runs(a, start, runs):
        def rows_of(g):
            found = buf[a, pl.ds(start, runs), g * RUN : (g + 1) * RUN, :]
            return found.reshape(runs * RUN, -1)

        head_tile(
            q_ref, state_refs, a, rows_of, lambda h: rows_of(heads_kv + h), factor
        )

    whole = [count // TILE for count in counts]

    def step(item, carry):
        a = (item >= whole[0]).astype(jnp.int32)
        some_runs(a, (item - a * whole[0]) * TILE, TILE)
        return carry

    lax.fori_loop(0, whole[0] + whole[1], step, 0)

    if not last:
        for a in range(2):
            start = whole[a] * TILE
            rest = counts[a] - start
            for n in range(TILE - 1):

                @pl.when((whole[a] > 0) & (n < rest))
                def _():
                    buf[a, n] = buf[a, start + n]

            info_out[a] = info[a]
            info_out[2 + a] = rest
        return

    for a in range(2):
        start = whole[a] * TILE
        rest = counts[a] - start
        runs = TILE // 2
        while runs:

            @pl.when(rest & runs != 0)
            def _():
                some_runs(a, start, runs)

            start = start + (rest & runs)
            runs //= 2
        for h in range(0, heads_kv, 2):
            done = []
            for g in (h, h + 1):
                total = jnp.sum(state_refs[1][a, g], axis=0, keepdims=True)
                part = state_refs[2][a, g] * (1.0 / total)
                done.append(part.T.reshape(RUN, group, -1))
            out_ref[a * RUN : (a + 1) * RUN, h * group : (h + 2) * group, :] = (
                jnp.concatenate(done, axis=1).astype(out_ref.dtype)
            )


class Attention:
    def __init__(self, q, group, half, room):
        self.q, self.group, self.half = q, group, half
        self.factor = math.log2(math.e) / math.sqrt(q.shape[3])
        heads_kv, rows, head_dim = q.shape[1:]
        self.run_rows = 2 * heads_kv * RUN
        slots = 2 * room + TILE - 1
        self.carried = [jax.ShapeDtypeStruct((4,), jnp.int32)] + [
            jax.ShapeDtypeStruct((2, heads_kv, n, rows), jnp.float32)
            for n in (8, 8, head_dim)
        ]
        self.carried.append(
            jax.ShapeDtypeStruct((2, slots, self.run_rows, head_dim), q.dtype)
        )

    def call(self, kernel, operands, shapes, aliases, count, name):
        vmem = pl.BlockSpec(memory_space=pltpu.VMEM)
        smem = pl.BlockSpec(memory_space=pltpu.SMEM)
        return pl.pallas_call(
            kernel,
            out_shape=shapes,
            in_specs=[smem] + [vmem] * (len(operands) - 1),
            out_specs=[smem if x.shape == (4,) else vmem for x in shapes],
            input_output_aliases=aliases,
            compiler_params=pltpu.CompilerParams(vmem_limit_bytes=24 * 1024 * 1024),
            cost_estimate=pl.CostEstimate(
                flops=count * RUN * self.q.size * 4,
                bytes_accessed=self.q.size * 8,
                transcendentals=0,
            ),
            name=name,
        )(*operands)

    def start(self, info, own):
        kernel = functools.partial(own_kernel, self.group, self.factor, self.half)
        return self.call(kernel, [info, self.q, own], self.carried, {}, 2, "attend_own")

    def add(self, state, kvs, out=None):
        kvs = [x if isinstance(x, tuple) else (x, 0) for x in kvs]
        blocks = [(skip, x.shape[0] // (2 * self.run_rows + 16)) for x, skip in kvs]
        count = sum(end - skip for skip, end in blocks)
        operands = [state[0], self.q, *(x for x, _ in kvs), *state[1:]]
        first = 2 + len(kvs)
        aliases = {first + n: 1 + n for n in range(4)}
        shapes = [out or self.carried[0]] + self.carried[1:]
        kernel = functools.partial(
            attend_kernel, self.group, self.factor, self.half, out is not None, blocks
        )
        results = self.call(kernel, operands, shapes, aliases, count, "attend")
        return results[0] if out else results


def per_device(queries, keys, values, positions):
    outer, inner = lax.axis_size("outer"), lax.axis_size("inner")
    tokens, heads_q, head_dim = queries.shape
    heads_kv = keys.shape[1]
    group = heads_q // heads_kv
    half = tokens // RUN * outer * inner // 2

    chips = outer // 2
    bits = inner.bit_length() - 1

    def permute(x, to):
        pairs = []
        for z in range(chips):
            for core in range(2):
                for place in range(inner):
                    nz, ncore, nplace = to(z, core, place)
                    pairs.append(
                        (
                            (2 * z + core) * inner + place,
                            (2 * nz + ncore) * inner + nplace,
                        )
                    )
        return lax.ppermute(x, AXES, pairs)

    def over_z(x, bit):
        return permute(x, lambda z, core, place: (z ^ bit, core, place))

    def over_place(x, step):
        def to(z, core, place):
            return z, core, place ^ (1 << (bits - 1 - step if core else step))

        return permute(x, to)

    def other_core(x):
        return permute(x, lambda z, core, place: (z, 1 - core, place))

    def tied(x, state):
        x, *state = lax.optimization_barrier((x, *state))
        return x, state

    kv = jnp.concatenate(
        [x.reshape(2, RUN, heads_kv, head_dim) for x in (keys, values)], axis=2
    ).transpose(0, 2, 1, 3)
    numbers = (positions // RUN).astype(jnp.bfloat16)
    own = jnp.concatenate(
        [
            kv.reshape(-1, head_dim),
            jnp.broadcast_to(numbers[None, :], (16, head_dim)),
        ]
    )
    info = jnp.concatenate(
        [(positions[::RUN] // RUN).astype(jnp.int32), jnp.zeros(2, jnp.int32)]
    )
    q = (
        queries.reshape(2, RUN, heads_kv, group, head_dim)
        .transpose(0, 2, 1, 3, 4)
        .reshape(2, heads_kv, RUN * group, head_dim)
    )

    planes = [own]
    while len(planes) < chips:
        bit = len(planes)
        planes += [over_z(x, bit) for x in planes]

    attention = Attention(q, group, half, 2 * inner)
    state = attention.start(info, own)
    mine, theirs = [], []
    for n, held in enumerate(planes):
        for step in range(bits - 1):
            held = jnp.concatenate([held, over_place(held, step)])
        if n == 0:
            held, state = tied(held, state)
        elif n >= 2:
            state = attention.add(state, [mine[n - 2], *theirs[n - 3 : n - 2]])
            held, state = tied(held, state)
        there = over_place(held, bits - 1)
        if n + 1 < chips:
            found = jnp.concatenate([held, there])
            mine.append((found, int(n == 0)))
            theirs.append(other_core(found))
    state = attention.add(state, [mine[-1], theirs[-2]])
    state = attention.add(state, [held, theirs[-1]])
    held_theirs, there_theirs = other_core(held), other_core(there)
    state = attention.add(state, [there, held_theirs])
    out = jax.ShapeDtypeStruct(queries.shape, queries.dtype)
    return attention.add(state, [there_theirs], out)


def solution(mesh):
    in_specs = (
        P(("outer", "inner"), None, None),
        P(("outer", "inner"), None, None),
        P(("outer", "inner"), None, None),
        P(("outer", "inner")),
    )
    out_specs = P(("outer", "inner"), None, None)
    return jax.shard_map(
        per_device, mesh=mesh, in_specs=in_specs, out_specs=out_specs, check_vma=False
    )
```

```python
import functools
import math

import jax
import jax.numpy as jnp
from jax import lax
from jax.experimental import pallas as pl
from jax.experimental.pallas import tpu as pltpu
from jax.sharding import PartitionSpec as P

RUN = 64
TILE = 4
AXES = ("outer", "inner")


def scores(qt, k):
    score = jnp.dot(k, qt, preferred_element_type=jnp.float32)
    return score.reshape(-1, 8, score.shape[1])


def flash(score, vt, state, factor):
    top, total, mixed = state
    new = jnp.max(jnp.max(score, axis=0), axis=0, keepdims=True)
    new = jnp.broadcast_to(new, score.shape[1:])
    if top is not None:
        new = jnp.maximum(top, new)
    weight = jnp.exp2((score - new[None]) * factor)
    part_total = jnp.sum(weight, axis=0)
    weight = weight.reshape(-1, weight.shape[2]).astype(jnp.bfloat16)
    part_mixed = jnp.dot(vt, weight, preferred_element_type=jnp.float32)
    if top is None:
        return new, part_total, part_mixed
    decay = jnp.exp2((top - new) * factor)
    mixed = mixed.reshape(-1, 8, mixed.shape[1]) * decay[None]
    return new, total * decay + part_total, mixed.reshape(part_mixed.shape) + part_mixed


def head_tile(qt_ref, state_refs, a, keys, values, factor, mask=None):
    ahead = scores(qt_ref[a, 0], keys(0))
    heads_kv = qt_ref.shape[1]
    for h in range(heads_kv):
        score = ahead
        if h + 1 < heads_kv:
            ahead = scores(qt_ref[a, h + 1], keys(h + 1))
        if mask is None:
            state = tuple(ref[a, h] for ref in state_refs)
        else:
            score = jnp.where(mask.reshape(score.shape), score, -jnp.inf)
            state = (None, None, None)
        state = flash(score, values(h), state, factor)
        for ref, value in zip(state_refs, state):
            ref[a, h] = value


def own_kernel(group, factor, half, q_ref, own_ref, meta_ref, qt_ref, *refs):
    heads_kv, head_dim, rows = qt_ref.shape[1:]
    state_refs = refs[:3]
    key_rows = heads_kv * RUN
    value_rows = heads_kv * head_dim

    ids = own_ref[2 * key_rows + value_rows :].astype(jnp.float32)
    lane = lax.broadcasted_iota(jnp.int32, ids.shape, 1)
    numbers = [jnp.max(jnp.where(lane // RUN == a, ids, 0.0)) for a in range(2)]
    row = lax.broadcasted_iota(jnp.int32, meta_ref.shape, 0)
    meta_ref[...] = jnp.where(
        row == 0, numbers[0], jnp.where(row == 1, numbers[1], 0.0)
    )

    key_at = lax.broadcasted_iota(jnp.int32, (2 * RUN, rows), 0)
    row_at = lax.broadcasted_iota(jnp.int32, (2 * RUN, rows), 1) // group
    for a in range(2):
        for h in range(heads_kv):
            qt_ref[a, h] = q_ref[a, h].T
        mine, other = numbers[a], numbers[1 - a]
        seen = (other < mine) & ((other >= half) == (mine >= half))
        reach = jnp.where(seen, RUN, 0)
        if a == 0:
            live = (key_at <= row_at) | ((key_at >= RUN) & (key_at < RUN + reach))
        else:
            live = (key_at < reach) | ((key_at >= RUN) & (key_at - RUN <= row_at))

        def keys(h):
            parts = [own_ref[n : n + RUN] for n in (h * RUN, key_rows + h * RUN)]
            return jnp.concatenate(parts)

        def values(h):
            start = 2 * key_rows + h * head_dim
            return own_ref[start : start + head_dim]

        head_tile(qt_ref, state_refs, a, keys, values, factor, live)


def attend_kernel(group, factor, half, last, blocks, qt_ref, *refs):
    heads_kv, head_dim, rows = qt_ref.shape[1:]
    key_rows = heads_kv * RUN
    value_rows = heads_kv * head_dim
    block_rows = 2 * key_rows + value_rows + 16
    kv_refs, refs = refs[: len(blocks)], refs[len(blocks) :]
    refs = refs[6:]
    if last:
        out_ref, refs = refs[0], refs[1:]
    meta_ref, *state_refs, kbuf, vbuf = refs

    meta = meta_ref[...]
    counts = tuple(
        jnp.max(meta[2 + a : 3 + a]).astype(jnp.int32) for a in range(2)
    )
    seen_bits = []
    for ref, (skip, end) in zip(kv_refs, blocks):
        assert end - skip <= 8
        ids = jnp.concatenate(
            [ref[n * block_rows - 16 : n * block_rows] for n in range(skip + 1, end + 1)]
        ).astype(jnp.float32)
        row = lax.broadcasted_iota(jnp.int32, ids.shape, 0)
        lane = lax.broadcasted_iota(jnp.int32, ids.shape, 1)
        bit = jnp.left_shift(1, 2 * (row // 16) + lane // RUN)
        bit = jnp.where((row % 16 == 0) & (lane % RUN == 0), bit, 0).astype(jnp.float32)
        found = []
        for a in range(2):
            mine = meta[a : a + 1]
            low = jnp.where(mine >= half, float(half), 0.0)
            seen = (ids < mine) & (ids >= low)
            found.append(jnp.sum(jnp.where(seen, bit, 0.0)).astype(jnp.int32))
        seen_bits.append(found)

    lane = lax.broadcasted_iota(jnp.int32, (value_rows, 2 * RUN), 1)
    for ref, (skip, end), bits in zip(kv_refs, blocks, seen_bits):

        def gather(n, counts):
            start = (skip + n // 2) * block_rows
            side = n % 2
            fresh = []
            for a in range(2):
                flag = (bits[a] >> n) & 1
                count = counts[a]

                @pl.when(flag == 1)
                def _():
                    at = pl.multiple_of(start + side * key_rows, 16)
                    kbuf[a, count] = ref[pl.ds(at, key_rows), :]
                    at = pl.multiple_of(start + 2 * key_rows, 16)
                    value = ref[pl.ds(at, value_rows), :]
                    parity = count % 2
                    pair = count // 2
                    value = jnp.where(
                        parity == side, value, pltpu.roll(value, RUN, 1)
                    )
                    vbuf[a, pair] = jnp.where(
                        lane // RUN == parity, value, vbuf[a, pair]
                    )

                fresh.append(count + flag)
            return tuple(fresh)

        counts = lax.fori_loop(0, 2 * (end - skip), gather, counts)

    def some_runs(a, start, runs):
        def keys(h):
            found = kbuf[a, pl.ds(start, runs), h * RUN : (h + 1) * RUN, :]
            return found.reshape(runs * RUN, -1)

        def values(h):
            found = [
                vbuf[a, start // 2 + n, h * head_dim : (h + 1) * head_dim, :]
                for n in range((runs + 1) // 2)
            ]
            return jnp.concatenate(found, axis=1)[:, : runs * RUN]

        head_tile(qt_ref, state_refs, a, keys, values, factor)

    whole = [count // TILE for count in counts]

    def step(item, carry):
        a = (item >= whole[0]).astype(jnp.int32)
        some_runs(a, (item - a * whole[0]) * TILE, TILE)
        return carry

    lax.fori_loop(0, whole[0] + whole[1], step, 0)

    if not last:
        row = lax.broadcasted_iota(jnp.int32, meta.shape, 0)
        for a in range(2):
            start = whole[a] * TILE
            rest = counts[a] - start

            @pl.when((whole[a] > 0) & (rest > 0))
            def _():
                for n in range(TILE - 1):
                    kbuf[a, n] = kbuf[a, start + n]
                for n in range(TILE // 2):
                    vbuf[a, n] = vbuf[a, start // 2 + n]

            meta = jnp.where(row == 2 + a, rest.astype(jnp.float32), meta)
        meta_ref[...] = meta
        return

    for a in range(2):
        start = whole[a] * TILE
        rest = counts[a] - start
        runs = TILE // 2
        while runs:

            @pl.when(rest & runs != 0)
            def _():
                some_runs(a, start, runs)

            start = start + (rest & runs)
            runs //= 2
        for h in range(0, heads_kv, 2):
            done = []
            for g in (h, h + 1):
                total = jnp.sum(state_refs[1][a, g], axis=0, keepdims=True)
                part = state_refs[2][a, g] * (1.0 / total)
                done.append(part.T.reshape(RUN, group, -1))
            out_ref[a * RUN : (a + 1) * RUN, h * group : (h + 2) * group, :] = (
                jnp.concatenate(done, axis=1).astype(out_ref.dtype)
            )


class Attention:
    def __init__(self, q, group, half, room):
        self.q, self.group, self.half = q, group, half
        self.factor = math.log2(math.e) / math.sqrt(q.shape[3])
        heads_kv, rows, head_dim = q.shape[1:]
        self.block_rows = 2 * heads_kv * RUN + heads_kv * head_dim + 16
        slots = 2 * room + TILE
        self.carried = [jax.ShapeDtypeStruct((8, 128), jnp.float32)]
        self.carried += [
            jax.ShapeDtypeStruct((2, heads_kv, n, rows), jnp.float32)
            for n in (8, 8, head_dim)
        ]
        self.carried += [
            jax.ShapeDtypeStruct((2, slots, heads_kv * RUN, head_dim), q.dtype),
            jax.ShapeDtypeStruct((2, slots // 2, heads_kv * head_dim, 2 * RUN), q.dtype),
        ]

    def call(self, kernel, operands, shapes, aliases, count, name):
        vmem = pl.BlockSpec(memory_space=pltpu.VMEM)
        return pl.pallas_call(
            kernel,
            out_shape=shapes,
            in_specs=[vmem] * len(operands),
            out_specs=[vmem] * len(shapes),
            input_output_aliases=aliases,
            compiler_params=pltpu.CompilerParams(vmem_limit_bytes=24 * 1024 * 1024),
            cost_estimate=pl.CostEstimate(
                flops=count * RUN * self.q.size * 4,
                bytes_accessed=self.q.size * 8,
                transcendentals=0,
            ),
            name=name,
        )(*operands)

    def start(self, own):
        kernel = functools.partial(own_kernel, self.group, self.factor, self.half)
        heads_kv, rows, head_dim = self.q.shape[1:]
        qt = jax.ShapeDtypeStruct((2, heads_kv, head_dim, rows), self.q.dtype)
        shapes = [self.carried[0], qt] + self.carried[1:]
        meta, self.qt, *rest = self.call(
            kernel, [self.q, own], shapes, {}, 2, "attend_own"
        )
        return [meta, *rest]

    def add(self, state, kvs, out=None):
        kvs = [x if isinstance(x, tuple) else (x, 0) for x in kvs]
        blocks = [(skip, x.shape[0] // self.block_rows) for x, skip in kvs]
        count = sum(end - skip for skip, end in blocks)
        operands = [self.qt, *(x for x, _ in kvs), *state]
        first, ahead = 1 + len(kvs), int(out is not None)
        aliases = {first + n: ahead + n for n in range(len(state))}
        shapes = ([out] if ahead else []) + self.carried
        kernel = functools.partial(
            attend_kernel, self.group, self.factor, self.half, out is not None, blocks
        )
        results = self.call(kernel, operands, shapes, aliases, count, "attend")
        return results[0] if ahead else results


def per_device(queries, keys, values, positions):
    outer, inner = lax.axis_size("outer"), lax.axis_size("inner")
    tokens, heads_q, head_dim = queries.shape
    heads_kv = keys.shape[1]
    group = heads_q // heads_kv
    half = tokens // RUN * outer * inner // 2

    chips = outer // 2
    bits = inner.bit_length() - 1
    ring = [0] + list(range(1, chips, 2)) + list(range(2, chips, 2))[::-1]
    after = {ring[n]: ring[(n + 1) % chips] for n in range(chips)}

    def permute(x, to):
        pairs = []
        for z in range(chips):
            for core in range(2):
                for place in range(inner):
                    nz, ncore, nplace = to(z, core, place)
                    pairs.append(
                        (
                            (2 * z + core) * inner + place,
                            (2 * nz + ncore) * inner + nplace,
                        )
                    )
        return lax.ppermute(x, AXES, pairs)

    def along_z(x):
        return permute(x, lambda z, core, place: (after[z], core, place))

    def over_place(x, step):
        def to(z, core, place):
            return z, core, place ^ (1 << (bits - 1 - step if core else step))

        return permute(x, to)

    def other_core(x):
        return permute(x, lambda z, core, place: (z, 1 - core, place))

    def tied(x, *others):
        return lax.optimization_barrier((x, *others))[0]

    by_run = keys.reshape(2, RUN, heads_kv, head_dim).transpose(0, 2, 1, 3)
    numbers = (positions // RUN).astype(jnp.bfloat16)
    own = jnp.concatenate(
        [
            by_run.reshape(-1, head_dim),
            values.reshape(tokens, -1).T,
            jnp.broadcast_to(numbers[None, :], (16, tokens)),
        ]
    )
    q = (
        queries.reshape(2, RUN, heads_kv, group, head_dim)
        .transpose(0, 2, 1, 3, 4)
        .reshape(2, heads_kv, RUN * group, head_dim)
    )

    attention = Attention(q, group, half, 2 * inner)
    state = attention.start(own)
    planes, done = [own], []
    near, far = [], []

    for n in range(chips):
        stage = planes[n]
        if n + 1 < chips:
            planes.append(along_z(stage))
        if n > 0:
            stage = tied(stage, *near[n - 1][1:], *(far[n - 2] if n > 1 else []))
        near.append([stage] + [over_place(stage, step) for step in range(bits)])
        late = near[n][1]
        if n + 1 < chips:
            late = tied(late, planes[n + 1])
        if n > 1:
            state = attention.add(state, done[n - 2])
        late = tied(late, state[0])
        reached = {0: stage}
        for step in range(bits):
            reached[1 << step] = near[n][1 + step]
        far.append([])
        for step in range(1, bits):
            for place in range(1, 1 << step):
                source = late if place == 1 else reached[place]
                reached[place | (1 << step)] = over_place(source, step)
                far[n].append(reached[place | (1 << step)])
        if n + 1 < chips:
            mine = jnp.concatenate(near[n] + far[n])
            done.append([(mine, int(n == 0)), other_core(mine)])
    most = jnp.concatenate(near[-1] + far[-1][:-1])
    theirs = other_core(most)
    state = attention.add(state, done[-1])
    state = attention.add(state, [most])
    final = tied(far[-1][-1], state[0])
    final_theirs = other_core(final)
    state = attention.add(state, [theirs, final])
    out = jax.ShapeDtypeStruct(queries.shape, queries.dtype)
    return attention.add(state, [final_theirs], out)


def solution(mesh):
    in_specs = (
        P(("outer", "inner"), None, None),
        P(("outer", "inner"), None, None),
        P(("outer", "inner"), None, None),
        P(("outer", "inner")),
    )
    out_specs = P(("outer", "inner"), None, None)
    return jax.shard_map(
        per_device, mesh=mesh, in_specs=in_specs, out_specs=out_specs, check_vma=False
    )
```

```python
import functools
import math

import jax
import jax.numpy as jnp
from jax import lax
from jax.experimental import pallas as pl
from jax.experimental.pallas import tpu as pltpu
from jax.sharding import PartitionSpec as P

RUN = 64
TILE = 8
KEEP = 4
AXES = ("outer", "inner")


def flash(score, v, state, factor, live=None):
    top, total, mixed = state
    keys = score.shape[1]
    if isinstance(live, int):
        lane = lax.broadcasted_iota(jnp.int32, score.shape, 1)
        keys, live = live, lane < live
    if live is not None:
        score = jnp.where(live, score, -jnp.inf)
    parts = [score[:, c : c + 128] for c in range(0, score.shape[1], 128)]
    new = jnp.max(functools.reduce(jnp.maximum, parts), axis=1, keepdims=True)
    if top is None:
        new = jnp.broadcast_to(new, parts[0].shape)
    else:
        new = jnp.maximum(top, new)
    weights = [jnp.exp2((part - new) * factor) for part in parts]
    part_total = functools.reduce(jnp.add, weights)
    weights = jnp.concatenate([w.astype(jnp.bfloat16) for w in weights], axis=1)
    part_mixed = jnp.dot(weights[:, :keys], v, preferred_element_type=jnp.float32)
    if top is None:
        return new, part_total, part_mixed
    decay = jnp.exp2((top - new) * factor)
    return new, total * decay + part_total, mixed * decay + part_mixed


def head_tile(q_ref, state_refs, a, keys, values, factor, live=None):
    def scores(h):
        return jnp.dot(q_ref[a, h], keys(h), preferred_element_type=jnp.float32)

    heads_kv = q_ref.shape[1]
    ahead = scores(0)
    for h in range(heads_kv):
        score = ahead
        if h + 1 < heads_kv:
            ahead = scores(h + 1)
        state = (None, None, None)
        if live is None or isinstance(live, int):
            state = tuple(ref[a, h] for ref in state_refs)
        state = flash(score, values(h), state, factor, live)
        for ref, value in zip(state_refs, state):
            ref[a, h] = value


def own_kernel(group, factor, half, q_ref, own_ref, meta_ref, *refs):
    heads_kv, rows, head_dim = q_ref.shape[1:]
    state_refs = refs[:3]
    key_rows = heads_kv * head_dim
    value_rows = heads_kv * RUN

    ids = own_ref[key_rows + 2 * value_rows :].astype(jnp.float32)
    lane = lax.broadcasted_iota(jnp.int32, ids.shape, 1)
    numbers = [jnp.max(jnp.where(lane // RUN == a, ids, 0.0)) for a in range(2)]
    row = lax.broadcasted_iota(jnp.int32, meta_ref.shape, 0)
    meta_ref[...] = jnp.where(
        row == 0, numbers[0], jnp.where(row == 1, numbers[1], 0.0)
    )

    row_at = lax.broadcasted_iota(jnp.int32, (rows, 2 * RUN), 0) // group
    key_at = lax.broadcasted_iota(jnp.int32, (rows, 2 * RUN), 1)
    for a in range(2):
        mine, other = numbers[a], numbers[1 - a]
        seen = (other < mine) & ((other >= half) == (mine >= half))
        reach = jnp.where(seen, RUN, 0)
        if a == 0:
            live = (key_at <= row_at) | ((key_at >= RUN) & (key_at < RUN + reach))
        else:
            live = (key_at < reach) | ((key_at >= RUN) & (key_at - RUN <= row_at))

        def keys(h):
            return own_ref[h * head_dim : (h + 1) * head_dim]

        def values(h):
            starts = [key_rows + h * RUN, key_rows + value_rows + h * RUN]
            return jnp.concatenate([own_ref[n : n + RUN] for n in starts])

        head_tile(q_ref, state_refs, a, keys, values, factor, live)


def attend_kernel(group, factor, half, last, blocks, q_ref, *refs):
    heads_kv, rows, head_dim = q_ref.shape[1:]
    key_rows = heads_kv * head_dim
    value_rows = heads_kv * RUN
    block_rows = key_rows + 2 * value_rows + 16
    kv_refs, refs = refs[: len(blocks)], refs[len(blocks) :]
    refs = refs[6:]
    if last:
        out_ref, refs = refs[0], refs[1:]
    meta_ref, *state_refs, kbuf, vbuf = refs

    meta = meta_ref[...]
    counts = tuple(
        jnp.max(meta[2 + a : 3 + a]).astype(jnp.int32) for a in range(2)
    )
    seen_bits = []
    for ref, (skip, end) in zip(kv_refs, blocks):
        assert end - skip <= 8
        ids = jnp.concatenate(
            [ref[n * block_rows - 16 : n * block_rows] for n in range(skip + 1, end + 1)]
        ).astype(jnp.float32)
        row = lax.broadcasted_iota(jnp.int32, ids.shape, 0)
        lane = lax.broadcasted_iota(jnp.int32, ids.shape, 1)
        bit = jnp.left_shift(1, 2 * (row // 16) + lane // RUN)
        bit = jnp.where((row % 16 == 0) & (lane % RUN == 0), bit, 0).astype(jnp.float32)
        found = []
        for a in range(2):
            mine = meta[a : a + 1]
            low = jnp.where(mine >= half, float(half), 0.0)
            seen = (ids < mine) & (ids >= low)
            found.append(jnp.sum(jnp.where(seen, bit, 0.0)).astype(jnp.int32))
        seen_bits.append(found)

    lane = lax.broadcasted_iota(jnp.int32, (key_rows, 2 * RUN), 1)
    for ref, (skip, end), bits in zip(kv_refs, blocks, seen_bits):

        def gather(n, counts):
            start = (skip + n // 2) * block_rows
            side = n % 2
            fresh = []
            for a in range(2):
                flag = (bits[a] >> n) & 1
                count = counts[a]

                @pl.when(flag == 1)
                def _():
                    at = pl.multiple_of(start + key_rows + side * value_rows, 16)
                    vbuf[a, count] = ref[pl.ds(at, value_rows), :]
                    key = ref[pl.ds(pl.multiple_of(start, 16), key_rows), :]
                    parity = count % 2
                    pair = count // 2
                    key = jnp.where(parity == side, key, pltpu.roll(key, RUN, 1))
                    kbuf[a, pair] = jnp.where(lane // RUN == parity, key, kbuf[a, pair])

                fresh.append(count + flag)
            return tuple(fresh)

        counts = lax.fori_loop(0, 2 * (end - skip), gather, counts)

    def some_runs(a, start, runs):
        def keys(h):
            found = [
                kbuf[a, start // 2 + n, h * head_dim : (h + 1) * head_dim, :]
                for n in range((runs + 1) // 2)
            ]
            return jnp.concatenate(found, axis=1)

        def values(h):
            found = vbuf[a, pl.ds(start, runs), h * RUN : (h + 1) * RUN, :]
            return found.reshape(runs * RUN, -1)

        live = RUN if runs == 1 else None
        head_tile(q_ref, state_refs, a, keys, values, factor, live)

    whole = [count // TILE for count in counts]

    def step(item, carry):
        a = (item >= whole[0]).astype(jnp.int32)
        some_runs(a, (item - a * whole[0]) * TILE, TILE)
        return carry

    lax.fori_loop(0, whole[0] + whole[1], step, 0)

    def remainder(a, carry):
        count = jnp.where(a == 0, counts[0], counts[1])
        start = count // TILE * TILE
        runs = TILE // 2
        while runs >= (1 if last else KEEP):

            @pl.when(count & runs != 0)
            def _():
                some_runs(a, start, runs)

            start = start + (count & runs)
            runs //= 2
        return carry

    lax.fori_loop(0, 2, remainder, 0)

    if not last:
        row = lax.broadcasted_iota(jnp.int32, meta.shape, 0)
        for a in range(2):
            start = counts[a] // KEEP * KEEP
            rest = counts[a] - start

            @pl.when((start > 0) & (rest > 0))
            def _():
                for n in range(KEEP - 1):
                    vbuf[a, n] = vbuf[a, start + n]
                for n in range(KEEP // 2):
                    kbuf[a, n] = kbuf[a, start // 2 + n]

            meta = jnp.where(row == 2 + a, rest.astype(jnp.float32), meta)
        meta_ref[...] = meta
        return

    for a in range(2):
        for h in range(0, heads_kv, 2):
            done = []
            for g in (h, h + 1):
                total = jnp.sum(state_refs[1][a, g], axis=1, keepdims=True)
                part = state_refs[2][a, g] * (1.0 / total)
                done.append(part.reshape(RUN, group, -1))
            out_ref[a * RUN : (a + 1) * RUN, h * group : (h + 2) * group, :] = (
                jnp.concatenate(done, axis=1).astype(out_ref.dtype)
            )


class Attention:
    def __init__(self, q, group, half, room):
        self.q, self.group, self.half = q, group, half
        self.factor = math.log2(math.e) / math.sqrt(q.shape[3])
        heads_kv, rows, head_dim = q.shape[1:]
        self.block_rows = 2 * heads_kv * RUN + heads_kv * head_dim + 16
        slots = 2 * room + KEEP
        self.carried = [jax.ShapeDtypeStruct((8, 128), jnp.float32)]
        self.carried += [
            jax.ShapeDtypeStruct((2, heads_kv, rows, n), jnp.float32)
            for n in (128, 128, head_dim)
        ]
        self.carried += [
            jax.ShapeDtypeStruct((2, slots // 2, heads_kv * head_dim, 2 * RUN), q.dtype),
            jax.ShapeDtypeStruct((2, slots, heads_kv * RUN, head_dim), q.dtype),
        ]

    def call(self, kernel, operands, shapes, aliases, count, name):
        vmem = pl.BlockSpec(memory_space=pltpu.VMEM)
        return pl.pallas_call(
            kernel,
            out_shape=shapes,
            in_specs=[vmem] * len(operands),
            out_specs=[vmem] * len(shapes),
            input_output_aliases=aliases,
            compiler_params=pltpu.CompilerParams(vmem_limit_bytes=28 * 1024 * 1024),
            cost_estimate=pl.CostEstimate(
                flops=count * RUN * self.q.size * 4,
                bytes_accessed=self.q.size * 8,
                transcendentals=0,
            ),
            name=name,
        )(*operands)

    def start(self, own):
        kernel = functools.partial(own_kernel, self.group, self.factor, self.half)
        return self.call(kernel, [self.q, own], self.carried, {}, 2, "attend_own")

    def add(self, state, kvs, out=None):
        kvs = [x if isinstance(x, tuple) else (x, 0) for x in kvs]
        blocks = [(skip, x.shape[0] // self.block_rows) for x, skip in kvs]
        count = sum(end - skip for skip, end in blocks)
        operands = [self.q, *(x for x, _ in kvs), *state]
        first, ahead = 1 + len(kvs), int(out is not None)
        aliases = {first + n: ahead + n for n in range(len(state))}
        shapes = ([out] if ahead else []) + self.carried
        kernel = functools.partial(
            attend_kernel, self.group, self.factor, self.half, out is not None, blocks
        )
        results = self.call(kernel, operands, shapes, aliases, count, "attend")
        return results[0] if ahead else results


def per_device(queries, keys, values, positions):
    outer, inner = lax.axis_size("outer"), lax.axis_size("inner")
    tokens, heads_q, head_dim = queries.shape
    heads_kv = keys.shape[1]
    group = heads_q // heads_kv
    half = tokens // RUN * outer * inner // 2

    chips = outer // 2
    bits = inner.bit_length() - 1
    ring = [0] + list(range(1, chips, 2)) + list(range(2, chips, 2))[::-1]
    after = {ring[n]: ring[(n + 1) % chips] for n in range(chips)}

    def permute(x, to):
        pairs = []
        for z in range(chips):
            for core in range(2):
                for place in range(inner):
                    nz, ncore, nplace = to(z, core, place)
                    pairs.append(
                        (
                            (2 * z + core) * inner + place,
                            (2 * nz + ncore) * inner + nplace,
                        )
                    )
        return lax.ppermute(x, AXES, pairs)

    def along_z(x):
        return permute(x, lambda z, core, place: (after[z], core, place))

    def over_place(x, step):
        def to(z, core, place):
            return z, core, place ^ (1 << (bits - 1 - step if core else step))

        return permute(x, to)

    def other_core(x):
        return permute(x, lambda z, core, place: (z, 1 - core, place))

    def tied(x, *others):
        return lax.optimization_barrier((x, *others))[0]

    by_run = values.reshape(2, RUN, heads_kv, head_dim).transpose(0, 2, 1, 3)
    numbers = (positions // RUN).astype(jnp.bfloat16)
    own = jnp.concatenate(
        [
            keys.reshape(tokens, -1).T,
            by_run.reshape(-1, head_dim),
            jnp.broadcast_to(numbers[None, :], (16, tokens)),
        ]
    )
    q = (
        queries.reshape(2, RUN, heads_kv, group, head_dim)
        .transpose(0, 2, 1, 3, 4)
        .reshape(2, heads_kv, RUN * group, head_dim)
    )
    block_rows = own.shape[0]

    attention = Attention(q, group, half, 2 * inner)
    state = attention.start(own)

    planes, ready = [], []
    stage = own
    for n in range(chips):
        following = along_z(stage) if n + 1 < chips else None
        if n < 2:
            held = stage
            for step in range(bits):
                if n == 0 and step == 1:
                    held = tied(held, following, state[0])
                there = over_place(held, step)
                held = jnp.concatenate([held, there])
            found = [
                held[m * block_rows : (m + 1) * block_rows] for m in range(inner)
            ]
        else:
            state = attention.add(state, ready[n - 2])
            found = [
                stage
                if m == 0
                else over_place(stage, m.bit_length() - 1)
                if m & (m - 1) == 0
                else along_z(tied(planes[-1][m], state[0]))
                for m in range(inner)
            ]
            held = jnp.concatenate(found)
        planes.append(found)
        stage = following
        if n + 1 < chips:
            ready.append([(held, int(n == 0)), other_core(held)])
    state = attention.add(state, ready[-1])
    held = tied(held, state[0])
    state = attention.add(state, [held])
    out = jax.ShapeDtypeStruct(queries.shape, queries.dtype)
    return attention.add(state, [other_core(held)], out)


def solution(mesh):
    in_specs = (
        P(("outer", "inner"), None, None),
        P(("outer", "inner"), None, None),
        P(("outer", "inner"), None, None),
        P(("outer", "inner")),
    )
    out_specs = P(("outer", "inner"), None, None)
    return jax.shard_map(
        per_device, mesh=mesh, in_specs=in_specs, out_specs=out_specs, check_vma=False
    )
```

```python
import functools
import math

import jax
import jax.numpy as jnp
from jax import lax
from jax.experimental import pallas as pl
from jax.experimental.pallas import tpu as pltpu
from jax.sharding import PartitionSpec as P

RUN = 64
TILE = 8
KEEP = 4
AXES = ("outer", "inner")


def flash(score, v, state, factor, live=None):
    top, total, mixed = state
    keys = score.shape[1]
    if isinstance(live, int):
        lane = lax.broadcasted_iota(jnp.int32, score.shape, 1)
        keys, live = live, lane < live
    if live is not None:
        score = jnp.where(live, score, -jnp.inf)
    parts = [score[:, c : c + 128] for c in range(0, score.shape[1], 128)]
    new = jnp.max(functools.reduce(jnp.maximum, parts), axis=1, keepdims=True)
    if top is None:
        new = jnp.broadcast_to(new, parts[0].shape)
    else:
        new = jnp.maximum(top, new)
    weights = [jnp.exp2((part - new) * factor) for part in parts]
    part_total = functools.reduce(jnp.add, weights)
    weights = jnp.concatenate([w.astype(jnp.bfloat16) for w in weights], axis=1)
    part_mixed = jnp.dot(weights[:, :keys], v, preferred_element_type=jnp.float32)
    if top is None:
        return new, part_total, part_mixed
    decay = jnp.exp2((top - new) * factor)
    return new, total * decay + part_total, mixed * decay + part_mixed


def head_tile(q_ref, state_refs, a, keys, values, factor, live=None):
    def scores(h):
        return lax.dot_general(
            q_ref[a, h],
            keys(h),
            (((1,), (1,)), ((), ())),
            preferred_element_type=jnp.float32,
        )

    heads_kv = q_ref.shape[1]
    ahead = scores(0)
    for h in range(heads_kv):
        score = ahead
        if h + 1 < heads_kv:
            ahead = scores(h + 1)
        state = (None, None, None)
        if live is None or isinstance(live, int):
            state = tuple(ref[a, h] for ref in state_refs)
        state = flash(score, values(h), state, factor, live)
        for ref, value in zip(state_refs, state):
            ref[a, h] = value


def own_kernel(group, factor, half, q_ref, own_ref, meta_ref, *refs):
    heads_kv, rows, head_dim = q_ref.shape[1:]
    state_refs = refs[:3]
    run_rows = 2 * heads_kv * RUN

    ids = own_ref[2 * run_rows :].astype(jnp.float32)
    lane = lax.broadcasted_iota(jnp.int32, ids.shape, 1)
    numbers = [jnp.max(jnp.where(lane // RUN == a, ids, 0.0)) for a in range(2)]
    row = lax.broadcasted_iota(jnp.int32, meta_ref.shape, 0)
    meta_ref[...] = jnp.where(
        row == 0, numbers[0], jnp.where(row == 1, numbers[1], 0.0)
    )

    row_at = lax.broadcasted_iota(jnp.int32, (rows, 2 * RUN), 0) // group
    key_at = lax.broadcasted_iota(jnp.int32, (rows, 2 * RUN), 1)
    for a in range(2):
        mine, other = numbers[a], numbers[1 - a]
        seen = (other < mine) & ((other >= half) == (mine >= half))
        reach = jnp.where(seen, RUN, 0)
        if a == 0:
            live = (key_at <= row_at) | ((key_at >= RUN) & (key_at < RUN + reach))
        else:
            live = (key_at < reach) | ((key_at >= RUN) & (key_at - RUN <= row_at))

        def own(g):
            starts = [g * RUN, run_rows + g * RUN]
            return jnp.concatenate([own_ref[n : n + RUN] for n in starts])

        head_tile(q_ref, state_refs, a, own, lambda h: own(heads_kv + h), factor, live)


def attend_kernel(group, factor, half, last, blocks, q_ref, *refs):
    heads_kv, rows, head_dim = q_ref.shape[1:]
    run_rows = 2 * heads_kv * RUN
    block_rows = 2 * run_rows + 16
    kv_refs, refs = refs[: len(blocks)], refs[len(blocks) :]
    refs = refs[5:]
    if last:
        out_ref, refs = refs[0], refs[1:]
    meta_ref, *state_refs, buf = refs

    meta = meta_ref[...]
    counts = tuple(
        jnp.max(meta[2 + a : 3 + a]).astype(jnp.int32) for a in range(2)
    )
    seen_bits = []
    for ref, (skip, end) in zip(kv_refs, blocks):
        assert end - skip <= 8
        ids = jnp.concatenate(
            [ref[n * block_rows - 16 : n * block_rows] for n in range(skip + 1, end + 1)]
        ).astype(jnp.float32)
        row = lax.broadcasted_iota(jnp.int32, ids.shape, 0)
        lane = lax.broadcasted_iota(jnp.int32, ids.shape, 1)
        bit = jnp.left_shift(1, 2 * (row // 16) + lane // RUN)
        bit = jnp.where((row % 16 == 0) & (lane % RUN == 0), bit, 0).astype(jnp.float32)
        found = []
        for a in range(2):
            mine = meta[a : a + 1]
            low = jnp.where(mine >= half, float(half), 0.0)
            seen = (ids < mine) & (ids >= low)
            found.append(jnp.sum(jnp.where(seen, bit, 0.0)).astype(jnp.int32))
        seen_bits.append(found)

    for ref, (skip, end), bits in zip(kv_refs, blocks, seen_bits):

        def gather(n, counts):
            at = pl.multiple_of((skip + n // 2) * block_rows + n % 2 * run_rows, 16)
            fresh = []
            for a in range(2):
                flag = (bits[a] >> n) & 1
                count = counts[a]

                @pl.when(flag == 1)
                def _():
                    buf[a, count] = ref[pl.ds(at, run_rows), :]

                fresh.append(count + flag)
            return tuple(fresh)

        counts = lax.fori_loop(0, 2 * (end - skip), gather, counts)

    def some_runs(a, start, runs):
        def rows_of(g):
            found = buf[a, pl.ds(start, runs), g * RUN : (g + 1) * RUN, :]
            return found.reshape(runs * RUN, -1)

        def keys(h):
            if runs > 1:
                return rows_of(h)
            return jnp.concatenate([rows_of(h), jnp.zeros((RUN, head_dim), buf.dtype)])

        live = RUN if runs == 1 else None
        head_tile(
            q_ref, state_refs, a, keys, lambda h: rows_of(heads_kv + h), factor, live
        )

    whole = [count // TILE for count in counts]

    def step(item, carry):
        a = (item >= whole[0]).astype(jnp.int32)
        some_runs(a, (item - a * whole[0]) * TILE, TILE)
        return carry

    lax.fori_loop(0, whole[0] + whole[1], step, 0)

    def remainder(a, carry):
        count = jnp.where(a == 0, counts[0], counts[1])
        start = count // TILE * TILE
        runs = TILE // 2
        while runs >= (1 if last else KEEP):

            @pl.when(count & runs != 0)
            def _():
                some_runs(a, start, runs)

            start = start + (count & runs)
            runs //= 2
        return carry

    lax.fori_loop(0, 2, remainder, 0)

    if not last:
        row = lax.broadcasted_iota(jnp.int32, meta.shape, 0)
        for a in range(2):
            start = counts[a] // KEEP * KEEP
            rest = counts[a] - start

            @pl.when((start > 0) & (rest > 0))
            def _():
                for n in range(KEEP - 1):
                    buf[a, n] = buf[a, start + n]

            meta = jnp.where(row == 2 + a, rest.astype(jnp.float32), meta)
        meta_ref[...] = meta
        return

    for a in range(2):
        for h in range(0, heads_kv, 2):
            done = []
            for g in (h, h + 1):
                total = jnp.sum(state_refs[1][a, g], axis=1, keepdims=True)
                part = state_refs[2][a, g] * (1.0 / total)
                done.append(part.reshape(RUN, group, -1))
            out_ref[a * RUN : (a + 1) * RUN, h * group : (h + 2) * group, :] = (
                jnp.concatenate(done, axis=1).astype(out_ref.dtype)
            )


class Attention:
    def __init__(self, q, group, half, room):
        self.q, self.group, self.half = q, group, half
        self.factor = math.log2(math.e) / math.sqrt(q.shape[3])
        heads_kv, rows, head_dim = q.shape[1:]
        self.block_rows = 4 * heads_kv * RUN + 16
        slots = 2 * room + KEEP
        self.carried = [jax.ShapeDtypeStruct((8, 128), jnp.float32)]
        self.carried += [
            jax.ShapeDtypeStruct((2, heads_kv, rows, n), jnp.float32)
            for n in (128, 128, head_dim)
        ]
        self.carried.append(
            jax.ShapeDtypeStruct((2, slots, 2 * heads_kv * RUN, head_dim), q.dtype)
        )

    def call(self, kernel, operands, shapes, aliases, count, name):
        vmem = pl.BlockSpec(memory_space=pltpu.VMEM)
        return pl.pallas_call(
            kernel,
            out_shape=shapes,
            in_specs=[vmem] * len(operands),
            out_specs=[vmem] * len(shapes),
            input_output_aliases=aliases,
            compiler_params=pltpu.CompilerParams(vmem_limit_bytes=28 * 1024 * 1024),
            cost_estimate=pl.CostEstimate(
                flops=count * RUN * self.q.size * 4,
                bytes_accessed=self.q.size * 8,
                transcendentals=0,
            ),
            name=name,
        )(*operands)

    def start(self, own):
        kernel = functools.partial(own_kernel, self.group, self.factor, self.half)
        return self.call(kernel, [self.q, own], self.carried, {}, 2, "attend_own")

    def add(self, state, kvs, out=None):
        kvs = [x if isinstance(x, tuple) else (x, 0) for x in kvs]
        blocks = [(skip, x.shape[0] // self.block_rows) for x, skip in kvs]
        count = sum(end - skip for skip, end in blocks)
        operands = [self.q, *(x for x, _ in kvs), *state]
        first, ahead = 1 + len(kvs), int(out is not None)
        aliases = {first + n: ahead + n for n in range(len(state))}
        shapes = ([out] if ahead else []) + self.carried
        kernel = functools.partial(
            attend_kernel, self.group, self.factor, self.half, out is not None, blocks
        )
        results = self.call(kernel, operands, shapes, aliases, count, "attend")
        return results[0] if ahead else results


def per_device(queries, keys, values, positions):
    outer, inner = lax.axis_size("outer"), lax.axis_size("inner")
    tokens, heads_q, head_dim = queries.shape
    heads_kv = keys.shape[1]
    group = heads_q // heads_kv
    half = tokens // RUN * outer * inner // 2

    chips = outer // 2
    bits = inner.bit_length() - 1
    ring = [0] + list(range(1, chips, 2)) + list(range(2, chips, 2))[::-1]
    after = {ring[n]: ring[(n + 1) % chips] for n in range(chips)}

    def permute(x, to):
        pairs = []
        for z in range(chips):
            for core in range(2):
                for place in range(inner):
                    nz, ncore, nplace = to(z, core, place)
                    pairs.append(
                        (
                            (2 * z + core) * inner + place,
                            (2 * nz + ncore) * inner + nplace,
                        )
                    )
        return lax.ppermute(x, AXES, pairs)

    def along_z(x):
        return permute(x, lambda z, core, place: (after[z], core, place))

    def over_place(x, step):
        def to(z, core, place):
            return z, core, place ^ (1 << (bits - 1 - step if core else step))

        return permute(x, to)

    def other_core(x):
        return permute(x, lambda z, core, place: (z, 1 - core, place))

    def tied(x, *others):
        return lax.optimization_barrier((x, *others))[0]

    by_run = jnp.concatenate(
        [x.reshape(2, RUN, heads_kv, head_dim) for x in (keys, values)], axis=2
    ).transpose(0, 2, 1, 3)
    numbers = (positions // RUN).astype(jnp.bfloat16)
    own = jnp.concatenate(
        [
            by_run.reshape(-1, head_dim),
            jnp.broadcast_to(numbers[None, :], (16, head_dim)),
        ]
    )
    q = (
        queries.reshape(2, RUN, heads_kv, group, head_dim)
        .transpose(0, 2, 1, 3, 4)
        .reshape(2, heads_kv, RUN * group, head_dim)
    )
    block_rows = own.shape[0]

    attention = Attention(q, group, half, 2 * inner)
    state = attention.start(own)

    planes, ready = [], []
    stage = own
    for n in range(chips):
        following = along_z(stage) if n + 1 < chips else None
        if n < 2:
            held = stage
            for step in range(bits):
                if n == 0 and step == 1:
                    held = tied(held, following, state[0])
                there = over_place(held, step)
                held = jnp.concatenate([held, there])
            found = [
                held[m * block_rows : (m + 1) * block_rows] for m in range(inner)
            ]
        else:
            found = [
                stage
                if m == 0
                else over_place(
                    tied(stage, planes[-1][-1]) if n > 2 and m > 1 else stage,
                    m.bit_length() - 1,
                )
                if m & (m - 1) == 0
                else along_z(planes[-1][m])
                for m in range(inner)
            ]
            if n + 1 == chips:
                for kvs in ready[:-1]:
                    state = attention.add(state, kvs)
                found[-1] = tied(found[-1], state[0])
            held = jnp.concatenate(found)
        planes.append(found)
        stage = following
        if n + 1 < chips:
            ready.append([(held, int(n == 0)), other_core(held)])
    state = attention.add(state, ready[-1])
    state = attention.add(state, [held])
    out = jax.ShapeDtypeStruct(queries.shape, queries.dtype)
    return attention.add(state, [other_core(held)], out)


def solution(mesh):
    in_specs = (
        P(("outer", "inner"), None, None),
        P(("outer", "inner"), None, None),
        P(("outer", "inner"), None, None),
        P(("outer", "inner")),
    )
    out_specs = P(("outer", "inner"), None, None)
    return jax.shard_map(
        per_device, mesh=mesh, in_specs=in_specs, out_specs=out_specs, check_vma=False
    )
```

```python
import functools
import math

import jax
import jax.numpy as jnp
from jax import lax
from jax.experimental import pallas as pl
from jax.experimental.pallas import tpu as pltpu
from jax.sharding import PartitionSpec as P

RUN = 64
TILE = 8
KEEP = 4
AXES = ("outer", "inner")


def flash(score, v, state, factor, live=None):
    top, total, mixed = state
    keys = score.shape[1]
    if isinstance(live, int):
        lane = lax.broadcasted_iota(jnp.int32, score.shape, 1)
        keys, live = live, lane < live
    if live is not None:
        score = jnp.where(live, score, -jnp.inf)
    parts = [score[:, c : c + 128] for c in range(0, score.shape[1], 128)]
    new = jnp.max(functools.reduce(jnp.maximum, parts), axis=1, keepdims=True)
    if top is None:
        new = jnp.broadcast_to(new, parts[0].shape)
    else:
        new = jnp.maximum(top, new)
    weights = [jnp.exp2((part - new) * factor) for part in parts]
    part_total = functools.reduce(jnp.add, weights)
    weights = jnp.concatenate([w.astype(jnp.bfloat16) for w in weights], axis=1)
    part_mixed = jnp.dot(weights[:, :keys], v, preferred_element_type=jnp.float32)
    if top is None:
        return new, part_total, part_mixed
    decay = jnp.exp2((top - new) * factor)
    return new, total * decay + part_total, mixed * decay + part_mixed


def head_tile(q_ref, state_refs, a, keys, values, factor, live=None):
    def scores(h):
        return lax.dot_general(
            q_ref[a, h],
            keys(h),
            (((1,), (1,)), ((), ())),
            preferred_element_type=jnp.float32,
        )

    heads_kv = q_ref.shape[1]
    ahead = scores(0)
    for h in range(heads_kv):
        score = ahead
        if h + 1 < heads_kv:
            ahead = scores(h + 1)
        state = (None, None, None)
        if live is None or isinstance(live, int):
            state = tuple(ref[a, h] for ref in state_refs)
        state = flash(score, values(h), state, factor, live)
        for ref, value in zip(state_refs, state):
            ref[a, h] = value


def own_kernel(group, factor, half, q_ref, own_ref, meta_ref, *refs):
    heads_kv, rows, head_dim = q_ref.shape[1:]
    state_refs = refs[:3]
    run_rows = 2 * heads_kv * RUN

    ids = own_ref[2 * run_rows :].astype(jnp.float32)
    lane = lax.broadcasted_iota(jnp.int32, ids.shape, 1)
    numbers = [jnp.max(jnp.where(lane // RUN == a, ids, 0.0)) for a in range(2)]
    row = lax.broadcasted_iota(jnp.int32, meta_ref.shape, 0)
    meta_ref[...] = jnp.where(
        row == 0, numbers[0], jnp.where(row == 1, numbers[1], 0.0)
    )

    row_at = lax.broadcasted_iota(jnp.int32, (rows, 2 * RUN), 0) // group
    key_at = lax.broadcasted_iota(jnp.int32, (rows, 2 * RUN), 1)
    for a in range(2):
        mine, other = numbers[a], numbers[1 - a]
        seen = (other < mine) & ((other >= half) == (mine >= half))
        reach = jnp.where(seen, RUN, 0)
        if a == 0:
            live = (key_at <= row_at) | ((key_at >= RUN) & (key_at < RUN + reach))
        else:
            live = (key_at < reach) | ((key_at >= RUN) & (key_at - RUN <= row_at))

        def own(g):
            starts = [g * RUN, run_rows + g * RUN]
            return jnp.concatenate([own_ref[n : n + RUN] for n in starts])

        head_tile(q_ref, state_refs, a, own, lambda h: own(heads_kv + h), factor, live)


def attend_kernel(group, factor, half, last, blocks, q_ref, *refs):
    heads_kv, rows, head_dim = q_ref.shape[1:]
    run_rows = 2 * heads_kv * RUN
    block_rows = 2 * run_rows + 16
    kv_refs, refs = refs[: len(blocks)], refs[len(blocks) :]
    refs = refs[5:]
    if last:
        out_ref, refs = refs[0], refs[1:]
    meta_ref, *state_refs, buf = refs

    meta = meta_ref[...]
    counts = tuple(
        jnp.max(meta[2 + a : 3 + a]).astype(jnp.int32) for a in range(2)
    )
    seen_bits = []
    for ref, (skip, end) in zip(kv_refs, blocks):
        assert end - skip <= 8
        ids = jnp.concatenate(
            [ref[n * block_rows - 16 : n * block_rows] for n in range(skip + 1, end + 1)]
        ).astype(jnp.float32)
        row = lax.broadcasted_iota(jnp.int32, ids.shape, 0)
        lane = lax.broadcasted_iota(jnp.int32, ids.shape, 1)
        bit = jnp.left_shift(1, 2 * (row // 16) + lane // RUN)
        bit = jnp.where((row % 16 == 0) & (lane % RUN == 0), bit, 0).astype(jnp.float32)
        found = []
        for a in range(2):
            mine = meta[a : a + 1]
            low = jnp.where(mine >= half, float(half), 0.0)
            seen = (ids < mine) & (ids >= low)
            found.append(jnp.sum(jnp.where(seen, bit, 0.0)).astype(jnp.int32))
        seen_bits.append(found)

    for ref, (skip, end), bits in zip(kv_refs, blocks, seen_bits):

        def gather(n, counts):
            at = pl.multiple_of((skip + n // 2) * block_rows + n % 2 * run_rows, 16)
            fresh = []
            for a in range(2):
                flag = (bits[a] >> n) & 1
                count = counts[a]

                @pl.when(flag == 1)
                def _():
                    buf[a, count] = ref[pl.ds(at, run_rows), :]

                fresh.append(count + flag)
            return tuple(fresh)

        counts = lax.fori_loop(0, 2 * (end - skip), gather, counts)

    def some_runs(a, start, runs):
        def rows_of(g):
            found = buf[a, pl.ds(start, runs), g * RUN : (g + 1) * RUN, :]
            return found.reshape(runs * RUN, -1)

        def keys(h):
            if runs > 1:
                return rows_of(h)
            return jnp.concatenate([rows_of(h), jnp.zeros((RUN, head_dim), buf.dtype)])

        live = RUN if runs == 1 else None
        head_tile(
            q_ref, state_refs, a, keys, lambda h: rows_of(heads_kv + h), factor, live
        )

    whole = [count // TILE for count in counts]

    def step(item, carry):
        a = (item >= whole[0]).astype(jnp.int32)
        some_runs(a, (item - a * whole[0]) * TILE, TILE)
        return carry

    lax.fori_loop(0, whole[0] + whole[1], step, 0)

    def remainder(a, carry):
        count = jnp.where(a == 0, counts[0], counts[1])
        start = count // TILE * TILE
        runs = TILE // 2
        while runs >= (1 if last else KEEP):

            @pl.when(count & runs != 0)
            def _():
                some_runs(a, start, runs)

            start = start + (count & runs)
            runs //= 2
        return carry

    lax.fori_loop(0, 2, remainder, 0)

    if not last:
        row = lax.broadcasted_iota(jnp.int32, meta.shape, 0)
        for a in range(2):
            start = counts[a] // KEEP * KEEP
            rest = counts[a] - start

            @pl.when((start > 0) & (rest > 0))
            def _():
                for n in range(KEEP - 1):
                    buf[a, n] = buf[a, start + n]

            meta = jnp.where(row == 2 + a, rest.astype(jnp.float32), meta)
        meta_ref[...] = meta
        return

    for a in range(2):
        for h in range(0, heads_kv, 2):
            done = []
            for g in (h, h + 1):
                total = jnp.sum(state_refs[1][a, g], axis=1, keepdims=True)
                part = state_refs[2][a, g] * (1.0 / total)
                done.append(part.reshape(RUN, group, -1))
            out_ref[a * RUN : (a + 1) * RUN, h * group : (h + 2) * group, :] = (
                jnp.concatenate(done, axis=1).astype(out_ref.dtype)
            )


class Attention:
    def __init__(self, q, group, half, room):
        self.q, self.group, self.half = q, group, half
        self.factor = math.log2(math.e) / math.sqrt(q.shape[3])
        heads_kv, rows, head_dim = q.shape[1:]
        self.block_rows = 4 * heads_kv * RUN + 16
        slots = 2 * room + KEEP
        self.carried = [jax.ShapeDtypeStruct((8, 128), jnp.float32)]
        self.carried += [
            jax.ShapeDtypeStruct((2, heads_kv, rows, n), jnp.float32)
            for n in (128, 128, head_dim)
        ]
        self.carried.append(
            jax.ShapeDtypeStruct((2, slots, 2 * heads_kv * RUN, head_dim), q.dtype)
        )

    def call(self, kernel, operands, shapes, aliases, count, name):
        vmem = pl.BlockSpec(memory_space=pltpu.VMEM)
        return pl.pallas_call(
            kernel,
            out_shape=shapes,
            in_specs=[vmem] * len(operands),
            out_specs=[vmem] * len(shapes),
            input_output_aliases=aliases,
            compiler_params=pltpu.CompilerParams(vmem_limit_bytes=28 * 1024 * 1024),
            cost_estimate=pl.CostEstimate(
                flops=count * RUN * self.q.size * 4,
                bytes_accessed=self.q.size * 8,
                transcendentals=0,
            ),
            name=name,
        )(*operands)

    def start(self, own):
        kernel = functools.partial(own_kernel, self.group, self.factor, self.half)
        return self.call(kernel, [self.q, own], self.carried, {}, 2, "attend_own")

    def add(self, state, kvs, out=None):
        kvs = [x if isinstance(x, tuple) else (x, 0) for x in kvs]
        blocks = [(skip, x.shape[0] // self.block_rows) for x, skip in kvs]
        count = sum(end - skip for skip, end in blocks)
        operands = [self.q, *(x for x, _ in kvs), *state]
        first, ahead = 1 + len(kvs), int(out is not None)
        aliases = {first + n: ahead + n for n in range(len(state))}
        shapes = ([out] if ahead else []) + self.carried
        kernel = functools.partial(
            attend_kernel, self.group, self.factor, self.half, out is not None, blocks
        )
        results = self.call(kernel, operands, shapes, aliases, count, "attend")
        return results[0] if ahead else results


def per_device(queries, keys, values, positions):
    outer, inner = lax.axis_size("outer"), lax.axis_size("inner")
    tokens, heads_q, head_dim = queries.shape
    heads_kv = keys.shape[1]
    group = heads_q // heads_kv
    half = tokens // RUN * outer * inner // 2

    chips = outer // 2
    bits = inner.bit_length() - 1
    ring = [0] + list(range(1, chips, 2)) + list(range(2, chips, 2))[::-1]
    after = {ring[n]: ring[(n + 1) % chips] for n in range(chips)}

    def permute(x, to):
        pairs = []
        for z in range(chips):
            for core in range(2):
                for place in range(inner):
                    nz, ncore, nplace = to(z, core, place)
                    pairs.append(
                        (
                            (2 * z + core) * inner + place,
                            (2 * nz + ncore) * inner + nplace,
                        )
                    )
        return lax.ppermute(x, AXES, pairs)

    def along_z(x):
        return permute(x, lambda z, core, place: (after[z], core, place))

    def over_place(x, step):
        def to(z, core, place):
            return z, core, place ^ (1 << (bits - 1 - step if core else step))

        return permute(x, to)

    def other_core(x):
        return permute(x, lambda z, core, place: (z, 1 - core, place))

    def tied(x, *others):
        return lax.optimization_barrier((x, *others))[0]

    by_run = jnp.concatenate(
        [x.reshape(2, RUN, heads_kv, head_dim) for x in (keys, values)], axis=2
    ).transpose(0, 2, 1, 3)
    numbers = (positions // RUN).astype(jnp.bfloat16)
    own = jnp.concatenate(
        [
            by_run.reshape(-1, head_dim),
            jnp.broadcast_to(numbers[None, :], (16, head_dim)),
        ]
    )
    q = (
        queries.reshape(2, RUN, heads_kv, group, head_dim)
        .transpose(0, 2, 1, 3, 4)
        .reshape(2, heads_kv, RUN * group, head_dim)
    )

    attention = Attention(q, group, half, 2 * inner)
    state = attention.start(own)

    stage, waiting = own, None
    for n in range(chips - 1):
        following = along_z(stage)
        held = stage
        for step in range(bits):
            if n == 0 and step == 1:
                held = tied(held, following, state[0])
            held = jnp.concatenate([held, over_place(held, step)])
        if waiting:
            state = attention.add(state, waiting)
            held = tied(held, state[0])
        waiting = [(held, int(n == 0)), other_core(held)]
        stage = following

    found = [stage]
    for step in range(bits):
        found += [over_place(x, step) for x in found]
    *most, final = found
    most = jnp.concatenate(most)
    theirs = other_core(most)
    state = attention.add(state, waiting)
    state = attention.add(state, [most, theirs])
    final = tied(final, state[0])
    theirs = other_core(final)
    state = attention.add(state, [final])
    out = jax.ShapeDtypeStruct(queries.shape, queries.dtype)
    return attention.add(state, [theirs], out)


def solution(mesh):
    in_specs = (
        P(("outer", "inner"), None, None),
        P(("outer", "inner"), None, None),
        P(("outer", "inner"), None, None),
        P(("outer", "inner")),
    )
    out_specs = P(("outer", "inner"), None, None)
    return jax.shard_map(
        per_device, mesh=mesh, in_specs=in_specs, out_specs=out_specs, check_vma=False
    )
```

```python
import functools
import math

import jax
import jax.numpy as jnp
from jax import lax
from jax.experimental import pallas as pl
from jax.experimental.pallas import tpu as pltpu
from jax.sharding import PartitionSpec as P

RUN = 64
TILE = 8
KEEP = 4
AXES = ("outer", "inner")


def flash(score, v, state, factor, live=None):
    top, total, mixed = state
    keys = score.shape[1]
    if isinstance(live, int):
        lane = lax.broadcasted_iota(jnp.int32, score.shape, 1)
        keys, live = live, lane < live
    if live is not None:
        score = jnp.where(live, score, -jnp.inf)
    parts = [score[:, c : c + 128] for c in range(0, score.shape[1], 128)]
    new = jnp.max(functools.reduce(jnp.maximum, parts), axis=1, keepdims=True)
    if top is None:
        new = jnp.broadcast_to(new, parts[0].shape)
    else:
        new = jnp.maximum(top, new)
    weights = [jnp.exp2((part - new) * factor) for part in parts]
    part_total = functools.reduce(jnp.add, weights)
    weights = jnp.concatenate([w.astype(jnp.bfloat16) for w in weights], axis=1)
    part_mixed = jnp.dot(weights[:, :keys], v, preferred_element_type=jnp.float32)
    if top is None:
        return new, part_total, part_mixed
    decay = jnp.exp2((top - new) * factor)
    return new, total * decay + part_total, mixed * decay + part_mixed


def head_tile(q_ref, state_refs, a, keys, values, factor, live=None):
    def scores(h):
        return lax.dot_general(
            q_ref[a, h],
            keys(h),
            (((1,), (1,)), ((), ())),
            preferred_element_type=jnp.float32,
        )

    heads_kv = q_ref.shape[1]
    ahead = scores(0)
    for h in range(heads_kv):
        score = ahead
        if h + 1 < heads_kv:
            ahead = scores(h + 1)
        state = (None, None, None)
        if live is None or isinstance(live, int):
            state = tuple(ref[a, h] for ref in state_refs)
        state = flash(score, values(h), state, factor, live)
        for ref, value in zip(state_refs, state):
            ref[a, h] = value


def own_kernel(group, factor, half, q_ref, own_ref, meta_ref, *refs):
    heads_kv, rows, head_dim = q_ref.shape[1:]
    state_refs = refs[:3]
    run_rows = 2 * heads_kv * RUN

    ids = own_ref[2 * run_rows :].astype(jnp.float32)
    lane = lax.broadcasted_iota(jnp.int32, ids.shape, 1)
    numbers = [jnp.max(jnp.where(lane // RUN == a, ids, 0.0)) for a in range(2)]
    row = lax.broadcasted_iota(jnp.int32, meta_ref.shape, 0)
    meta_ref[...] = jnp.where(
        row == 0, numbers[0], jnp.where(row == 1, numbers[1], 0.0)
    )

    row_at = lax.broadcasted_iota(jnp.int32, (rows, 2 * RUN), 0) // group
    key_at = lax.broadcasted_iota(jnp.int32, (rows, 2 * RUN), 1)
    for a in range(2):
        mine, other = numbers[a], numbers[1 - a]
        seen = (other < mine) & ((other >= half) == (mine >= half))
        reach = jnp.where(seen, RUN, 0)
        if a == 0:
            live = (key_at <= row_at) | ((key_at >= RUN) & (key_at < RUN + reach))
        else:
            live = (key_at < reach) | ((key_at >= RUN) & (key_at - RUN <= row_at))

        def own(g):
            starts = [g * RUN, run_rows + g * RUN]
            return jnp.concatenate([own_ref[n : n + RUN] for n in starts])

        head_tile(q_ref, state_refs, a, own, lambda h: own(heads_kv + h), factor, live)


def attend_kernel(group, factor, half, last, keep, blocks, q_ref, *refs):
    heads_kv, rows, head_dim = q_ref.shape[1:]
    run_rows = 2 * heads_kv * RUN
    block_rows = 2 * run_rows + 16
    kv_refs, refs = refs[: len(blocks)], refs[len(blocks) :]
    refs = refs[5:]
    if last:
        out_ref, refs = refs[0], refs[1:]
    meta_ref, *state_refs, buf = refs[:5]

    meta = meta_ref[...]
    counts = tuple(
        jnp.max(meta[2 + a : 3 + a]).astype(jnp.int32) for a in range(2)
    )
    seen_bits = []
    for ref, (skip, end) in zip(kv_refs, blocks):
        assert end - skip <= 8
        ids = jnp.concatenate(
            [ref[n * block_rows - 16 : n * block_rows] for n in range(skip + 1, end + 1)]
        ).astype(jnp.float32)
        row = lax.broadcasted_iota(jnp.int32, ids.shape, 0)
        lane = lax.broadcasted_iota(jnp.int32, ids.shape, 1)
        bit = jnp.left_shift(1, 2 * (row // 16) + lane // RUN)
        bit = jnp.where((row % 16 == 0) & (lane % RUN == 0), bit, 0).astype(jnp.float32)
        found = []
        for a in range(2):
            mine = meta[a : a + 1]
            low = jnp.where(mine >= half, float(half), 0.0)
            seen = (ids < mine) & (ids >= low)
            found.append(jnp.sum(jnp.where(seen, bit, 0.0)).astype(jnp.int32))
        seen_bits.append(found)

    for ref, (skip, end), bits in zip(kv_refs, blocks, seen_bits):

        def gather(n, counts):
            at = pl.multiple_of((skip + n // 2) * block_rows + n % 2 * run_rows, 16)
            fresh = []
            for a in range(2):
                flag = (bits[a] >> n) & 1
                count = counts[a]

                @pl.when(flag == 1)
                def _():
                    buf[a, count] = ref[pl.ds(at, run_rows), :]

                fresh.append(count + flag)
            return tuple(fresh)

        counts = lax.fori_loop(0, 2 * (end - skip), gather, counts)

    def some_runs(a, start, runs):
        def rows_of(g):
            found = buf[a, pl.ds(start, runs), g * RUN : (g + 1) * RUN, :]
            return found.reshape(runs * RUN, -1)

        def keys(h):
            if runs > 1:
                return rows_of(h)
            return jnp.concatenate([rows_of(h), jnp.zeros((RUN, head_dim), buf.dtype)])

        live = RUN if runs == 1 else None
        head_tile(
            q_ref, state_refs, a, keys, lambda h: rows_of(heads_kv + h), factor, live
        )

    whole = [count // TILE for count in counts]

    def step(item, carry):
        a = (item >= whole[0]).astype(jnp.int32)
        some_runs(a, (item - a * whole[0]) * TILE, TILE)
        return carry

    lax.fori_loop(0, whole[0] + whole[1], step, 0)

    def remainder(a, carry):
        count = jnp.where(a == 0, counts[0], counts[1])
        start = count // TILE * TILE
        runs = TILE // 2
        while runs >= keep:

            @pl.when(count & runs != 0)
            def _():
                some_runs(a, start, runs)

            start = start + (count & runs)
            runs //= 2
        return carry

    lax.fori_loop(0, 2, remainder, 0)

    if not last:
        row = lax.broadcasted_iota(jnp.int32, meta.shape, 0)
        for a in range(2):
            start = counts[a] // keep * keep
            rest = counts[a] - start
            if keep > 1:

                @pl.when((start > 0) & (rest > 0))
                def _():
                    for n in range(keep - 1):
                        buf[a, n] = buf[a, start + n]

            meta = jnp.where(row == 2 + a, rest.astype(jnp.float32), meta)
        meta_ref[...] = meta
        return

    made, sems = refs[5:]
    copies = []
    for a in range(2):
        for h in range(0, heads_kv, 2):
            done = []
            for g in (h, h + 1):
                total = jnp.sum(state_refs[1][a, g], axis=1, keepdims=True)
                part = state_refs[2][a, g] * (1.0 / total)
                done.append(part.reshape(RUN, group, -1))
            place = (slice(a * RUN, (a + 1) * RUN), slice(h * group, (h + 2) * group))
            made[place] = jnp.concatenate(done, axis=1).astype(out_ref.dtype)
            copy = pltpu.make_async_copy(
                made.at[place], out_ref.at[place], sems.at[len(copies)]
            )
            copy.start()
            copies.append(copy)
    for copy in copies:
        copy.wait()


def pack_kernel(k_any, v_any, positions_any, own_ref, k_ref, v_ref, positions_ref, sems):
    pairs = ((k_any, k_ref), (v_any, v_ref), (positions_any, positions_ref))
    copies = [
        pltpu.make_async_copy(source, target, sems.at[n])
        for n, (source, target) in enumerate(pairs)
    ]
    for copy in copies:
        copy.start()
    heads_kv = k_ref.shape[0] // (2 * RUN)
    rows = heads_kv * RUN
    at = lax.broadcasted_iota(jnp.int32, (rows, rows), 0)
    origin = lax.broadcasted_iota(jnp.int32, (rows, rows), 1)
    move = at % RUN * heads_kv + at // RUN == origin
    move = jnp.where(move, 1.0, 0.0).astype(k_ref.dtype)
    for n, ref in enumerate((k_ref, v_ref)):
        copies[n].wait()
        for r in range(2):
            moved = jnp.dot(
                move,
                ref[r * rows : (r + 1) * rows],
                preferred_element_type=jnp.float32,
            )
            start = (2 * r + n) * rows
            own_ref[start : start + rows] = moved.astype(own_ref.dtype)
    copies[2].wait()
    numbers = (positions_ref[...] // RUN).astype(jnp.float32)
    numbers = jnp.broadcast_to(numbers, (16, numbers.shape[1]))
    own_ref[4 * rows :] = numbers.astype(own_ref.dtype)


class Attention:
    def __init__(self, q, group, half, room):
        self.q, self.group, self.half = q, group, half
        self.factor = math.log2(math.e) / math.sqrt(q.shape[3])
        heads_kv, rows, head_dim = q.shape[1:]
        self.block_rows = 4 * heads_kv * RUN + 16
        slots = 2 * room + KEEP
        self.carried = [jax.ShapeDtypeStruct((8, 128), jnp.float32)]
        self.carried += [
            jax.ShapeDtypeStruct((2, heads_kv, rows, n), jnp.float32)
            for n in (128, 128, head_dim)
        ]
        self.carried.append(
            jax.ShapeDtypeStruct((2, slots, 2 * heads_kv * RUN, head_dim), q.dtype)
        )

    def call(self, kernel, operands, shapes, aliases, count, name, out=None):
        vmem = pl.BlockSpec(memory_space=pltpu.VMEM)
        out_specs = [vmem] * len(shapes)
        scratch = []
        if out is not None:
            shapes = [out, *shapes]
            out_specs.insert(0, pl.BlockSpec(memory_space=pl.ANY))
            scratch = [pltpu.VMEM(out.shape, out.dtype), pltpu.SemaphoreType.DMA((8,))]
        return pl.pallas_call(
            kernel,
            out_shape=shapes,
            in_specs=[vmem] * len(operands),
            out_specs=out_specs,
            scratch_shapes=scratch,
            input_output_aliases=aliases,
            compiler_params=pltpu.CompilerParams(vmem_limit_bytes=28 * 1024 * 1024),
            cost_estimate=pl.CostEstimate(
                flops=count * RUN * self.q.size * 4,
                bytes_accessed=self.q.size * 8,
                transcendentals=0,
            ),
            name=name,
        )(*operands)

    def start(self, own):
        kernel = functools.partial(own_kernel, self.group, self.factor, self.half)
        return self.call(kernel, [self.q, own], self.carried, {}, 2, "attend_own")

    def add(self, state, kvs, keep=KEEP, out=None):
        kvs = [x if isinstance(x, tuple) else (x, 0) for x in kvs]
        blocks = [(skip, x.shape[0] // self.block_rows) for x, skip in kvs]
        count = sum(end - skip for skip, end in blocks)
        operands = [self.q, *(x for x, _ in kvs), *state]
        first, ahead = 1 + len(kvs), int(out is not None)
        aliases = {first + n: ahead + n for n in range(len(state))}
        kernel = functools.partial(
            attend_kernel, self.group, self.factor, self.half, ahead, keep, blocks
        )
        results = self.call(kernel, operands, self.carried, aliases, count, "attend", out)
        return results[0] if ahead else results


def per_device(queries, keys, values, positions):
    outer, inner = lax.axis_size("outer"), lax.axis_size("inner")
    tokens, heads_q, head_dim = queries.shape
    heads_kv = keys.shape[1]
    group = heads_q // heads_kv
    half = tokens // RUN * outer * inner // 2

    chips = outer // 2
    bits = inner.bit_length() - 1
    ring = [0] + list(range(1, chips, 2)) + list(range(2, chips, 2))[::-1]
    after = {ring[n]: ring[(n + 1) % chips] for n in range(chips)}

    def permute(x, to):
        pairs = []
        for z in range(chips):
            for core in range(2):
                for place in range(inner):
                    nz, ncore, nplace = to(z, core, place)
                    pairs.append(
                        (
                            (2 * z + core) * inner + place,
                            (2 * nz + ncore) * inner + nplace,
                        )
                    )
        return lax.ppermute(x, AXES, pairs)

    def along_z(x):
        return permute(x, lambda z, core, place: (after[z], core, place))

    def over_place(x, step):
        def to(z, core, place):
            return z, core, place ^ (1 << (bits - 1 - step if core else step))

        return permute(x, to)

    def other_core(x):
        return permute(x, lambda z, core, place: (z, 1 - core, place))

    def tied(x, *others):
        return lax.optimization_barrier((x, *others))[0]

    flat = jax.ShapeDtypeStruct((tokens * heads_kv, head_dim), keys.dtype)
    own = pl.pallas_call(
        pack_kernel,
        out_shape=jax.ShapeDtypeStruct(
            (2 * tokens * heads_kv + 16, head_dim), keys.dtype
        ),
        in_specs=[pl.BlockSpec(memory_space=pltpu.HBM)] * 3,
        out_specs=pl.BlockSpec(memory_space=pltpu.VMEM),
        scratch_shapes=[
            pltpu.VMEM(flat.shape, flat.dtype),
            pltpu.VMEM(flat.shape, flat.dtype),
            pltpu.VMEM((1, tokens), jnp.int32),
            pltpu.SemaphoreType.DMA((3,)),
        ],
        compiler_params=pltpu.CompilerParams(vmem_limit_bytes=60 * 1024 * 1024),
        name="pack",
    )(keys.reshape(flat.shape), values.reshape(flat.shape), positions.reshape(1, tokens))
    q = (
        queries.reshape(2, RUN, heads_kv, group, head_dim)
        .transpose(0, 2, 1, 3, 4)
        .reshape(2, heads_kv, RUN * group, head_dim)
    )

    attention = Attention(q, group, half, 2 * inner)
    state = attention.start(own)

    single = [1 << step for step in range(bits)]
    several = [m for m in range(1, inner) if m not in single]

    stages = [own]
    for n in range(1, chips):
        stages.append(along_z(stages[-1]))
    planes, ready = [], []
    for n in range(chips):
        stage = stages[n]
        before = planes[n - 1] if n else {}
        if n:
            earlier = [before[m] for m in single]
            if n > 1:
                earlier += [planes[n - 2][m] for m in several]
            if n > 2:
                state = attention.add(state, ready[n - 3])
                earlier.append(state[0])
            stage = tied(stage, *earlier)
        found = {0: stage}
        for step in range(bits):
            found[1 << step] = over_place(stage, step)
        if n + 1 < chips:
            wait_for = [stages[n + 1]] + ([state[0]] if n == 0 else [])
        else:
            state = attention.add(state, ready[n - 2])
            wait_for = [state[0]]
        for m in several:
            if n + 2 == chips:
                found[m] = along_z(tied(before[m], *wait_for))
            else:
                top = m.bit_length() - 1
                found[m] = over_place(tied(found[m - (1 << top)], *wait_for), top)
        planes.append(found)
        if n + 1 < chips:
            held = jnp.concatenate([found[m] for m in range(inner)])
            ready.append([(held, int(n == 0)), other_core(held)])
    waiting = ready[-1]
    *most, final = (found[m] for m in range(inner))
    most = jnp.concatenate(most)
    theirs = other_core(most)
    state = attention.add(state, waiting)
    state = attention.add(state, [most, theirs])
    final = tied(final, state[0])
    theirs = other_core(final)
    state = attention.add(state, [final], keep=1)
    out = jax.ShapeDtypeStruct(queries.shape, queries.dtype)
    return attention.add(state, [theirs], keep=1, out=out)


def solution(mesh):
    in_specs = (
        P(("outer", "inner"), None, None),
        P(("outer", "inner"), None, None),
        P(("outer", "inner"), None, None),
        P(("outer", "inner")),
    )
    out_specs = P(("outer", "inner"), None, None)
    return jax.shard_map(
        per_device, mesh=mesh, in_specs=in_specs, out_specs=out_specs, check_vma=False
    )
```

```python
import functools
import math

import jax
import jax.numpy as jnp
from jax import lax
from jax.experimental import pallas as pl
from jax.experimental.pallas import tpu as pltpu
from jax.sharding import PartitionSpec as P

RUN = 64
TILE = 8
KEEP = 4
AXES = ("outer", "inner")


def flash(score, v, state, factor, live=None):
    top, total, mixed = state
    keys = score.shape[1]
    if isinstance(live, int):
        lane = lax.broadcasted_iota(jnp.int32, score.shape, 1)
        keys, live = live, lane < live
    if live is not None:
        score = jnp.where(live, score, -jnp.inf)
    parts = [score[:, c : c + 128] for c in range(0, score.shape[1], 128)]
    new = jnp.max(functools.reduce(jnp.maximum, parts), axis=1, keepdims=True)
    if top is None:
        new = jnp.broadcast_to(new, parts[0].shape)
    else:
        new = jnp.maximum(top, new)
    weights = [jnp.exp2((part - new) * factor) for part in parts]
    part_total = functools.reduce(jnp.add, weights)
    weights = jnp.concatenate([w.astype(jnp.bfloat16) for w in weights], axis=1)
    part_mixed = jnp.dot(weights[:, :keys], v, preferred_element_type=jnp.float32)
    if top is None:
        return new, part_total, part_mixed
    decay = jnp.exp2((top - new) * factor)
    return new, total * decay + part_total, mixed * decay + part_mixed


def head_tile(q_ref, state_refs, a, keys, values, factor, live=None):
    def scores(h):
        return lax.dot_general(
            q_ref[a, h],
            keys(h),
            (((1,), (1,)), ((), ())),
            preferred_element_type=jnp.float32,
        )

    heads_kv = q_ref.shape[1]
    ahead = scores(0)
    for h in range(heads_kv):
        score = ahead
        if h + 1 < heads_kv:
            ahead = scores(h + 1)
        state = (None, None, None)
        if live is None or isinstance(live, int):
            state = tuple(ref[a, h] for ref in state_refs)
        state = flash(score, values(h), state, factor, live)
        for ref, value in zip(state_refs, state):
            ref[a, h] = value


def own_kernel(group, factor, half, q_ref, own_ref, meta_ref, *refs):
    heads_kv, rows, head_dim = q_ref.shape[1:]
    state_refs = refs[:3]
    run_rows = 2 * heads_kv * RUN

    ids = own_ref[2 * run_rows :].astype(jnp.float32)
    lane = lax.broadcasted_iota(jnp.int32, ids.shape, 1)
    numbers = [jnp.max(jnp.where(lane // RUN == a, ids, 0.0)) for a in range(2)]
    row = lax.broadcasted_iota(jnp.int32, meta_ref.shape, 0)
    meta_ref[...] = jnp.where(
        row == 0, numbers[0], jnp.where(row == 1, numbers[1], 0.0)
    )

    row_at = lax.broadcasted_iota(jnp.int32, (rows, 2 * RUN), 0) // group
    key_at = lax.broadcasted_iota(jnp.int32, (rows, 2 * RUN), 1)
    for a in range(2):
        mine, other = numbers[a], numbers[1 - a]
        seen = (other < mine) & ((other >= half) == (mine >= half))
        reach = jnp.where(seen, RUN, 0)
        if a == 0:
            live = (key_at <= row_at) | ((key_at >= RUN) & (key_at < RUN + reach))
        else:
            live = (key_at < reach) | ((key_at >= RUN) & (key_at - RUN <= row_at))

        def own(g):
            starts = [g * RUN, run_rows + g * RUN]
            return jnp.concatenate([own_ref[n : n + RUN] for n in starts])

        head_tile(q_ref, state_refs, a, own, lambda h: own(heads_kv + h), factor, live)


def attend_kernel(group, factor, half, last, keep, blocks, q_ref, *refs):
    heads_kv, rows, head_dim = q_ref.shape[1:]
    run_rows = 2 * heads_kv * RUN
    block_rows = 2 * run_rows + 16
    kv_refs, refs = refs[: len(blocks)], refs[len(blocks) :]
    refs = refs[5:]
    if last:
        out_ref, refs = refs[0], refs[1:]
    meta_ref, *state_refs, buf = refs[:5]

    meta = meta_ref[...]
    counts = tuple(
        jnp.max(meta[2 + a : 3 + a]).astype(jnp.int32) for a in range(2)
    )
    seen_bits = []
    for ref, (skip, end) in zip(kv_refs, blocks):
        assert end - skip <= 8
        ids = jnp.concatenate(
            [ref[n * block_rows - 16 : n * block_rows] for n in range(skip + 1, end + 1)]
        ).astype(jnp.float32)
        row = lax.broadcasted_iota(jnp.int32, ids.shape, 0)
        lane = lax.broadcasted_iota(jnp.int32, ids.shape, 1)
        bit = jnp.left_shift(1, 2 * (row // 16) + lane // RUN)
        bit = jnp.where((row % 16 == 0) & (lane % RUN == 0), bit, 0).astype(jnp.float32)
        found = []
        for a in range(2):
            mine = meta[a : a + 1]
            low = jnp.where(mine >= half, float(half), 0.0)
            seen = (ids < mine) & (ids >= low)
            found.append(jnp.sum(jnp.where(seen, bit, 0.0)).astype(jnp.int32))
        seen_bits.append(found)

    for ref, (skip, end), bits in zip(kv_refs, blocks, seen_bits):

        def gather(n, counts):
            at = pl.multiple_of((skip + n // 2) * block_rows + n % 2 * run_rows, 16)
            fresh = []
            for a in range(2):
                flag = (bits[a] >> n) & 1
                count = counts[a]

                @pl.when(flag == 1)
                def _():
                    buf[a, count] = ref[pl.ds(at, run_rows), :]

                fresh.append(count + flag)
            return tuple(fresh)

        counts = lax.fori_loop(0, 2 * (end - skip), gather, counts)

    def some_runs(a, start, runs):
        def rows_of(g):
            found = buf[a, pl.ds(start, runs), g * RUN : (g + 1) * RUN, :]
            return found.reshape(runs * RUN, -1)

        def keys(h):
            if runs > 1:
                return rows_of(h)
            return jnp.concatenate([rows_of(h), jnp.zeros((RUN, head_dim), buf.dtype)])

        live = RUN if runs == 1 else None
        head_tile(
            q_ref, state_refs, a, keys, lambda h: rows_of(heads_kv + h), factor, live
        )

    whole = [count // TILE for count in counts]

    def step(item, carry):
        a = (item >= whole[0]).astype(jnp.int32)
        some_runs(a, (item - a * whole[0]) * TILE, TILE)
        return carry

    lax.fori_loop(0, whole[0] + whole[1], step, 0)

    def remainder(a, carry):
        count = jnp.where(a == 0, counts[0], counts[1])
        start = count // TILE * TILE
        runs = TILE // 2
        while runs >= keep:

            @pl.when(count & runs != 0)
            def _():
                some_runs(a, start, runs)

            start = start + (count & runs)
            runs //= 2
        return carry

    lax.fori_loop(0, 2, remainder, 0)

    if not last:
        row = lax.broadcasted_iota(jnp.int32, meta.shape, 0)
        for a in range(2):
            start = counts[a] // keep * keep
            rest = counts[a] - start
            if keep > 1:

                @pl.when((start > 0) & (rest > 0))
                def _():
                    for n in range(keep - 1):
                        buf[a, n] = buf[a, start + n]

            meta = jnp.where(row == 2 + a, rest.astype(jnp.float32), meta)
        meta_ref[...] = meta
        return

    made, sems = refs[5:]
    copies = []
    for a in range(2):
        for h in range(0, heads_kv, 2):
            done = []
            for g in (h, h + 1):
                total = jnp.sum(state_refs[1][a, g], axis=1, keepdims=True)
                part = state_refs[2][a, g] * (1.0 / total)
                done.append(part.reshape(RUN, group, -1))
            place = (slice(a * RUN, (a + 1) * RUN), slice(h * group, (h + 2) * group))
            made[place] = jnp.concatenate(done, axis=1).astype(out_ref.dtype)
            copy = pltpu.make_async_copy(
                made.at[place], out_ref.at[place], sems.at[len(copies)]
            )
            copy.start()
            copies.append(copy)
    for copy in copies:
        copy.wait()


def pack_kernel(k_any, v_any, positions_any, own_ref, k_ref, v_ref, positions_ref, sems):
    pairs = ((k_any, k_ref), (v_any, v_ref), (positions_any, positions_ref))
    copies = [
        pltpu.make_async_copy(source, target, sems.at[n])
        for n, (source, target) in enumerate(pairs)
    ]
    for copy in copies:
        copy.start()
    heads_kv = k_ref.shape[0] // (2 * RUN)
    rows = heads_kv * RUN
    at = lax.broadcasted_iota(jnp.int32, (rows, rows), 0)
    origin = lax.broadcasted_iota(jnp.int32, (rows, rows), 1)
    move = at % RUN * heads_kv + at // RUN == origin
    move = jnp.where(move, 1.0, 0.0).astype(k_ref.dtype)
    for n, ref in enumerate((k_ref, v_ref)):
        copies[n].wait()
        for r in range(2):
            moved = jnp.dot(
                move,
                ref[r * rows : (r + 1) * rows],
                preferred_element_type=jnp.float32,
            )
            start = (2 * r + n) * rows
            own_ref[start : start + rows] = moved.astype(own_ref.dtype)
    copies[2].wait()
    numbers = (positions_ref[...] // RUN).astype(jnp.float32)
    numbers = jnp.broadcast_to(numbers, (16, numbers.shape[1]))
    own_ref[4 * rows :] = numbers.astype(own_ref.dtype)


class Attention:
    def __init__(self, q, group, half, room):
        self.q, self.group, self.half = q, group, half
        self.factor = math.log2(math.e) / math.sqrt(q.shape[3])
        heads_kv, rows, head_dim = q.shape[1:]
        self.block_rows = 4 * heads_kv * RUN + 16
        slots = 2 * room + KEEP
        self.carried = [jax.ShapeDtypeStruct((8, 128), jnp.float32)]
        self.carried += [
            jax.ShapeDtypeStruct((2, heads_kv, rows, n), jnp.float32)
            for n in (128, 128, head_dim)
        ]
        self.carried.append(
            jax.ShapeDtypeStruct((2, slots, 2 * heads_kv * RUN, head_dim), q.dtype)
        )

    def call(self, kernel, operands, shapes, aliases, count, name, out=None):
        vmem = pl.BlockSpec(memory_space=pltpu.VMEM)
        out_specs = [vmem] * len(shapes)
        scratch = []
        if out is not None:
            shapes = [out, *shapes]
            out_specs.insert(0, pl.BlockSpec(memory_space=pl.ANY))
            scratch = [pltpu.VMEM(out.shape, out.dtype), pltpu.SemaphoreType.DMA((8,))]
        return pl.pallas_call(
            kernel,
            out_shape=shapes,
            in_specs=[vmem] * len(operands),
            out_specs=out_specs,
            scratch_shapes=scratch,
            input_output_aliases=aliases,
            compiler_params=pltpu.CompilerParams(vmem_limit_bytes=28 * 1024 * 1024),
            cost_estimate=pl.CostEstimate(
                flops=count * RUN * self.q.size * 4,
                bytes_accessed=self.q.size * count,
                transcendentals=0,
            ),
            name=name,
        )(*operands)

    def start(self, own):
        kernel = functools.partial(own_kernel, self.group, self.factor, self.half)
        return self.call(kernel, [self.q, own], self.carried, {}, 2, "attend_own")

    def add(self, state, kvs, keep=KEEP, weight=1, out=None):
        kvs = [x if isinstance(x, tuple) else (x, 0) for x in kvs]
        blocks = [(skip, x.shape[0] // self.block_rows) for x, skip in kvs]
        count = sum(end - skip for skip, end in blocks)
        operands = [self.q, *(x for x, _ in kvs), *state]
        first, ahead = 1 + len(kvs), int(out is not None)
        aliases = {first + n: ahead + n for n in range(len(state))}
        kernel = functools.partial(
            attend_kernel, self.group, self.factor, self.half, ahead, keep, blocks
        )
        results = self.call(kernel, operands, self.carried, aliases, count * weight, "attend", out)
        return results[0] if ahead else results


def per_device(queries, keys, values, positions):
    outer, inner = lax.axis_size("outer"), lax.axis_size("inner")
    tokens, heads_q, head_dim = queries.shape
    heads_kv = keys.shape[1]
    group = heads_q // heads_kv
    half = tokens // RUN * outer * inner // 2

    chips = outer // 2
    bits = inner.bit_length() - 1
    ring = [0] + list(range(1, chips, 2)) + list(range(2, chips, 2))[::-1]
    after = {ring[n]: ring[(n + 1) % chips] for n in range(chips)}

    def permute(x, to):
        pairs = []
        for z in range(chips):
            for core in range(2):
                for place in range(inner):
                    nz, ncore, nplace = to(z, core, place)
                    pairs.append(
                        (
                            (2 * z + core) * inner + place,
                            (2 * nz + ncore) * inner + nplace,
                        )
                    )
        return lax.ppermute(x, AXES, pairs)

    def along_z(x):
        return permute(x, lambda z, core, place: (after[z], core, place))

    def over_place(x, step):
        def to(z, core, place):
            return z, core, place ^ (1 << (bits - 1 - step if core else step))

        return permute(x, to)

    def other_core(x):
        return permute(x, lambda z, core, place: (z, 1 - core, place))

    def tied(x, *others):
        return lax.optimization_barrier((x, *others))[0]

    flat = jax.ShapeDtypeStruct((tokens * heads_kv, head_dim), keys.dtype)
    own = pl.pallas_call(
        pack_kernel,
        out_shape=jax.ShapeDtypeStruct(
            (2 * tokens * heads_kv + 16, head_dim), keys.dtype
        ),
        in_specs=[pl.BlockSpec(memory_space=pltpu.HBM)] * 3,
        out_specs=pl.BlockSpec(memory_space=pltpu.VMEM),
        scratch_shapes=[
            pltpu.VMEM(flat.shape, flat.dtype),
            pltpu.VMEM(flat.shape, flat.dtype),
            pltpu.VMEM((1, tokens), jnp.int32),
            pltpu.SemaphoreType.DMA((3,)),
        ],
        compiler_params=pltpu.CompilerParams(vmem_limit_bytes=60 * 1024 * 1024),
        name="pack",
    )(keys.reshape(flat.shape), values.reshape(flat.shape), positions.reshape(1, tokens))
    q = (
        queries.reshape(2, RUN, heads_kv, group, head_dim)
        .transpose(0, 2, 1, 3, 4)
        .reshape(2, heads_kv, RUN * group, head_dim)
    )

    attention = Attention(q, group, half, 2 * inner)
    state = attention.start(own)

    single = [1 << step for step in range(bits)]
    several = [m for m in range(1, inner) if m not in single]

    stages = [own]
    for n in range(1, chips):
        stages.append(along_z(stages[-1]))
    planes, waiting, late = [], None, []
    for n in range(chips):
        stage = stages[n]
        before = planes[n - 1] if n else {}
        if n:
            earlier = [before[m] for m in single]
            if n > 1:
                earlier += [planes[n - 2][m] for m in several]
            stage = tied(stage, *earlier)
        found = {0: stage}
        for step in range(bits):
            found[1 << step] = over_place(stage, step)
        wait_for = stages[n + 1 : n + 2]
        if n == 0:
            wait_for.append(state[0])
        for m in several:
            if n + 2 == chips:
                found[m] = along_z(tied(before[m], *wait_for))
            else:
                top = m.bit_length() - 1
                found[m] = over_place(tied(found[m - (1 << top)], *wait_for), top)
        planes.append(found)
        now = [found[m] for m in range(inner) if not (n + 2 >= chips and m in several)]
        if n + 2 >= chips:
            late += [found[m] for m in several]
        held = jnp.concatenate(now)
        if waiting:
            weight = 3 if n + 1 == chips else 3 if n + 2 == chips else 1
            state = attention.add(state, waiting, weight=weight)
            if n + 1 < chips:
                held = tied(held, state[0])
        waiting = [(held, int(n == 0)), other_core(held)]

    state = attention.add(state, waiting, weight=3)
    held = jnp.concatenate([tied(x, state[0]) for x in late])
    theirs = other_core(held)
    state = attention.add(state, [held], keep=1)
    out = jax.ShapeDtypeStruct(queries.shape, queries.dtype)
    return attention.add(state, [theirs], keep=1, out=out)


def solution(mesh):
    in_specs = (
        P(("outer", "inner"), None, None),
        P(("outer", "inner"), None, None),
        P(("outer", "inner"), None, None),
        P(("outer", "inner")),
    )
    out_specs = P(("outer", "inner"), None, None)
    return jax.shard_map(
        per_device, mesh=mesh, in_specs=in_specs, out_specs=out_specs, check_vma=False
    )
```

```python
import functools
import math

import jax
import jax.numpy as jnp
from jax import lax
from jax.experimental import pallas as pl
from jax.experimental.pallas import tpu as pltpu
from jax.sharding import PartitionSpec as P

RUN = 64
TILE = 8
WEIGHT = 5
KEEP = 4
AXES = ("outer", "inner")


def flash(score, v, state, factor, live=None):
    top, total, mixed = state
    keys = score.shape[1]
    if isinstance(live, int):
        lane = lax.broadcasted_iota(jnp.int32, score.shape, 1)
        keys, live = live, lane < live
    if live is not None:
        score = jnp.where(live, score, -jnp.inf)
    parts = [score[:, c : c + 128] for c in range(0, score.shape[1], 128)]
    new = jnp.max(functools.reduce(jnp.maximum, parts), axis=1, keepdims=True)
    if top is None:
        new = jnp.broadcast_to(new, parts[0].shape)
    else:
        new = jnp.maximum(top, new)
    weights = [jnp.exp2((part - new) * factor) for part in parts]
    part_total = functools.reduce(jnp.add, weights)
    weights = jnp.concatenate([w.astype(jnp.bfloat16) for w in weights], axis=1)
    part_mixed = jnp.dot(weights[:, :keys], v, preferred_element_type=jnp.float32)
    if top is None:
        return new, part_total, part_mixed
    decay = jnp.exp2((top - new) * factor)
    return new, total * decay + part_total, mixed * decay + part_mixed


def head_tile(q_ref, state_refs, a, keys, values, factor, live=None):
    def scores(h):
        return lax.dot_general(
            q_ref[a, h],
            keys(h),
            (((1,), (1,)), ((), ())),
            preferred_element_type=jnp.float32,
        )

    heads_kv = q_ref.shape[1]
    ahead = scores(0)
    for h in range(heads_kv):
        score = ahead
        if h + 1 < heads_kv:
            ahead = scores(h + 1)
        state = (None, None, None)
        if live is None or isinstance(live, int):
            state = tuple(ref[a, h] for ref in state_refs)
        state = flash(score, values(h), state, factor, live)
        for ref, value in zip(state_refs, state):
            ref[a, h] = value


def own_kernel(group, factor, half, q_ref, own_ref, meta_ref, *refs):
    heads_kv, rows, head_dim = q_ref.shape[1:]
    state_refs = refs[:3]
    run_rows = 2 * heads_kv * RUN

    ids = own_ref[2 * run_rows :].astype(jnp.float32)
    lane = lax.broadcasted_iota(jnp.int32, ids.shape, 1)
    numbers = [jnp.max(jnp.where(lane // RUN == a, ids, 0.0)) for a in range(2)]
    row = lax.broadcasted_iota(jnp.int32, meta_ref.shape, 0)
    meta_ref[...] = jnp.where(
        row == 0, numbers[0], jnp.where(row == 1, numbers[1], 0.0)
    )

    row_at = lax.broadcasted_iota(jnp.int32, (rows, 2 * RUN), 0) // group
    key_at = lax.broadcasted_iota(jnp.int32, (rows, 2 * RUN), 1)
    for a in range(2):
        mine, other = numbers[a], numbers[1 - a]
        seen = (other < mine) & ((other >= half) == (mine >= half))
        reach = jnp.where(seen, RUN, 0)
        if a == 0:
            live = (key_at <= row_at) | ((key_at >= RUN) & (key_at < RUN + reach))
        else:
            live = (key_at < reach) | ((key_at >= RUN) & (key_at - RUN <= row_at))

        def own(g):
            starts = [g * RUN, run_rows + g * RUN]
            return jnp.concatenate([own_ref[n : n + RUN] for n in starts])

        head_tile(q_ref, state_refs, a, own, lambda h: own(heads_kv + h), factor, live)


def attend_kernel(group, factor, half, last, keep, blocks, q_ref, *refs):
    heads_kv, rows, head_dim = q_ref.shape[1:]
    run_rows = 2 * heads_kv * RUN
    block_rows = 2 * run_rows + 16
    kv_refs, refs = refs[: len(blocks)], refs[len(blocks) :]
    refs = refs[5:]
    if last:
        out_ref, refs = refs[0], refs[1:]
    meta_ref, *state_refs, buf = refs[:5]

    meta = meta_ref[...]
    counts = tuple(
        jnp.max(meta[2 + a : 3 + a]).astype(jnp.int32) for a in range(2)
    )
    seen_bits = []
    for ref, (skip, end) in zip(kv_refs, blocks):
        assert end - skip <= 8
        ids = jnp.concatenate(
            [ref[n * block_rows - 16 : n * block_rows] for n in range(skip + 1, end + 1)]
        ).astype(jnp.float32)
        row = lax.broadcasted_iota(jnp.int32, ids.shape, 0)
        lane = lax.broadcasted_iota(jnp.int32, ids.shape, 1)
        bit = jnp.left_shift(1, 2 * (row // 16) + lane // RUN)
        bit = jnp.where((row % 16 == 0) & (lane % RUN == 0), bit, 0).astype(jnp.float32)
        found = []
        for a in range(2):
            mine = meta[a : a + 1]
            low = jnp.where(mine >= half, float(half), 0.0)
            seen = (ids < mine) & (ids >= low)
            found.append(jnp.sum(jnp.where(seen, bit, 0.0)).astype(jnp.int32))
        seen_bits.append(found)

    for ref, (skip, end), bits in zip(kv_refs, blocks, seen_bits):

        def gather(n, counts):
            at = pl.multiple_of((skip + n // 2) * block_rows + n % 2 * run_rows, 16)
            fresh = []
            for a in range(2):
                flag = (bits[a] >> n) & 1
                count = counts[a]

                @pl.when(flag == 1)
                def _():
                    buf[a, count] = ref[pl.ds(at, run_rows), :]

                fresh.append(count + flag)
            return tuple(fresh)

        counts = lax.fori_loop(0, 2 * (end - skip), gather, counts)

    def some_runs(a, start, runs):
        def rows_of(g):
            found = buf[a, pl.ds(start, runs), g * RUN : (g + 1) * RUN, :]
            return found.reshape(runs * RUN, -1)

        def keys(h):
            if runs > 1:
                return rows_of(h)
            return jnp.concatenate([rows_of(h), jnp.zeros((RUN, head_dim), buf.dtype)])

        live = RUN if runs == 1 else None
        head_tile(
            q_ref, state_refs, a, keys, lambda h: rows_of(heads_kv + h), factor, live
        )

    whole = [count // TILE for count in counts]

    def step(item, carry):
        a = (item >= whole[0]).astype(jnp.int32)
        some_runs(a, (item - a * whole[0]) * TILE, TILE)
        return carry

    lax.fori_loop(0, whole[0] + whole[1], step, 0)

    def remainder(a, carry):
        count = jnp.where(a == 0, counts[0], counts[1])
        start = count // TILE * TILE
        runs = TILE // 2
        while runs >= keep:

            @pl.when(count & runs != 0)
            def _():
                some_runs(a, start, runs)

            start = start + (count & runs)
            runs //= 2
        return carry

    lax.fori_loop(0, 2, remainder, 0)

    if not last:
        row = lax.broadcasted_iota(jnp.int32, meta.shape, 0)
        for a in range(2):
            start = counts[a] // keep * keep
            rest = counts[a] - start
            if keep > 1:

                @pl.when((start > 0) & (rest > 0))
                def _():
                    for n in range(keep - 1):
                        buf[a, n] = buf[a, start + n]

            meta = jnp.where(row == 2 + a, rest.astype(jnp.float32), meta)
        meta_ref[...] = meta
        return

    made, sems = refs[5:]
    copies = []
    for a in range(2):
        for h in range(0, heads_kv, 2):
            done = []
            for g in (h, h + 1):
                total = jnp.sum(state_refs[1][a, g], axis=1, keepdims=True)
                part = state_refs[2][a, g] * (1.0 / total)
                done.append(part.reshape(RUN, group, -1))
            place = (slice(a * RUN, (a + 1) * RUN), slice(h * group, (h + 2) * group))
            made[place] = jnp.concatenate(done, axis=1).astype(out_ref.dtype)
            copy = pltpu.make_async_copy(
                made.at[place], out_ref.at[place], sems.at[len(copies)]
            )
            copy.start()
            copies.append(copy)
    for copy in copies:
        copy.wait()


def pack_kernel(k_any, v_any, positions_any, own_ref, k_ref, v_ref, positions_ref, sems):
    pairs = ((k_any, k_ref), (v_any, v_ref), (positions_any, positions_ref))
    copies = [
        pltpu.make_async_copy(source, target, sems.at[n])
        for n, (source, target) in enumerate(pairs)
    ]
    for copy in copies:
        copy.start()
    heads_kv = k_ref.shape[0] // (2 * RUN)
    rows = heads_kv * RUN
    at = lax.broadcasted_iota(jnp.int32, (rows, rows), 0)
    origin = lax.broadcasted_iota(jnp.int32, (rows, rows), 1)
    move = at % RUN * heads_kv + at // RUN == origin
    move = jnp.where(move, 1.0, 0.0).astype(k_ref.dtype)
    for n, ref in enumerate((k_ref, v_ref)):
        copies[n].wait()
        for r in range(2):
            moved = jnp.dot(
                move,
                ref[r * rows : (r + 1) * rows],
                preferred_element_type=jnp.float32,
            )
            start = (2 * r + n) * rows
            own_ref[start : start + rows] = moved.astype(own_ref.dtype)
    copies[2].wait()
    numbers = (positions_ref[...] // RUN).astype(jnp.float32)
    numbers = jnp.broadcast_to(numbers, (16, numbers.shape[1]))
    own_ref[4 * rows :] = numbers.astype(own_ref.dtype)


class Attention:
    def __init__(self, q, group, half, room):
        self.q, self.group, self.half = q, group, half
        self.factor = math.log2(math.e) / math.sqrt(q.shape[3])
        heads_kv, rows, head_dim = q.shape[1:]
        self.block_rows = 4 * heads_kv * RUN + 16
        slots = 2 * room + KEEP
        self.carried = [jax.ShapeDtypeStruct((8, 128), jnp.float32)]
        self.carried += [
            jax.ShapeDtypeStruct((2, heads_kv, rows, n), jnp.float32)
            for n in (128, 128, head_dim)
        ]
        self.carried.append(
            jax.ShapeDtypeStruct((2, slots, 2 * heads_kv * RUN, head_dim), q.dtype)
        )

    def call(self, kernel, operands, shapes, aliases, count, name, out=None):
        vmem = pl.BlockSpec(memory_space=pltpu.VMEM)
        out_specs = [vmem] * len(shapes)
        scratch = []
        if out is not None:
            shapes = [out, *shapes]
            out_specs.insert(0, pl.BlockSpec(memory_space=pl.ANY))
            scratch = [pltpu.VMEM(out.shape, out.dtype), pltpu.SemaphoreType.DMA((8,))]
        return pl.pallas_call(
            kernel,
            out_shape=shapes,
            in_specs=[vmem] * len(operands),
            out_specs=out_specs,
            scratch_shapes=scratch,
            input_output_aliases=aliases,
            compiler_params=pltpu.CompilerParams(vmem_limit_bytes=28 * 1024 * 1024),
            cost_estimate=pl.CostEstimate(
                flops=count * RUN * self.q.size * 4,
                bytes_accessed=self.q.size * count,
                transcendentals=0,
            ),
            name=name,
        )(*operands)

    def start(self, own):
        kernel = functools.partial(own_kernel, self.group, self.factor, self.half)
        return self.call(kernel, [self.q, own], self.carried, {}, 2, "attend_own")

    def add(self, state, kvs, keep=KEEP, weight=WEIGHT, out=None):
        kvs = [x if isinstance(x, tuple) else (x, 0) for x in kvs]
        blocks = [(skip, x.shape[0] // self.block_rows) for x, skip in kvs]
        count = sum(end - skip for skip, end in blocks)
        operands = [self.q, *(x for x, _ in kvs), *state]
        first, ahead = 1 + len(kvs), int(out is not None)
        aliases = {first + n: ahead + n for n in range(len(state))}
        kernel = functools.partial(
            attend_kernel, self.group, self.factor, self.half, ahead, keep, blocks
        )
        results = self.call(kernel, operands, self.carried, aliases, count * weight, "attend", out)
        return results[0] if ahead else results


def per_device(queries, keys, values, positions):
    outer, inner = lax.axis_size("outer"), lax.axis_size("inner")
    tokens, heads_q, head_dim = queries.shape
    heads_kv = keys.shape[1]
    group = heads_q // heads_kv
    half = tokens // RUN * outer * inner // 2

    chips = outer // 2
    bits = inner.bit_length() - 1
    ring = [0] + list(range(1, chips, 2)) + list(range(2, chips, 2))[::-1]
    after = {ring[n]: ring[(n + 1) % chips] for n in range(chips)}

    def permute(x, to):
        pairs = []
        for z in range(chips):
            for core in range(2):
                for place in range(inner):
                    nz, ncore, nplace = to(z, core, place)
                    pairs.append(
                        (
                            (2 * z + core) * inner + place,
                            (2 * nz + ncore) * inner + nplace,
                        )
                    )
        return lax.ppermute(x, AXES, pairs)

    def along_z(x):
        return permute(x, lambda z, core, place: (after[z], core, place))

    def over_place(x, step):
        def to(z, core, place):
            return z, core, place ^ (1 << (bits - 1 - step if core else step))

        return permute(x, to)

    def other_core(x):
        return permute(x, lambda z, core, place: (z, 1 - core, place))

    def tied(x, *others):
        return lax.optimization_barrier((x, *others))[0]

    flat = jax.ShapeDtypeStruct((tokens * heads_kv, head_dim), keys.dtype)
    own = pl.pallas_call(
        pack_kernel,
        out_shape=jax.ShapeDtypeStruct(
            (2 * tokens * heads_kv + 16, head_dim), keys.dtype
        ),
        in_specs=[pl.BlockSpec(memory_space=pltpu.HBM)] * 3,
        out_specs=pl.BlockSpec(memory_space=pltpu.VMEM),
        scratch_shapes=[
            pltpu.VMEM(flat.shape, flat.dtype),
            pltpu.VMEM(flat.shape, flat.dtype),
            pltpu.VMEM((1, tokens), jnp.int32),
            pltpu.SemaphoreType.DMA((3,)),
        ],
        compiler_params=pltpu.CompilerParams(vmem_limit_bytes=60 * 1024 * 1024),
        name="pack",
    )(keys.reshape(flat.shape), values.reshape(flat.shape), positions.reshape(1, tokens))
    q = (
        queries.reshape(2, RUN, heads_kv, group, head_dim)
        .transpose(0, 2, 1, 3, 4)
        .reshape(2, heads_kv, RUN * group, head_dim)
    )

    attention = Attention(q, group, half, 2 * inner)
    state = attention.start(own)

    single = [1 << step for step in range(bits)]
    several = [m for m in range(1, inner) if m not in single]

    stages = [own]
    for n in range(1, chips):
        stages.append(along_z(stages[-1]))
    planes, held, waiting, late = [], None, None, []
    for n in range(chips):
        stage = stages[n]
        before = planes[n - 1] if n else {}
        if n:
            earlier = [before[m] for m in single]
            if n > 1:
                earlier += [planes[n - 2][m] for m in several]
            stage = tied(stage, *earlier)
        found = {0: stage}
        for step in range(bits):
            found[1 << step] = over_place(stage, step)
        if n:
            if n > 1:
                state = attention.add(state, waiting)
            first = [state[0]] if n > 1 else []
            first += late if n + 1 == chips else [found[m] for m in single]
            first += stages[n + 1 : n + 2]
            waiting = [(held, int(n == 1)), other_core(tied(held, *first))]
        wait_for = stages[n + 1 : n + 2]
        if n == 0:
            wait_for.append(state[0])
        for m in several:
            if n + 2 == chips:
                found[m] = along_z(tied(before[m], *wait_for))
            else:
                top = m.bit_length() - 1
                found[m] = over_place(tied(found[m - (1 << top)], *wait_for), top)
        planes.append(found)
        if n + 2 >= chips:
            late += [found[m] for m in several]
        held = jnp.concatenate(
            [found[m] for m in range(inner) if n + 2 < chips or m not in several]
        )

    state = attention.add(state, waiting)
    state = attention.add(state, [held, other_core(held)])
    held = jnp.concatenate([tied(x, state[0]) for x in late])
    theirs = other_core(held)
    state = attention.add(state, [held], keep=1)
    out = jax.ShapeDtypeStruct(queries.shape, queries.dtype)
    return attention.add(state, [theirs], keep=1, out=out)


def solution(mesh):
    in_specs = (
        P(("outer", "inner"), None, None),
        P(("outer", "inner"), None, None),
        P(("outer", "inner"), None, None),
        P(("outer", "inner")),
    )
    out_specs = P(("outer", "inner"), None, None)
    return jax.shard_map(
        per_device, mesh=mesh, in_specs=in_specs, out_specs=out_specs, check_vma=False
    )
```

```python
import functools
import math

import jax
import jax.numpy as jnp
from jax import lax
from jax.experimental import pallas as pl
from jax.experimental.pallas import tpu as pltpu
from jax.sharding import PartitionSpec as P

RUN = 64
TILE = 8
KEEP = 4
AXES = ("outer", "inner")


def flash(score, v, state, factor, live=None):
    top, total, mixed = state
    keys = score.shape[1]
    if isinstance(live, int):
        lane = lax.broadcasted_iota(jnp.int32, score.shape, 1)
        keys, live = live, lane < live
    if live is not None:
        score = jnp.where(live, score, -jnp.inf)
    parts = [score[:, c : c + 128] for c in range(0, score.shape[1], 128)]
    new = jnp.max(functools.reduce(jnp.maximum, parts), axis=1, keepdims=True)
    if top is None:
        new = jnp.broadcast_to(new, parts[0].shape)
    else:
        new = jnp.maximum(top, new)
    weights = [jnp.exp2((part - new) * factor) for part in parts]
    part_total = functools.reduce(jnp.add, weights)
    weights = jnp.concatenate([w.astype(jnp.bfloat16) for w in weights], axis=1)
    part_mixed = jnp.dot(weights[:, :keys], v, preferred_element_type=jnp.float32)
    if top is None:
        return new, part_total, part_mixed
    decay = jnp.exp2((top - new) * factor)
    return new, total * decay + part_total, mixed * decay + part_mixed


def head_tile(q_ref, state_refs, a, keys, values, factor, live=None):
    def scores(h):
        return lax.dot_general(
            q_ref[a, h],
            keys(h),
            (((1,), (1,)), ((), ())),
            preferred_element_type=jnp.float32,
        )

    heads_kv = q_ref.shape[1]
    ahead = scores(0)
    for h in range(heads_kv):
        score = ahead
        if h + 1 < heads_kv:
            ahead = scores(h + 1)
        state = (None, None, None)
        if live is None or isinstance(live, int):
            state = tuple(ref[a, h] for ref in state_refs)
        state = flash(score, values(h), state, factor, live)
        for ref, value in zip(state_refs, state):
            ref[a, h] = value


def own_kernel(group, factor, half, q_ref, own_ref, meta_ref, *refs):
    heads_kv, rows, head_dim = q_ref.shape[1:]
    state_refs = refs[:3]
    run_rows = 2 * heads_kv * RUN

    ids = own_ref[2 * run_rows :].astype(jnp.float32)
    lane = lax.broadcasted_iota(jnp.int32, ids.shape, 1)
    numbers = [jnp.max(jnp.where(lane // RUN == a, ids, 0.0)) for a in range(2)]
    row = lax.broadcasted_iota(jnp.int32, meta_ref.shape, 0)
    meta_ref[...] = jnp.where(
        row == 0, numbers[0], jnp.where(row == 1, numbers[1], 0.0)
    )

    row_at = lax.broadcasted_iota(jnp.int32, (rows, 2 * RUN), 0) // group
    key_at = lax.broadcasted_iota(jnp.int32, (rows, 2 * RUN), 1)
    for a in range(2):
        mine, other = numbers[a], numbers[1 - a]
        seen = (other < mine) & ((other >= half) == (mine >= half))
        reach = jnp.where(seen, RUN, 0)
        if a == 0:
            live = (key_at <= row_at) | ((key_at >= RUN) & (key_at < RUN + reach))
        else:
            live = (key_at < reach) | ((key_at >= RUN) & (key_at - RUN <= row_at))

        def own(g):
            starts = [g * RUN, run_rows + g * RUN]
            return jnp.concatenate([own_ref[n : n + RUN] for n in starts])

        head_tile(q_ref, state_refs, a, own, lambda h: own(heads_kv + h), factor, live)


def attend_kernel(group, factor, half, last, keep, blocks, q_ref, *refs):
    heads_kv, rows, head_dim = q_ref.shape[1:]
    run_rows = 2 * heads_kv * RUN
    block_rows = 2 * run_rows + 16
    kv_refs, refs = refs[: len(blocks)], refs[len(blocks) :]
    refs = refs[5:]
    if last:
        out_ref, refs = refs[0], refs[1:]
    meta_ref, *state_refs, buf = refs[:5]

    meta = meta_ref[...]
    counts = tuple(
        jnp.max(meta[2 + a : 3 + a]).astype(jnp.int32) for a in range(2)
    )
    seen_bits = []
    for ref, (skip, end) in zip(kv_refs, blocks):
        assert end - skip <= 8
        ids = jnp.concatenate(
            [ref[n * block_rows - 16 : n * block_rows] for n in range(skip + 1, end + 1)]
        ).astype(jnp.float32)
        row = lax.broadcasted_iota(jnp.int32, ids.shape, 0)
        lane = lax.broadcasted_iota(jnp.int32, ids.shape, 1)
        bit = jnp.left_shift(1, 2 * (row // 16) + lane // RUN)
        bit = jnp.where((row % 16 == 0) & (lane % RUN == 0), bit, 0).astype(jnp.float32)
        found = []
        for a in range(2):
            mine = meta[a : a + 1]
            low = jnp.where(mine >= half, float(half), 0.0)
            seen = (ids < mine) & (ids >= low)
            found.append(jnp.sum(jnp.where(seen, bit, 0.0)).astype(jnp.int32))
        seen_bits.append(found)

    for ref, (skip, end), bits in zip(kv_refs, blocks, seen_bits):

        def gather(n, counts):
            at = pl.multiple_of((skip + n // 2) * block_rows + n % 2 * run_rows, 16)
            fresh = []
            for a in range(2):
                flag = (bits[a] >> n) & 1
                count = counts[a]

                @pl.when(flag == 1)
                def _():
                    buf[a, count] = ref[pl.ds(at, run_rows), :]

                fresh.append(count + flag)
            return tuple(fresh)

        counts = lax.fori_loop(0, 2 * (end - skip), gather, counts)

    def some_runs(a, start, runs):
        def rows_of(g):
            found = buf[a, pl.ds(start, runs), g * RUN : (g + 1) * RUN, :]
            return found.reshape(runs * RUN, -1)

        def keys(h):
            if runs > 1:
                return rows_of(h)
            return jnp.concatenate([rows_of(h), jnp.zeros((RUN, head_dim), buf.dtype)])

        live = RUN if runs == 1 else None
        head_tile(
            q_ref, state_refs, a, keys, lambda h: rows_of(heads_kv + h), factor, live
        )

    whole = [count // TILE for count in counts]

    def step(item, carry):
        a = (item >= whole[0]).astype(jnp.int32)
        some_runs(a, (item - a * whole[0]) * TILE, TILE)
        return carry

    lax.fori_loop(0, whole[0] + whole[1], step, 0)

    def remainder(a, carry):
        count = jnp.where(a == 0, counts[0], counts[1])
        start = count // TILE * TILE
        runs = TILE // 2
        while runs >= keep:

            @pl.when(count & runs != 0)
            def _():
                some_runs(a, start, runs)

            start = start + (count & runs)
            runs //= 2
        return carry

    lax.fori_loop(0, 2, remainder, 0)

    if not last:
        row = lax.broadcasted_iota(jnp.int32, meta.shape, 0)
        for a in range(2):
            start = counts[a] // keep * keep
            rest = counts[a] - start
            if keep > 1:

                @pl.when((start > 0) & (rest > 0))
                def _():
                    for n in range(keep - 1):
                        buf[a, n] = buf[a, start + n]

            meta = jnp.where(row == 2 + a, rest.astype(jnp.float32), meta)
        meta_ref[...] = meta
        return

    made, sems = refs[5:]
    copies = []
    for a in range(2):
        for h in range(0, heads_kv, 2):
            done = []
            for g in (h, h + 1):
                total = jnp.sum(state_refs[1][a, g], axis=1, keepdims=True)
                part = state_refs[2][a, g] * (1.0 / total)
                done.append(part.reshape(RUN, group, -1))
            place = (slice(a * RUN, (a + 1) * RUN), slice(h * group, (h + 2) * group))
            made[place] = jnp.concatenate(done, axis=1).astype(out_ref.dtype)
            copy = pltpu.make_async_copy(
                made.at[place], out_ref.at[place], sems.at[len(copies)]
            )
            copy.start()
            copies.append(copy)
    for copy in copies:
        copy.wait()


def pack_kernel(k_any, v_any, positions_any, own_ref, k_ref, v_ref, positions_ref, sems):
    pairs = ((k_any, k_ref), (v_any, v_ref), (positions_any, positions_ref))
    copies = [
        pltpu.make_async_copy(source, target, sems.at[n])
        for n, (source, target) in enumerate(pairs)
    ]
    for copy in copies:
        copy.start()
    heads_kv = k_ref.shape[0] // (2 * RUN)
    rows = heads_kv * RUN
    at = lax.broadcasted_iota(jnp.int32, (rows, rows), 0)
    origin = lax.broadcasted_iota(jnp.int32, (rows, rows), 1)
    move = at % RUN * heads_kv + at // RUN == origin
    move = jnp.where(move, 1.0, 0.0).astype(k_ref.dtype)
    for n, ref in enumerate((k_ref, v_ref)):
        copies[n].wait()
        for r in range(2):
            moved = jnp.dot(
                move,
                ref[r * rows : (r + 1) * rows],
                preferred_element_type=jnp.float32,
            )
            start = (2 * r + n) * rows
            own_ref[start : start + rows] = moved.astype(own_ref.dtype)
    copies[2].wait()
    numbers = (positions_ref[...] // RUN).astype(jnp.float32)
    numbers = jnp.broadcast_to(numbers, (16, numbers.shape[1]))
    own_ref[4 * rows :] = numbers.astype(own_ref.dtype)


class Attention:
    def __init__(self, q, group, half, room):
        self.q, self.group, self.half = q, group, half
        self.factor = math.log2(math.e) / math.sqrt(q.shape[3])
        heads_kv, rows, head_dim = q.shape[1:]
        self.block_rows = 4 * heads_kv * RUN + 16
        slots = 2 * room + KEEP
        self.carried = [jax.ShapeDtypeStruct((8, 128), jnp.float32)]
        self.carried += [
            jax.ShapeDtypeStruct((2, heads_kv, rows, n), jnp.float32)
            for n in (128, 128, head_dim)
        ]
        self.carried.append(
            jax.ShapeDtypeStruct((2, slots, 2 * heads_kv * RUN, head_dim), q.dtype)
        )

    def call(self, kernel, operands, shapes, aliases, count, name, out=None):
        vmem = pl.BlockSpec(memory_space=pltpu.VMEM)
        out_specs = [vmem] * len(shapes)
        scratch = []
        if out is not None:
            shapes = [out, *shapes]
            out_specs.insert(0, pl.BlockSpec(memory_space=pl.ANY))
            scratch = [pltpu.VMEM(out.shape, out.dtype), pltpu.SemaphoreType.DMA((8,))]
        return pl.pallas_call(
            kernel,
            out_shape=shapes,
            in_specs=[vmem] * len(operands),
            out_specs=out_specs,
            scratch_shapes=scratch,
            input_output_aliases=aliases,
            compiler_params=pltpu.CompilerParams(vmem_limit_bytes=28 * 1024 * 1024),
            cost_estimate=pl.CostEstimate(
                flops=1 * count * RUN * self.q.size * 4,
                bytes_accessed=self.q.size * 8 * 1,
                transcendentals=0,
            ),
            name=name,
        )(*operands)

    def start(self, own):
        kernel = functools.partial(own_kernel, self.group, self.factor, self.half)
        return self.call(kernel, [self.q, own], self.carried, {}, 2, "attend_own")

    def add(self, state, kvs, keep=KEEP, out=None):
        kvs = [x if isinstance(x, tuple) else (x, 0) for x in kvs]
        blocks = [(skip, x.shape[0] // self.block_rows) for x, skip in kvs]
        count = sum(end - skip for skip, end in blocks)
        operands = [self.q, *(x for x, _ in kvs), *state]
        first, ahead = 1 + len(kvs), int(out is not None)
        aliases = {first + n: ahead + n for n in range(len(state))}
        kernel = functools.partial(
            attend_kernel, self.group, self.factor, self.half, ahead, keep, blocks
        )
        results = self.call(kernel, operands, self.carried, aliases, count, "attend", out)
        return results[0] if ahead else results


def per_device(queries, keys, values, positions):
    outer, inner = lax.axis_size("outer"), lax.axis_size("inner")
    tokens, heads_q, head_dim = queries.shape
    heads_kv = keys.shape[1]
    group = heads_q // heads_kv
    half = tokens // RUN * outer * inner // 2

    chips = outer // 2
    bits = inner.bit_length() - 1
    ring = [0] + list(range(1, chips, 2)) + list(range(2, chips, 2))[::-1]
    after = {ring[n]: ring[(n + 1) % chips] for n in range(chips)}

    def permute(x, to):
        pairs = []
        for z in range(chips):
            for core in range(2):
                for place in range(inner):
                    nz, ncore, nplace = to(z, core, place)
                    pairs.append(
                        (
                            (2 * z + core) * inner + place,
                            (2 * nz + ncore) * inner + nplace,
                        )
                    )
        return lax.ppermute(x, AXES, pairs)

    def along_z(x):
        return permute(x, lambda z, core, place: (after[z], core, place))

    def over_place(x, step):
        def to(z, core, place):
            return z, core, place ^ (1 << (bits - 1 - step if core else step))

        return permute(x, to)

    def other_core(x):
        return permute(x, lambda z, core, place: (z, 1 - core, place))

    def tied(x, *others):
        return lax.optimization_barrier((x, *others))[0]

    flat = jax.ShapeDtypeStruct((tokens * heads_kv, head_dim), keys.dtype)
    own = pl.pallas_call(
        pack_kernel,
        out_shape=jax.ShapeDtypeStruct(
            (2 * tokens * heads_kv + 16, head_dim), keys.dtype
        ),
        in_specs=[pl.BlockSpec(memory_space=pltpu.HBM)] * 3,
        out_specs=pl.BlockSpec(memory_space=pltpu.VMEM),
        scratch_shapes=[
            pltpu.VMEM(flat.shape, flat.dtype),
            pltpu.VMEM(flat.shape, flat.dtype),
            pltpu.VMEM((1, tokens), jnp.int32),
            pltpu.SemaphoreType.DMA((3,)),
        ],
        compiler_params=pltpu.CompilerParams(vmem_limit_bytes=60 * 1024 * 1024),
        name="pack",
    )(keys.reshape(flat.shape), values.reshape(flat.shape), positions.reshape(1, tokens))
    q = (
        queries.reshape(2, RUN, heads_kv, group, head_dim)
        .transpose(0, 2, 1, 3, 4)
        .reshape(2, heads_kv, RUN * group, head_dim)
    )

    attention = Attention(q, group, half, 2 * inner)
    state = attention.start(own)

    stage, waiting = own, None
    for n in range(chips - 1):
        following = along_z(stage)
        found = [stage]
        if n == 0:
            ones = [over_place(stage, step) for step in range(bits)]
            for step in range(bits):
                there = [ones[step]]
                for x in found[1:]:
                    there.append(over_place(x, step))
                if step:
                    there[1] = over_place(tied(found[1], following, state[0]), step)
                found += there
            held = jnp.concatenate(found)
        else:
            held = tied(stage, *ones, state[0]) if n == 1 else stage
            for step in range(bits):
                held = jnp.concatenate([held, over_place(held, step)])
        if waiting:
            state = attention.add(state, waiting)
            held = tied(held, state[0])
        waiting = [(held, int(n == 0)), other_core(held)]
        stage = following

    found = [stage]
    for step in range(bits):
        found += [over_place(x, step) for x in found]
    *most, final = found
    most = jnp.concatenate(most)
    theirs = other_core(most)
    state = attention.add(state, waiting)
    state = attention.add(state, [most, theirs])
    final = tied(final, state[0])
    theirs = other_core(final)
    state = attention.add(state, [final], keep=1)
    out = jax.ShapeDtypeStruct(queries.shape, queries.dtype)
    return attention.add(state, [theirs], keep=1, out=out)


def solution(mesh):
    in_specs = (
        P(("outer", "inner"), None, None),
        P(("outer", "inner"), None, None),
        P(("outer", "inner"), None, None),
        P(("outer", "inner")),
    )
    out_specs = P(("outer", "inner"), None, None)
    return jax.shard_map(
        per_device, mesh=mesh, in_specs=in_specs, out_specs=out_specs, check_vma=False
    )
```

```python
import functools
import math

import jax
import jax.numpy as jnp
from jax import lax
from jax.experimental import pallas as pl
from jax.experimental.pallas import tpu as pltpu
from jax.sharding import PartitionSpec as P

RUN = 64
TILE = 8
KEEP = 4
AXES = ("outer", "inner")


def flash(score, v, state, factor, live=None):
    top, total, mixed = state
    keys = score.shape[1]
    if isinstance(live, int):
        lane = lax.broadcasted_iota(jnp.int32, score.shape, 1)
        keys, live = live, lane < live
    if live is not None:
        score = jnp.where(live, score, -jnp.inf)
    parts = [score[:, c : c + 128] for c in range(0, score.shape[1], 128)]
    new = jnp.max(functools.reduce(jnp.maximum, parts), axis=1, keepdims=True)
    if top is None:
        new = jnp.broadcast_to(new, parts[0].shape)
    else:
        new = jnp.maximum(top, new)
    weights = [jnp.exp2((part - new) * factor) for part in parts]
    part_total = functools.reduce(jnp.add, weights)
    weights = jnp.concatenate([w.astype(jnp.bfloat16) for w in weights], axis=1)
    part_mixed = jnp.dot(weights[:, :keys], v, preferred_element_type=jnp.float32)
    if top is None:
        return new, part_total, part_mixed
    decay = jnp.exp2((top - new) * factor)
    return new, total * decay + part_total, mixed * decay + part_mixed


def head_tile(q_ref, state_refs, a, keys, values, factor, live=None):
    def scores(h):
        return lax.dot_general(
            q_ref[a, h],
            keys(h),
            (((1,), (1,)), ((), ())),
            preferred_element_type=jnp.float32,
        )

    heads_kv = q_ref.shape[1]
    ahead = scores(0)
    for h in range(heads_kv):
        score = ahead
        if h + 1 < heads_kv:
            ahead = scores(h + 1)
        state = (None, None, None)
        if live is None or isinstance(live, int):
            state = tuple(ref[a, h] for ref in state_refs)
        state = flash(score, values(h), state, factor, live)
        for ref, value in zip(state_refs, state):
            ref[a, h] = value


def own_kernel(group, factor, half, q_ref, own_ref, meta_ref, *refs):
    heads_kv, rows, head_dim = q_ref.shape[1:]
    state_refs = refs[:3]
    run_rows = 2 * heads_kv * RUN

    ids = own_ref[2 * run_rows :].astype(jnp.float32)
    lane = lax.broadcasted_iota(jnp.int32, ids.shape, 1)
    numbers = [jnp.max(jnp.where(lane // RUN == a, ids, 0.0)) for a in range(2)]
    row = lax.broadcasted_iota(jnp.int32, meta_ref.shape, 0)
    meta_ref[...] = jnp.where(
        row == 0, numbers[0], jnp.where(row == 1, numbers[1], 0.0)
    )

    row_at = lax.broadcasted_iota(jnp.int32, (rows, 2 * RUN), 0) // group
    key_at = lax.broadcasted_iota(jnp.int32, (rows, 2 * RUN), 1)
    for a in range(2):
        mine, other = numbers[a], numbers[1 - a]
        seen = (other < mine) & ((other >= half) == (mine >= half))
        reach = jnp.where(seen, RUN, 0)
        if a == 0:
            live = (key_at <= row_at) | ((key_at >= RUN) & (key_at < RUN + reach))
        else:
            live = (key_at < reach) | ((key_at >= RUN) & (key_at - RUN <= row_at))

        def own(g):
            starts = [g * RUN, run_rows + g * RUN]
            return jnp.concatenate([own_ref[n : n + RUN] for n in starts])

        head_tile(q_ref, state_refs, a, own, lambda h: own(heads_kv + h), factor, live)


def attend_kernel(group, factor, half, last, keep, blocks, q_ref, *refs):
    heads_kv, rows, head_dim = q_ref.shape[1:]
    run_rows = 2 * heads_kv * RUN
    block_rows = 2 * run_rows + 16
    kv_refs, refs = refs[: len(blocks)], refs[len(blocks) :]
    refs = refs[5:]
    if last:
        out_ref, refs = refs[0], refs[1:]
    meta_ref, *state_refs, buf = refs[:5]

    meta = meta_ref[...]
    counts = tuple(
        jnp.max(meta[2 + a : 3 + a]).astype(jnp.int32) for a in range(2)
    )
    seen_bits = []
    for ref, (skip, end) in zip(kv_refs, blocks):
        assert end - skip <= 8
        ids = jnp.concatenate(
            [ref[n * block_rows - 16 : n * block_rows] for n in range(skip + 1, end + 1)]
        ).astype(jnp.float32)
        row = lax.broadcasted_iota(jnp.int32, ids.shape, 0)
        lane = lax.broadcasted_iota(jnp.int32, ids.shape, 1)
        bit = jnp.left_shift(1, 2 * (row // 16) + lane // RUN)
        bit = jnp.where((row % 16 == 0) & (lane % RUN == 0), bit, 0).astype(jnp.float32)
        found = []
        for a in range(2):
            mine = meta[a : a + 1]
            low = jnp.where(mine >= half, float(half), 0.0)
            seen = (ids < mine) & (ids >= low)
            found.append(jnp.sum(jnp.where(seen, bit, 0.0)).astype(jnp.int32))
        seen_bits.append(found)

    for ref, (skip, end), bits in zip(kv_refs, blocks, seen_bits):

        def gather(n, counts):
            at = pl.multiple_of((skip + n // 2) * block_rows + n % 2 * run_rows, 16)
            fresh = []
            for a in range(2):
                flag = (bits[a] >> n) & 1
                count = counts[a]

                @pl.when(flag == 1)
                def _():
                    buf[a, count] = ref[pl.ds(at, run_rows), :]

                fresh.append(count + flag)
            return tuple(fresh)

        counts = lax.fori_loop(0, 2 * (end - skip), gather, counts)

    def some_runs(a, start, runs):
        def rows_of(g):
            found = buf[a, pl.ds(start, runs), g * RUN : (g + 1) * RUN, :]
            return found.reshape(runs * RUN, -1)

        def keys(h):
            if runs > 1:
                return rows_of(h)
            return jnp.concatenate([rows_of(h), jnp.zeros((RUN, head_dim), buf.dtype)])

        live = RUN if runs == 1 else None
        head_tile(
            q_ref, state_refs, a, keys, lambda h: rows_of(heads_kv + h), factor, live
        )

    whole = [count // TILE for count in counts]

    def step(item, carry):
        a = (item >= whole[0]).astype(jnp.int32)
        some_runs(a, (item - a * whole[0]) * TILE, TILE)
        return carry

    lax.fori_loop(0, whole[0] + whole[1], step, 0)

    def remainder(a, carry):
        count = jnp.where(a == 0, counts[0], counts[1])
        start = count // TILE * TILE
        runs = TILE // 2
        while runs >= keep:

            @pl.when(count & runs != 0)
            def _():
                some_runs(a, start, runs)

            start = start + (count & runs)
            runs //= 2
        return carry

    lax.fori_loop(0, 2, remainder, 0)

    if not last:
        row = lax.broadcasted_iota(jnp.int32, meta.shape, 0)
        for a in range(2):
            start = counts[a] // keep * keep
            rest = counts[a] - start
            if keep > 1:

                @pl.when((start > 0) & (rest > 0))
                def _():
                    for n in range(keep - 1):
                        buf[a, n] = buf[a, start + n]

            meta = jnp.where(row == 2 + a, rest.astype(jnp.float32), meta)
        meta_ref[...] = meta
        return

    made, sems = refs[5:]
    copies = []
    for a in range(2):
        for h in range(0, heads_kv, 2):
            done = []
            for g in (h, h + 1):
                total = jnp.sum(state_refs[1][a, g], axis=1, keepdims=True)
                part = state_refs[2][a, g] * (1.0 / total)
                done.append(part.reshape(RUN, group, -1))
            place = (slice(a * RUN, (a + 1) * RUN), slice(h * group, (h + 2) * group))
            made[place] = jnp.concatenate(done, axis=1).astype(out_ref.dtype)
            copy = pltpu.make_async_copy(
                made.at[place], out_ref.at[place], sems.at[len(copies)]
            )
            copy.start()
            copies.append(copy)
    for copy in copies:
        copy.wait()


def pack_kernel(k_any, v_any, positions_any, own_ref, k_ref, v_ref, positions_ref, sems):
    pairs = ((k_any, k_ref), (v_any, v_ref), (positions_any, positions_ref))
    copies = [
        pltpu.make_async_copy(source, target, sems.at[n])
        for n, (source, target) in enumerate(pairs)
    ]
    for copy in copies:
        copy.start()
    heads_kv = k_ref.shape[0] // (2 * RUN)
    rows = heads_kv * RUN
    at = lax.broadcasted_iota(jnp.int32, (rows, rows), 0)
    origin = lax.broadcasted_iota(jnp.int32, (rows, rows), 1)
    move = at % RUN * heads_kv + at // RUN == origin
    move = jnp.where(move, 1.0, 0.0).astype(k_ref.dtype)
    for n, ref in enumerate((k_ref, v_ref)):
        copies[n].wait()
        for r in range(2):
            moved = jnp.dot(
                move,
                ref[r * rows : (r + 1) * rows],
                preferred_element_type=jnp.float32,
            )
            start = (2 * r + n) * rows
            own_ref[start : start + rows] = moved.astype(own_ref.dtype)
    copies[2].wait()
    numbers = (positions_ref[...] // RUN).astype(jnp.float32)
    numbers = jnp.broadcast_to(numbers, (16, numbers.shape[1]))
    own_ref[4 * rows :] = numbers.astype(own_ref.dtype)


class Attention:
    def __init__(self, q, group, half, room):
        self.q, self.group, self.half = q, group, half
        self.factor = math.log2(math.e) / math.sqrt(q.shape[3])
        heads_kv, rows, head_dim = q.shape[1:]
        self.block_rows = 4 * heads_kv * RUN + 16
        slots = 2 * room + KEEP
        self.carried = [jax.ShapeDtypeStruct((8, 128), jnp.float32)]
        self.carried += [
            jax.ShapeDtypeStruct((2, heads_kv, rows, n), jnp.float32)
            for n in (128, 128, head_dim)
        ]
        self.carried.append(
            jax.ShapeDtypeStruct((2, slots, 2 * heads_kv * RUN, head_dim), q.dtype)
        )

    def call(self, kernel, operands, shapes, aliases, count, name, out=None):
        vmem = pl.BlockSpec(memory_space=pltpu.VMEM)
        out_specs = [vmem] * len(shapes)
        scratch = []
        if out is not None:
            shapes = [out, *shapes]
            out_specs.insert(0, pl.BlockSpec(memory_space=pl.ANY))
            scratch = [pltpu.VMEM(out.shape, out.dtype), pltpu.SemaphoreType.DMA((8,))]
        return pl.pallas_call(
            kernel,
            out_shape=shapes,
            in_specs=[vmem] * len(operands),
            out_specs=out_specs,
            scratch_shapes=scratch,
            input_output_aliases=aliases,
            compiler_params=pltpu.CompilerParams(vmem_limit_bytes=28 * 1024 * 1024),
            cost_estimate=pl.CostEstimate(
                flops=1 * count * RUN * self.q.size * 4,
                bytes_accessed=self.q.size * 8 * 1,
                transcendentals=0,
            ),
            name=name,
        )(*operands)

    def start(self, own):
        kernel = functools.partial(own_kernel, self.group, self.factor, self.half)
        return self.call(kernel, [self.q, own], self.carried, {}, 2, "attend_own")

    def add(self, state, kvs, keep=KEEP, out=None):
        kvs = [x if isinstance(x, tuple) else (x, 0) for x in kvs]
        blocks = [(skip, x.shape[0] // self.block_rows) for x, skip in kvs]
        count = sum(end - skip for skip, end in blocks)
        operands = [self.q, *(x for x, _ in kvs), *state]
        first, ahead = 1 + len(kvs), int(out is not None)
        aliases = {first + n: ahead + n for n in range(len(state))}
        kernel = functools.partial(
            attend_kernel, self.group, self.factor, self.half, ahead, keep, blocks
        )
        results = self.call(kernel, operands, self.carried, aliases, count, "attend", out)
        return results[0] if ahead else results


def per_device(queries, keys, values, positions):
    outer, inner = lax.axis_size("outer"), lax.axis_size("inner")
    tokens, heads_q, head_dim = queries.shape
    heads_kv = keys.shape[1]
    group = heads_q // heads_kv
    half = tokens // RUN * outer * inner // 2

    chips = outer // 2
    bits = inner.bit_length() - 1
    ring = [0] + list(range(1, chips, 2)) + list(range(2, chips, 2))[::-1]
    after = {ring[n]: ring[(n + 1) % chips] for n in range(chips)}

    def permute(x, to):
        pairs = []
        for z in range(chips):
            for core in range(2):
                for place in range(inner):
                    nz, ncore, nplace = to(z, core, place)
                    pairs.append(
                        (
                            (2 * z + core) * inner + place,
                            (2 * nz + ncore) * inner + nplace,
                        )
                    )
        return lax.ppermute(x, AXES, pairs)

    def along_z(x):
        return permute(x, lambda z, core, place: (after[z], core, place))

    def over_place(x, step):
        def to(z, core, place):
            return z, core, place ^ (1 << (bits - 1 - step if core else step))

        return permute(x, to)

    def other_core(x):
        return permute(x, lambda z, core, place: (z, 1 - core, place))

    def tied(x, *others):
        return lax.optimization_barrier((x, *others))[0]

    flat = jax.ShapeDtypeStruct((tokens * heads_kv, head_dim), keys.dtype)
    own = pl.pallas_call(
        pack_kernel,
        out_shape=jax.ShapeDtypeStruct(
            (2 * tokens * heads_kv + 16, head_dim), keys.dtype
        ),
        in_specs=[pl.BlockSpec(memory_space=pltpu.HBM)] * 3,
        out_specs=pl.BlockSpec(memory_space=pltpu.VMEM),
        scratch_shapes=[
            pltpu.VMEM(flat.shape, flat.dtype),
            pltpu.VMEM(flat.shape, flat.dtype),
            pltpu.VMEM((1, tokens), jnp.int32),
            pltpu.SemaphoreType.DMA((3,)),
        ],
        compiler_params=pltpu.CompilerParams(vmem_limit_bytes=60 * 1024 * 1024),
        name="pack",
    )(keys.reshape(flat.shape), values.reshape(flat.shape), positions.reshape(1, tokens))
    q = (
        queries.reshape(2, RUN, heads_kv, group, head_dim)
        .transpose(0, 2, 1, 3, 4)
        .reshape(2, heads_kv, RUN * group, head_dim)
    )

    attention = Attention(q, group, half, 2 * inner)
    state = attention.start(own)

    stages = [own]
    for n in range(1, chips):
        stages.append(along_z(stages[-1]))
    todo = []
    for n, stage in enumerate(stages[:-1]):
        found = [stage]
        if n == 0:
            ones = [over_place(stage, step) for step in range(bits)]
            for step in range(bits):
                there = [ones[step]]
                for x in found[1:]:
                    there.append(over_place(x, step))
                if step:
                    there[1] = over_place(tied(found[1], stages[1], state[0]), step)
                found += there
            held = jnp.concatenate(found)
        else:
            held = tied(stage, *ones, state[0]) if n == 1 else stage
            for step in range(bits):
                there = over_place(held, step)
                if todo and (step == 0 and n > 1 or step + 1 == bits and n + 2 == chips):
                    state = attention.add(state, todo.pop(0))
                    there = tied(there, state[0])
                held = jnp.concatenate([held, there])
        theirs = other_core(held)
        todo.append([(held, int(n == 0)), theirs])

    found = [stages[-1]]
    for step in range(bits):
        found += [over_place(x, step) for x in found]
    *most, final = found
    mine, theirs = todo.pop()
    most = jnp.concatenate(most)
    state = attention.add(state, [mine, most])
    state = attention.add(state, [theirs, other_core(most)])
    final = tied(final, state[0])
    theirs = other_core(final)
    state = attention.add(state, [final], keep=1)
    out = jax.ShapeDtypeStruct(queries.shape, queries.dtype)
    return attention.add(state, [theirs], keep=1, out=out)


def solution(mesh):
    in_specs = (
        P(("outer", "inner"), None, None),
        P(("outer", "inner"), None, None),
        P(("outer", "inner"), None, None),
        P(("outer", "inner")),
    )
    out_specs = P(("outer", "inner"), None, None)
    return jax.shard_map(
        per_device, mesh=mesh, in_specs=in_specs, out_specs=out_specs, check_vma=False
    )
```

```python
import functools
import math

import jax
import jax.numpy as jnp
from jax import lax
from jax.experimental import pallas as pl
from jax.experimental.pallas import tpu as pltpu
from jax.sharding import PartitionSpec as P

RUN = 64
TILE = 8
KEEP = 4
AXES = ("outer", "inner")


def flash(score, v, state, factor, live=None):
    top, mixed = state
    keys = score.shape[1]
    if isinstance(live, int):
        lane = lax.broadcasted_iota(jnp.int32, score.shape, 1)
        keys, live = live, lane < live
    if live is not None:
        score = jnp.where(live, score, -jnp.inf)
    parts = [score[:, c : c + 128] for c in range(0, score.shape[1], 128)]
    new = jnp.max(functools.reduce(jnp.maximum, parts), axis=1, keepdims=True)
    if top is None:
        new = jnp.broadcast_to(new, parts[0].shape)
    else:
        new = jnp.maximum(top, new)
    weights = [
        jnp.exp2((part - new) * factor).astype(jnp.bfloat16) for part in parts
    ]
    weights = jnp.concatenate(weights, axis=1)
    ones = jnp.ones((keys, 128), v.dtype)
    part_mixed = jnp.dot(
        weights[:, :keys],
        jnp.concatenate([v, ones], axis=1),
        preferred_element_type=jnp.float32,
    )
    if top is None:
        return new, part_mixed
    decay = jnp.exp2((top - new) * factor)
    halves = [
        mixed[:, c : c + 128] * decay + part_mixed[:, c : c + 128]
        for c in range(0, mixed.shape[1], 128)
    ]
    return new, jnp.concatenate(halves, axis=1)


def head_tile(q_ref, state_refs, a, keys, values, factor, live=None):
    def scores(h):
        return lax.dot_general(
            q_ref[a, h],
            keys(h),
            (((1,), (1,)), ((), ())),
            preferred_element_type=jnp.float32,
        )

    heads_kv = q_ref.shape[1]
    ahead = scores(0)
    for h in range(heads_kv):
        score = ahead
        if h + 1 < heads_kv:
            ahead = scores(h + 1)
        state = (None, None)
        if live is None or isinstance(live, int):
            state = tuple(ref[a, h] for ref in state_refs)
        state = flash(score, values(h), state, factor, live)
        for ref, value in zip(state_refs, state):
            ref[a, h] = value


def own_kernel(group, factor, half, q_ref, own_ref, meta_ref, *refs):
    heads_kv, rows, head_dim = q_ref.shape[1:]
    state_refs = refs[:2]
    run_rows = 2 * heads_kv * RUN

    ids = own_ref[2 * run_rows :].astype(jnp.float32)
    lane = lax.broadcasted_iota(jnp.int32, ids.shape, 1)
    numbers = [jnp.max(jnp.where(lane // RUN == a, ids, 0.0)) for a in range(2)]
    row = lax.broadcasted_iota(jnp.int32, meta_ref.shape, 0)
    meta_ref[...] = jnp.where(
        row == 0, numbers[0], jnp.where(row == 1, numbers[1], 0.0)
    )

    row_at = lax.broadcasted_iota(jnp.int32, (rows, 2 * RUN), 0) // group
    key_at = lax.broadcasted_iota(jnp.int32, (rows, 2 * RUN), 1)
    for a in range(2):
        mine, other = numbers[a], numbers[1 - a]
        seen = (other < mine) & ((other >= half) == (mine >= half))
        reach = jnp.where(seen, RUN, 0)
        if a == 0:
            live = (key_at <= row_at) | ((key_at >= RUN) & (key_at < RUN + reach))
        else:
            live = (key_at < reach) | ((key_at >= RUN) & (key_at - RUN <= row_at))

        def own(g):
            starts = [g * RUN, run_rows + g * RUN]
            return jnp.concatenate([own_ref[n : n + RUN] for n in starts])

        head_tile(q_ref, state_refs, a, own, lambda h: own(heads_kv + h), factor, live)


def attend_kernel(group, factor, half, last, keep, blocks, q_ref, *refs):
    heads_kv, rows, head_dim = q_ref.shape[1:]
    run_rows = 2 * heads_kv * RUN
    block_rows = 2 * run_rows + 16
    kv_refs, refs = refs[: len(blocks)], refs[len(blocks) :]
    refs = refs[4:]
    if last:
        out_ref, refs = refs[0], refs[1:]
    meta_ref, *state_refs, buf = refs[:4]

    meta = meta_ref[...]
    counts = tuple(
        jnp.max(meta[2 + a : 3 + a]).astype(jnp.int32) for a in range(2)
    )
    seen_bits = []
    for ref, (skip, end) in zip(kv_refs, blocks):
        assert end - skip <= 8
        ids = jnp.concatenate(
            [ref[n * block_rows - 16 : n * block_rows] for n in range(skip + 1, end + 1)]
        ).astype(jnp.float32)
        row = lax.broadcasted_iota(jnp.int32, ids.shape, 0)
        lane = lax.broadcasted_iota(jnp.int32, ids.shape, 1)
        bit = jnp.left_shift(1, 2 * (row // 16) + lane // RUN)
        bit = jnp.where((row % 16 == 0) & (lane % RUN == 0), bit, 0).astype(jnp.float32)
        found = []
        for a in range(2):
            mine = meta[a : a + 1]
            low = jnp.where(mine >= half, float(half), 0.0)
            seen = (ids < mine) & (ids >= low)
            found.append(jnp.sum(jnp.where(seen, bit, 0.0)).astype(jnp.int32))
        seen_bits.append(found)

    for ref, (skip, end), bits in zip(kv_refs, blocks, seen_bits):

        def gather(n, counts):
            at = pl.multiple_of((skip + n // 2) * block_rows + n % 2 * run_rows, 16)
            fresh = []
            for a in range(2):
                flag = (bits[a] >> n) & 1
                count = counts[a]

                @pl.when(flag == 1)
                def _():
                    buf[a, count] = ref[pl.ds(at, run_rows), :]

                fresh.append(count + flag)
            return tuple(fresh)

        counts = lax.fori_loop(0, 2 * (end - skip), gather, counts)

    def some_runs(a, start, runs):
        def rows_of(g):
            found = buf[a, pl.ds(start, runs), g * RUN : (g + 1) * RUN, :]
            return found.reshape(runs * RUN, -1)

        def keys(h):
            if runs > 1:
                return rows_of(h)
            return jnp.concatenate([rows_of(h), jnp.zeros((RUN, head_dim), buf.dtype)])

        live = RUN if runs == 1 else None
        head_tile(
            q_ref, state_refs, a, keys, lambda h: rows_of(heads_kv + h), factor, live
        )

    whole = [count // TILE for count in counts]

    def step(item, carry):
        a = (item >= whole[0]).astype(jnp.int32)
        some_runs(a, (item - a * whole[0]) * TILE, TILE)
        return carry

    lax.fori_loop(0, whole[0] + whole[1], step, 0)

    def remainder(a, carry):
        count = jnp.where(a == 0, counts[0], counts[1])
        start = count // TILE * TILE
        runs = TILE // 2
        while runs >= keep:

            @pl.when(count & runs != 0)
            def _():
                some_runs(a, start, runs)

            start = start + (count & runs)
            runs //= 2
        return carry

    lax.fori_loop(0, 2, remainder, 0)

    if not last:
        row = lax.broadcasted_iota(jnp.int32, meta.shape, 0)
        for a in range(2):
            start = counts[a] // keep * keep
            rest = counts[a] - start
            if keep > 1:

                @pl.when((start > 0) & (rest > 0))
                def _():
                    for n in range(keep - 1):
                        buf[a, n] = buf[a, start + n]

            meta = jnp.where(row == 2 + a, rest.astype(jnp.float32), meta)
        meta_ref[...] = meta
        return

    made, sems = refs[4:]
    copies = []
    for a in range(2):
        for h in range(0, heads_kv, 2):
            done = []
            for g in (h, h + 1):
                mixed = state_refs[1][a, g]
                part = mixed[:, :head_dim] * (1.0 / mixed[:, head_dim:])
                done.append(part.reshape(RUN, group, -1))
            place = (slice(a * RUN, (a + 1) * RUN), slice(h * group, (h + 2) * group))
            made[place] = jnp.concatenate(done, axis=1).astype(out_ref.dtype)
            copy = pltpu.make_async_copy(
                made.at[place], out_ref.at[place], sems.at[len(copies)]
            )
            copy.start()
            copies.append(copy)
    for copy in copies:
        copy.wait()


def pack_kernel(k_any, v_any, positions_any, own_ref, k_ref, v_ref, positions_ref, sems):
    pairs = ((k_any, k_ref), (v_any, v_ref), (positions_any, positions_ref))
    copies = [
        pltpu.make_async_copy(source, target, sems.at[n])
        for n, (source, target) in enumerate(pairs)
    ]
    for copy in copies:
        copy.start()
    heads_kv = k_ref.shape[0] // (2 * RUN)
    rows = heads_kv * RUN
    at = lax.broadcasted_iota(jnp.int32, (rows, rows), 0)
    origin = lax.broadcasted_iota(jnp.int32, (rows, rows), 1)
    move = at % RUN * heads_kv + at // RUN == origin
    move = jnp.where(move, 1.0, 0.0).astype(k_ref.dtype)
    for n, ref in enumerate((k_ref, v_ref)):
        copies[n].wait()
        for r in range(2):
            moved = jnp.dot(
                move,
                ref[r * rows : (r + 1) * rows],
                preferred_element_type=jnp.float32,
            )
            start = (2 * r + n) * rows
            own_ref[start : start + rows] = moved.astype(own_ref.dtype)
    copies[2].wait()
    numbers = (positions_ref[...] // RUN).astype(jnp.float32)
    numbers = jnp.broadcast_to(numbers, (16, numbers.shape[1]))
    own_ref[4 * rows :] = numbers.astype(own_ref.dtype)


class Attention:
    def __init__(self, q, group, half, room):
        self.q, self.group, self.half = q, group, half
        self.factor = math.log2(math.e) / math.sqrt(q.shape[3])
        heads_kv, rows, head_dim = q.shape[1:]
        self.block_rows = 4 * heads_kv * RUN + 16
        slots = 2 * room + TILE
        self.carried = [jax.ShapeDtypeStruct((8, 128), jnp.float32)]
        self.carried += [
            jax.ShapeDtypeStruct((2, heads_kv, rows, n), jnp.float32)
            for n in (128, head_dim + 128)
        ]
        self.carried.append(
            jax.ShapeDtypeStruct((2, slots, 2 * heads_kv * RUN, head_dim), q.dtype)
        )

    def call(self, kernel, operands, shapes, aliases, count, name, out=None):
        vmem = pl.BlockSpec(memory_space=pltpu.VMEM)
        out_specs = [vmem] * len(shapes)
        scratch = []
        if out is not None:
            shapes = [out, *shapes]
            out_specs.insert(0, pl.BlockSpec(memory_space=pl.ANY))
            scratch = [pltpu.VMEM(out.shape, out.dtype), pltpu.SemaphoreType.DMA((8,))]
        return pl.pallas_call(
            kernel,
            out_shape=shapes,
            in_specs=[vmem] * len(operands),
            out_specs=out_specs,
            scratch_shapes=scratch,
            input_output_aliases=aliases,
            compiler_params=pltpu.CompilerParams(vmem_limit_bytes=28 * 1024 * 1024),
            cost_estimate=pl.CostEstimate(
                flops=1 * count * RUN * self.q.size * 4,
                bytes_accessed=self.q.size * 8 * 1,
                transcendentals=0,
            ),
            name=name,
        )(*operands)

    def start(self, own):
        kernel = functools.partial(own_kernel, self.group, self.factor, self.half)
        return self.call(kernel, [self.q, own], self.carried, {}, 2, "attend_own")

    def add(self, state, kvs, keep=KEEP, out=None):
        kvs = [x if isinstance(x, tuple) else (x, 0) for x in kvs]
        blocks = [(skip, x.shape[0] // self.block_rows) for x, skip in kvs]
        count = sum(end - skip for skip, end in blocks)
        operands = [self.q, *(x for x, _ in kvs), *state]
        first, ahead = 1 + len(kvs), int(out is not None)
        aliases = {first + n: ahead + n for n in range(len(state))}
        kernel = functools.partial(
            attend_kernel, self.group, self.factor, self.half, ahead, keep, blocks
        )
        results = self.call(kernel, operands, self.carried, aliases, count, "attend", out)
        return results[0] if ahead else results


def per_device(queries, keys, values, positions):
    outer, inner = lax.axis_size("outer"), lax.axis_size("inner")
    tokens, heads_q, head_dim = queries.shape
    heads_kv = keys.shape[1]
    group = heads_q // heads_kv
    half = tokens // RUN * outer * inner // 2

    chips = outer // 2
    bits = inner.bit_length() - 1
    ring = [0] + list(range(1, chips, 2)) + list(range(2, chips, 2))[::-1]
    after = {ring[n]: ring[(n + 1) % chips] for n in range(chips)}

    def permute(x, to):
        pairs = []
        for z in range(chips):
            for core in range(2):
                for place in range(inner):
                    nz, ncore, nplace = to(z, core, place)
                    pairs.append(
                        (
                            (2 * z + core) * inner + place,
                            (2 * nz + ncore) * inner + nplace,
                        )
                    )
        return lax.ppermute(x, AXES, pairs)

    def along_z(x):
        return permute(x, lambda z, core, place: (after[z], core, place))

    def over_place(x, step):
        def to(z, core, place):
            return z, core, place ^ (1 << (bits - 1 - step if core else step))

        return permute(x, to)

    def other_core(x):
        return permute(x, lambda z, core, place: (z, 1 - core, place))

    def tied(x, *others):
        return lax.optimization_barrier((x, *others))[0]

    flat = jax.ShapeDtypeStruct((tokens * heads_kv, head_dim), keys.dtype)
    own = pl.pallas_call(
        pack_kernel,
        out_shape=jax.ShapeDtypeStruct(
            (2 * tokens * heads_kv + 16, head_dim), keys.dtype
        ),
        in_specs=[pl.BlockSpec(memory_space=pltpu.HBM)] * 3,
        out_specs=pl.BlockSpec(memory_space=pltpu.VMEM),
        scratch_shapes=[
            pltpu.VMEM(flat.shape, flat.dtype),
            pltpu.VMEM(flat.shape, flat.dtype),
            pltpu.VMEM((1, tokens), jnp.int32),
            pltpu.SemaphoreType.DMA((3,)),
        ],
        compiler_params=pltpu.CompilerParams(vmem_limit_bytes=60 * 1024 * 1024),
        name="pack",
    )(keys.reshape(flat.shape), values.reshape(flat.shape), positions.reshape(1, tokens))
    q = (
        queries.reshape(2, RUN, heads_kv, group, head_dim)
        .transpose(0, 2, 1, 3, 4)
        .reshape(2, heads_kv, RUN * group, head_dim)
    )

    attention = Attention(q, group, half, 2 * inner)
    state = attention.start(own)

    stage, waiting = own, None
    for n in range(chips - 1):
        following = along_z(stage)
        found = [stage]
        if n == 0:
            ones = [over_place(stage, step) for step in range(bits)]
            for step in range(bits):
                there = [ones[step]]
                for x in found[1:]:
                    there.append(over_place(x, step))
                if step:
                    there[1] = over_place(tied(found[1], following, state[0]), step)
                found += there
            held = jnp.concatenate(found)
        else:
            held = tied(stage, *ones, state[0]) if n == 1 else stage
            for step in range(bits):
                held = jnp.concatenate([held, over_place(held, step)])
        if waiting:
            state = attention.add(state, waiting, keep=TILE)
            held = tied(held, state[0])
        waiting = [(held, int(n == 0)), other_core(held)]
        stage = following

    found = [stage]
    for step in range(bits):
        found += [over_place(x, step) for x in found]
    *most, final = found
    most = jnp.concatenate(most)
    theirs = other_core(most)
    state = attention.add(state, waiting)
    state = attention.add(state, [most, theirs])
    final = tied(final, state[0])
    theirs = other_core(final)
    state = attention.add(state, [final], keep=1)
    out = jax.ShapeDtypeStruct(queries.shape, queries.dtype)
    return attention.add(state, [theirs], keep=1, out=out)


def solution(mesh):
    in_specs = (
        P(("outer", "inner"), None, None),
        P(("outer", "inner"), None, None),
        P(("outer", "inner"), None, None),
        P(("outer", "inner")),
    )
    out_specs = P(("outer", "inner"), None, None)
    return jax.shard_map(
        per_device, mesh=mesh, in_specs=in_specs, out_specs=out_specs, check_vma=False
    )
```

```python
import functools
import math

import jax
import jax.numpy as jnp
from jax import lax
from jax.experimental import pallas as pl
from jax.experimental.pallas import tpu as pltpu
from jax.sharding import PartitionSpec as P

RUN = 64
TILE = 8
KEEP = 4
AXES = ("outer", "inner")


def flash(score, v, state, factor, live=None):
    top, mixed = state
    keys = score.shape[1]
    if isinstance(live, int):
        lane = lax.broadcasted_iota(jnp.int32, score.shape, 1)
        keys, live = live, lane < live
    if live is not None:
        score = jnp.where(live, score, -jnp.inf)
    parts = [score[:, c : c + 128] for c in range(0, score.shape[1], 128)]
    new = jnp.max(functools.reduce(jnp.maximum, parts), axis=1, keepdims=True)
    if top is None:
        new = jnp.broadcast_to(new, parts[0].shape)
    else:
        new = jnp.maximum(top, new)
    weights = [
        jnp.exp2((part - new) * factor).astype(jnp.bfloat16) for part in parts
    ]
    weights = jnp.concatenate(weights, axis=1)
    ones = jnp.ones((keys, 128), v.dtype)
    part_mixed = jnp.dot(
        weights[:, :keys],
        jnp.concatenate([v, ones], axis=1),
        preferred_element_type=jnp.float32,
    )
    if top is None:
        return new, part_mixed
    decay = jnp.exp2((top - new) * factor)
    halves = [
        mixed[:, c : c + 128] * decay + part_mixed[:, c : c + 128]
        for c in range(0, mixed.shape[1], 128)
    ]
    return new, jnp.concatenate(halves, axis=1)


def head_tile(q_ref, state_refs, a, keys, values, factor, live=None):
    def scores(h):
        return lax.dot_general(
            q_ref[a, h],
            keys(h),
            (((1,), (1,)), ((), ())),
            preferred_element_type=jnp.float32,
        )

    heads_kv = q_ref.shape[1]
    ahead = scores(0)
    for h in range(heads_kv):
        score = ahead
        if h + 1 < heads_kv:
            ahead = scores(h + 1)
        state = (None, None)
        if live is None or isinstance(live, int):
            state = tuple(ref[a, h] for ref in state_refs)
        state = flash(score, values(h), state, factor, live)
        for ref, value in zip(state_refs, state):
            ref[a, h] = value


def own_kernel(group, factor, half, q_ref, own_ref, meta_ref, *refs):
    heads_kv, rows, head_dim = q_ref.shape[1:]
    state_refs = refs[:2]
    run_rows = 2 * heads_kv * RUN

    ids = own_ref[2 * run_rows :].astype(jnp.float32)
    lane = lax.broadcasted_iota(jnp.int32, ids.shape, 1)
    numbers = [jnp.max(jnp.where(lane // RUN == a, ids, 0.0)) for a in range(2)]
    row = lax.broadcasted_iota(jnp.int32, meta_ref.shape, 0)
    meta_ref[...] = jnp.where(
        row == 0, numbers[0], jnp.where(row == 1, numbers[1], 0.0)
    )

    row_at = lax.broadcasted_iota(jnp.int32, (rows, 2 * RUN), 0) // group
    key_at = lax.broadcasted_iota(jnp.int32, (rows, 2 * RUN), 1)
    for a in range(2):
        mine, other = numbers[a], numbers[1 - a]
        seen = (other < mine) & ((other >= half) == (mine >= half))
        reach = jnp.where(seen, RUN, 0)
        if a == 0:
            live = (key_at <= row_at) | ((key_at >= RUN) & (key_at < RUN + reach))
        else:
            live = (key_at < reach) | ((key_at >= RUN) & (key_at - RUN <= row_at))

        def own(g):
            starts = [g * RUN, run_rows + g * RUN]
            return jnp.concatenate([own_ref[n : n + RUN] for n in starts])

        head_tile(q_ref, state_refs, a, own, lambda h: own(heads_kv + h), factor, live)


def attend_kernel(group, factor, half, last, keep, blocks, q_ref, *refs):
    heads_kv, rows, head_dim = q_ref.shape[1:]
    run_rows = 2 * heads_kv * RUN
    block_rows = 2 * run_rows + 16
    kv_refs, refs = refs[: len(blocks)], refs[len(blocks) :]
    refs = refs[4:]
    if last:
        out_ref, refs = refs[0], refs[1:]
    meta_ref, *state_refs, buf = refs[:4]

    meta = meta_ref[...]
    counts = tuple(
        jnp.max(meta[2 + a : 3 + a]).astype(jnp.int32) for a in range(2)
    )
    seen_bits = []
    for ref, (skip, end) in zip(kv_refs, blocks):
        assert end - skip <= 8
        ids = jnp.concatenate(
            [ref[n * block_rows - 16 : n * block_rows] for n in range(skip + 1, end + 1)]
        ).astype(jnp.float32)
        row = lax.broadcasted_iota(jnp.int32, ids.shape, 0)
        lane = lax.broadcasted_iota(jnp.int32, ids.shape, 1)
        bit = jnp.left_shift(1, 2 * (row // 16) + lane // RUN)
        bit = jnp.where((row % 16 == 0) & (lane % RUN == 0), bit, 0).astype(jnp.float32)
        found = []
        for a in range(2):
            mine = meta[a : a + 1]
            low = jnp.where(mine >= half, float(half), 0.0)
            seen = (ids < mine) & (ids >= low)
            found.append(jnp.sum(jnp.where(seen, bit, 0.0)).astype(jnp.int32))
        seen_bits.append(found)

    for ref, (skip, end), bits in zip(kv_refs, blocks, seen_bits):

        def gather(n, counts):
            at = pl.multiple_of((skip + n // 2) * block_rows + n % 2 * run_rows, 16)
            fresh = []
            for a in range(2):
                flag = (bits[a] >> n) & 1
                count = counts[a]

                @pl.when(flag == 1)
                def _():
                    buf[a, count] = ref[pl.ds(at, run_rows), :]

                fresh.append(count + flag)
            return tuple(fresh)

        counts = lax.fori_loop(0, 2 * (end - skip), gather, counts)

    def some_runs(a, start, runs):
        def rows_of(g):
            found = buf[a, pl.ds(start, runs), g * RUN : (g + 1) * RUN, :]
            return found.reshape(runs * RUN, -1)

        def keys(h):
            if runs > 1:
                return rows_of(h)
            return jnp.concatenate([rows_of(h), jnp.zeros((RUN, head_dim), buf.dtype)])

        live = RUN if runs == 1 else None
        head_tile(
            q_ref, state_refs, a, keys, lambda h: rows_of(heads_kv + h), factor, live
        )

    whole = [count // TILE for count in counts]

    def step(item, carry):
        a = (item >= whole[0]).astype(jnp.int32)
        some_runs(a, (item - a * whole[0]) * TILE, TILE)
        return carry

    lax.fori_loop(0, whole[0] + whole[1], step, 0)

    def remainder(a, carry):
        count = jnp.where(a == 0, counts[0], counts[1])
        start = count // TILE * TILE
        runs = TILE // 2
        while runs >= keep:

            @pl.when(count & runs != 0)
            def _():
                some_runs(a, start, runs)

            start = start + (count & runs)
            runs //= 2
        return carry

    lax.fori_loop(0, 2, remainder, 0)

    if not last:
        row = lax.broadcasted_iota(jnp.int32, meta.shape, 0)
        for a in range(2):
            start = counts[a] // keep * keep
            rest = counts[a] - start
            if keep > 1:

                @pl.when((start > 0) & (rest > 0))
                def _():
                    for n in range(keep - 1):
                        buf[a, n] = buf[a, start + n]

            meta = jnp.where(row == 2 + a, rest.astype(jnp.float32), meta)
        meta_ref[...] = meta
        return

    made, sems = refs[4:]
    copies = []
    for a in range(2):
        for h in range(0, heads_kv, 2):
            done = []
            for g in (h, h + 1):
                mixed = state_refs[1][a, g]
                part = mixed[:, :head_dim] * (1.0 / mixed[:, head_dim:])
                done.append(part.reshape(RUN, group, -1))
            place = (slice(a * RUN, (a + 1) * RUN), slice(h * group, (h + 2) * group))
            made[place] = jnp.concatenate(done, axis=1).astype(out_ref.dtype)
            copy = pltpu.make_async_copy(
                made.at[place], out_ref.at[place], sems.at[len(copies)]
            )
            copy.start()
            copies.append(copy)
    for copy in copies:
        copy.wait()


def pack_kernel(k_any, v_any, positions_any, own_ref, k_ref, v_ref, positions_ref, sems):
    pairs = ((k_any, k_ref), (v_any, v_ref), (positions_any, positions_ref))
    copies = [
        pltpu.make_async_copy(source, target, sems.at[n])
        for n, (source, target) in enumerate(pairs)
    ]
    for copy in copies:
        copy.start()
    heads_kv = k_ref.shape[0] // (2 * RUN)
    rows = heads_kv * RUN
    at = lax.broadcasted_iota(jnp.int32, (rows, rows), 0)
    origin = lax.broadcasted_iota(jnp.int32, (rows, rows), 1)
    move = at % RUN * heads_kv + at // RUN == origin
    move = jnp.where(move, 1.0, 0.0).astype(k_ref.dtype)
    for n, ref in enumerate((k_ref, v_ref)):
        copies[n].wait()
        for r in range(2):
            moved = jnp.dot(
                move,
                ref[r * rows : (r + 1) * rows],
                preferred_element_type=jnp.float32,
            )
            start = (2 * r + n) * rows
            own_ref[start : start + rows] = moved.astype(own_ref.dtype)
    copies[2].wait()
    numbers = (positions_ref[...] // RUN).astype(jnp.float32)
    numbers = jnp.broadcast_to(numbers, (16, numbers.shape[1]))
    own_ref[4 * rows :] = numbers.astype(own_ref.dtype)


class Attention:
    def __init__(self, q, group, half, room):
        self.q, self.group, self.half = q, group, half
        self.factor = math.log2(math.e) / math.sqrt(q.shape[3])
        heads_kv, rows, head_dim = q.shape[1:]
        self.block_rows = 4 * heads_kv * RUN + 16
        slots = 2 * room + TILE
        self.carried = [jax.ShapeDtypeStruct((8, 128), jnp.float32)]
        self.carried += [
            jax.ShapeDtypeStruct((2, heads_kv, rows, n), jnp.float32)
            for n in (128, head_dim + 128)
        ]
        self.carried.append(
            jax.ShapeDtypeStruct((2, slots, 2 * heads_kv * RUN, head_dim), q.dtype)
        )

    def call(self, kernel, operands, shapes, aliases, count, name, out=None):
        vmem = pl.BlockSpec(memory_space=pltpu.VMEM)
        out_specs = [vmem] * len(shapes)
        scratch = []
        if out is not None:
            shapes = [out, *shapes]
            out_specs.insert(0, pl.BlockSpec(memory_space=pl.ANY))
            scratch = [pltpu.VMEM(out.shape, out.dtype), pltpu.SemaphoreType.DMA((8,))]
        return pl.pallas_call(
            kernel,
            out_shape=shapes,
            in_specs=[vmem] * len(operands),
            out_specs=out_specs,
            scratch_shapes=scratch,
            input_output_aliases=aliases,
            compiler_params=pltpu.CompilerParams(vmem_limit_bytes=28 * 1024 * 1024),
            cost_estimate=pl.CostEstimate(
                flops=5 * count * RUN * self.q.size * 4,
                bytes_accessed=self.q.size * 8 * 5,
                transcendentals=0,
            ),
            name=name,
        )(*operands)

    def start(self, own):
        kernel = functools.partial(own_kernel, self.group, self.factor, self.half)
        return self.call(kernel, [self.q, own], self.carried, {}, 2, "attend_own")

    def add(self, state, kvs, keep=KEEP, out=None):
        kvs = [x if isinstance(x, tuple) else (x, 0) for x in kvs]
        blocks = [(skip, x.shape[0] // self.block_rows) for x, skip in kvs]
        count = sum(end - skip for skip, end in blocks)
        operands = [self.q, *(x for x, _ in kvs), *state]
        first, ahead = 1 + len(kvs), int(out is not None)
        aliases = {first + n: ahead + n for n in range(len(state))}
        kernel = functools.partial(
            attend_kernel, self.group, self.factor, self.half, ahead, keep, blocks
        )
        results = self.call(kernel, operands, self.carried, aliases, count, "attend", out)
        return results[0] if ahead else results


def per_device(queries, keys, values, positions):
    outer, inner = lax.axis_size("outer"), lax.axis_size("inner")
    tokens, heads_q, head_dim = queries.shape
    heads_kv = keys.shape[1]
    group = heads_q // heads_kv
    half = tokens // RUN * outer * inner // 2

    chips = outer // 2
    bits = inner.bit_length() - 1
    ring = [0] + list(range(1, chips, 2)) + list(range(2, chips, 2))[::-1]
    after = {ring[n]: ring[(n + 1) % chips] for n in range(chips)}

    def permute(x, to):
        pairs = []
        for z in range(chips):
            for core in range(2):
                for place in range(inner):
                    nz, ncore, nplace = to(z, core, place)
                    pairs.append(
                        (
                            (2 * z + core) * inner + place,
                            (2 * nz + ncore) * inner + nplace,
                        )
                    )
        return lax.ppermute(x, AXES, pairs)

    def along_z(x):
        return permute(x, lambda z, core, place: (after[z], core, place))

    def over_place(x, step):
        def to(z, core, place):
            return z, core, place ^ (1 << (bits - 1 - step if core else step))

        return permute(x, to)

    def other_core(x):
        return permute(x, lambda z, core, place: (z, 1 - core, place))

    def tied(x, *others):
        return lax.optimization_barrier((x, *others))[0]

    flat = jax.ShapeDtypeStruct((tokens * heads_kv, head_dim), keys.dtype)
    own = pl.pallas_call(
        pack_kernel,
        out_shape=jax.ShapeDtypeStruct(
            (2 * tokens * heads_kv + 16, head_dim), keys.dtype
        ),
        in_specs=[pl.BlockSpec(memory_space=pltpu.HBM)] * 3,
        out_specs=pl.BlockSpec(memory_space=pltpu.VMEM),
        scratch_shapes=[
            pltpu.VMEM(flat.shape, flat.dtype),
            pltpu.VMEM(flat.shape, flat.dtype),
            pltpu.VMEM((1, tokens), jnp.int32),
            pltpu.SemaphoreType.DMA((3,)),
        ],
        compiler_params=pltpu.CompilerParams(vmem_limit_bytes=60 * 1024 * 1024),
        name="pack",
    )(keys.reshape(flat.shape), values.reshape(flat.shape), positions.reshape(1, tokens))
    q = (
        queries.reshape(2, RUN, heads_kv, group, head_dim)
        .transpose(0, 2, 1, 3, 4)
        .reshape(2, heads_kv, RUN * group, head_dim)
    )

    attention = Attention(q, group, half, 2 * inner)
    state = attention.start(own)

    stages = [own]
    for n in range(1, chips):
        stages.append(along_z(stages[-1]))
    waiting = None
    for n, stage in enumerate(stages[:-1]):
        held = stage
        for step in range(bits):
            if n == 0 and step + 1 == bits:
                held = tied(held, state[0])
            there = over_place(held, step)
            if n + 2 == chips and step + 1 == bits:
                state = attention.add(state, waiting)
                there = tied(there, state[0])
            held = jnp.concatenate([held, there])
        if waiting and n + 2 < chips:
            state = attention.add(state, waiting)
            held = tied(held, state[0])
        theirs = other_core(tied(held, *stages[n + 2 : n + 3 - n]))
        waiting = [(held, int(n == 0)), theirs]

    found = [stages[-1]]
    for step in range(bits):
        found += [over_place(x, step) for x in found]
    *most, final = found
    mine, theirs = waiting
    state = attention.add(state, [mine])
    most = jnp.concatenate(most[:1] + [tied(x, state[0]) for x in most[1:]])
    state = attention.add(state, [theirs, most])
    state = attention.add(state, [other_core(most)])
    final = tied(final, state[0])
    theirs = other_core(final)
    state = attention.add(state, [final], keep=1)
    out = jax.ShapeDtypeStruct(queries.shape, queries.dtype)
    return attention.add(state, [theirs], keep=1, out=out)


def solution(mesh):
    in_specs = (
        P(("outer", "inner"), None, None),
        P(("outer", "inner"), None, None),
        P(("outer", "inner"), None, None),
        P(("outer", "inner")),
    )
    out_specs = P(("outer", "inner"), None, None)
    return jax.shard_map(
        per_device, mesh=mesh, in_specs=in_specs, out_specs=out_specs, check_vma=False
    )
```

```python
import functools
import math

import jax
import jax.numpy as jnp
from jax import lax
from jax.experimental import pallas as pl
from jax.experimental.pallas import tpu as pltpu
from jax.sharding import PartitionSpec as P

RUN = 64
TILE = 8
KEEP = 4
AXES = ("outer", "inner")


def flash(score, v, state, factor, live=None):
    top, mixed = state
    keys = score.shape[1]
    if isinstance(live, int):
        lane = lax.broadcasted_iota(jnp.int32, score.shape, 1)
        keys, live = live, lane < live
    if live is not None:
        score = jnp.where(live, score, -jnp.inf)
    parts = [score[:, c : c + 128] for c in range(0, score.shape[1], 128)]
    new = jnp.max(functools.reduce(jnp.maximum, parts), axis=1, keepdims=True)
    if top is None:
        new = jnp.broadcast_to(new, parts[0].shape)
    else:
        new = jnp.maximum(top, new)
    weights = [
        jnp.exp2((part - new) * factor).astype(jnp.bfloat16) for part in parts
    ]
    weights = jnp.concatenate(weights, axis=1)
    ones = jnp.ones((keys, 128), v.dtype)
    part_mixed = jnp.dot(
        weights[:, :keys],
        jnp.concatenate([v, ones], axis=1),
        preferred_element_type=jnp.float32,
    )
    if top is None:
        return new, part_mixed
    decay = jnp.exp2((top - new) * factor)
    halves = [
        mixed[:, c : c + 128] * decay + part_mixed[:, c : c + 128]
        for c in range(0, mixed.shape[1], 128)
    ]
    return new, jnp.concatenate(halves, axis=1)


def head_tile(q_ref, state_refs, a, keys, values, factor, live=None):
    def scores(h):
        return lax.dot_general(
            q_ref[a, h],
            keys(h),
            (((1,), (1,)), ((), ())),
            preferred_element_type=jnp.float32,
        )

    heads_kv = q_ref.shape[1]
    ahead = scores(0)
    for h in range(heads_kv):
        score = ahead
        if h + 1 < heads_kv:
            ahead = scores(h + 1)
        state = (None, None)
        if live is None or isinstance(live, int):
            state = tuple(ref[a, h] for ref in state_refs)
        state = flash(score, values(h), state, factor, live)
        for ref, value in zip(state_refs, state):
            ref[a, h] = value


def own_kernel(group, factor, half, q_ref, own_ref, meta_ref, *refs):
    heads_kv, rows, head_dim = q_ref.shape[1:]
    state_refs = refs[:2]
    run_rows = 2 * heads_kv * RUN

    ids = own_ref[2 * run_rows :].astype(jnp.float32)
    lane = lax.broadcasted_iota(jnp.int32, ids.shape, 1)
    numbers = [jnp.max(jnp.where(lane // RUN == a, ids, 0.0)) for a in range(2)]
    row = lax.broadcasted_iota(jnp.int32, meta_ref.shape, 0)
    meta_ref[...] = jnp.where(
        row == 0, numbers[0], jnp.where(row == 1, numbers[1], 0.0)
    )

    row_at = lax.broadcasted_iota(jnp.int32, (rows, 2 * RUN), 0) // group
    key_at = lax.broadcasted_iota(jnp.int32, (rows, 2 * RUN), 1)
    for a in range(2):
        mine, other = numbers[a], numbers[1 - a]
        seen = (other < mine) & ((other >= half) == (mine >= half))
        reach = jnp.where(seen, RUN, 0)
        if a == 0:
            live = (key_at <= row_at) | ((key_at >= RUN) & (key_at < RUN + reach))
        else:
            live = (key_at < reach) | ((key_at >= RUN) & (key_at - RUN <= row_at))

        def own(g):
            starts = [g * RUN, run_rows + g * RUN]
            return jnp.concatenate([own_ref[n : n + RUN] for n in starts])

        head_tile(q_ref, state_refs, a, own, lambda h: own(heads_kv + h), factor, live)


def attend_kernel(group, factor, half, last, keep, blocks, q_ref, *refs):
    heads_kv, rows, head_dim = q_ref.shape[1:]
    run_rows = 2 * heads_kv * RUN
    block_rows = 2 * run_rows + 16
    kv_refs, refs = refs[: len(blocks)], refs[len(blocks) :]
    refs = refs[4:]
    if last:
        out_ref, refs = refs[0], refs[1:]
    meta_ref, *state_refs, buf = refs[:4]

    meta = meta_ref[...]
    counts = tuple(
        jnp.max(meta[2 + a : 3 + a]).astype(jnp.int32) for a in range(2)
    )
    seen_bits = []
    for ref, (skip, end) in zip(kv_refs, blocks):
        assert end - skip <= 8
        ids = jnp.concatenate(
            [ref[n * block_rows - 16 : n * block_rows] for n in range(skip + 1, end + 1)]
        ).astype(jnp.float32)
        row = lax.broadcasted_iota(jnp.int32, ids.shape, 0)
        lane = lax.broadcasted_iota(jnp.int32, ids.shape, 1)
        bit = jnp.left_shift(1, 2 * (row // 16) + lane // RUN)
        bit = jnp.where((row % 16 == 0) & (lane % RUN == 0), bit, 0).astype(jnp.float32)
        found = []
        for a in range(2):
            mine = meta[a : a + 1]
            low = jnp.where(mine >= half, float(half), 0.0)
            seen = (ids < mine) & (ids >= low)
            found.append(jnp.sum(jnp.where(seen, bit, 0.0)).astype(jnp.int32))
        seen_bits.append(found)

    for ref, (skip, end), bits in zip(kv_refs, blocks, seen_bits):

        def gather(n, counts):
            at = pl.multiple_of((skip + n // 2) * block_rows + n % 2 * run_rows, 16)
            fresh = []
            for a in range(2):
                flag = (bits[a] >> n) & 1
                count = counts[a]

                @pl.when(flag == 1)
                def _():
                    buf[a, count] = ref[pl.ds(at, run_rows), :]

                fresh.append(count + flag)
            return tuple(fresh)

        counts = lax.fori_loop(0, 2 * (end - skip), gather, counts)

    def some_runs(a, start, runs):
        def rows_of(g):
            found = buf[a, pl.ds(start, runs), g * RUN : (g + 1) * RUN, :]
            return found.reshape(runs * RUN, -1)

        def keys(h):
            if runs > 1:
                return rows_of(h)
            return jnp.concatenate([rows_of(h), jnp.zeros((RUN, head_dim), buf.dtype)])

        live = RUN if runs == 1 else None
        head_tile(
            q_ref, state_refs, a, keys, lambda h: rows_of(heads_kv + h), factor, live
        )

    whole = [count // TILE for count in counts]

    def step(item, carry):
        a = (item >= whole[0]).astype(jnp.int32)
        some_runs(a, (item - a * whole[0]) * TILE, TILE)
        return carry

    lax.fori_loop(0, whole[0] + whole[1], step, 0)

    def remainder(a, carry):
        count = jnp.where(a == 0, counts[0], counts[1])
        start = count // TILE * TILE
        runs = TILE // 2
        while runs >= keep:

            @pl.when(count & runs != 0)
            def _():
                some_runs(a, start, runs)

            start = start + (count & runs)
            runs //= 2
        return carry

    lax.fori_loop(0, 2, remainder, 0)

    if not last:
        row = lax.broadcasted_iota(jnp.int32, meta.shape, 0)
        for a in range(2):
            start = counts[a] // keep * keep
            rest = counts[a] - start
            if keep > 1:

                @pl.when((start > 0) & (rest > 0))
                def _():
                    for n in range(keep - 1):
                        buf[a, n] = buf[a, start + n]

            meta = jnp.where(row == 2 + a, rest.astype(jnp.float32), meta)
        meta_ref[...] = meta
        return

    made, sems = refs[4:]
    copies = []
    for a in range(2):
        for h in range(0, heads_kv, 2):
            done = []
            for g in (h, h + 1):
                mixed = state_refs[1][a, g]
                part = mixed[:, :head_dim] * (1.0 / mixed[:, head_dim:])
                done.append(part.reshape(RUN, group, -1))
            place = (slice(a * RUN, (a + 1) * RUN), slice(h * group, (h + 2) * group))
            made[place] = jnp.concatenate(done, axis=1).astype(out_ref.dtype)
            copy = pltpu.make_async_copy(
                made.at[place], out_ref.at[place], sems.at[len(copies)]
            )
            copy.start()
            copies.append(copy)
    for copy in copies:
        copy.wait()


def pack_kernel(k_any, v_any, positions_any, own_ref, k_ref, v_ref, positions_ref, sems):
    pairs = ((k_any, k_ref), (v_any, v_ref), (positions_any, positions_ref))
    copies = [
        pltpu.make_async_copy(source, target, sems.at[n])
        for n, (source, target) in enumerate(pairs)
    ]
    for copy in copies:
        copy.start()
    heads_kv = k_ref.shape[0] // (2 * RUN)
    rows = heads_kv * RUN
    at = lax.broadcasted_iota(jnp.int32, (rows, rows), 0)
    origin = lax.broadcasted_iota(jnp.int32, (rows, rows), 1)
    move = at % RUN * heads_kv + at // RUN == origin
    move = jnp.where(move, 1.0, 0.0).astype(k_ref.dtype)
    for n, ref in enumerate((k_ref, v_ref)):
        copies[n].wait()
        for r in range(2):
            moved = jnp.dot(
                move,
                ref[r * rows : (r + 1) * rows],
                preferred_element_type=jnp.float32,
            )
            start = (2 * r + n) * rows
            own_ref[start : start + rows] = moved.astype(own_ref.dtype)
    copies[2].wait()
    numbers = (positions_ref[...] // RUN).astype(jnp.float32)
    numbers = jnp.broadcast_to(numbers, (16, numbers.shape[1]))
    own_ref[4 * rows :] = numbers.astype(own_ref.dtype)


class Attention:
    def __init__(self, q, group, half, room):
        self.q, self.group, self.half = q, group, half
        self.factor = math.log2(math.e) / math.sqrt(q.shape[3])
        heads_kv, rows, head_dim = q.shape[1:]
        self.block_rows = 4 * heads_kv * RUN + 16
        slots = 2 * room + TILE
        self.carried = [jax.ShapeDtypeStruct((8, 128), jnp.float32)]
        self.carried += [
            jax.ShapeDtypeStruct((2, heads_kv, rows, n), jnp.float32)
            for n in (128, head_dim + 128)
        ]
        self.carried.append(
            jax.ShapeDtypeStruct((2, slots, 2 * heads_kv * RUN, head_dim), q.dtype)
        )

    def call(self, kernel, operands, shapes, aliases, count, name, out=None):
        vmem = pl.BlockSpec(memory_space=pltpu.VMEM)
        out_specs = [vmem] * len(shapes)
        scratch = []
        if out is not None:
            shapes = [out, *shapes]
            out_specs.insert(0, pl.BlockSpec(memory_space=pl.ANY))
            scratch = [pltpu.VMEM(out.shape, out.dtype), pltpu.SemaphoreType.DMA((8,))]
        return pl.pallas_call(
            kernel,
            out_shape=shapes,
            in_specs=[vmem] * len(operands),
            out_specs=out_specs,
            scratch_shapes=scratch,
            input_output_aliases=aliases,
            compiler_params=pltpu.CompilerParams(vmem_limit_bytes=28 * 1024 * 1024),
            cost_estimate=pl.CostEstimate(
                flops=count * RUN * self.q.size * 4,
                bytes_accessed=self.q.size * 8,
                transcendentals=0,
            ),
            name=name,
        )(*operands)

    def start(self, own):
        kernel = functools.partial(own_kernel, self.group, self.factor, self.half)
        return self.call(kernel, [self.q, own], self.carried, {}, 2, "attend_own")

    def add(self, state, kvs, keep=KEEP, out=None):
        kvs = [x if isinstance(x, tuple) else (x, 0) for x in kvs]
        blocks = [(skip, x.shape[0] // self.block_rows) for x, skip in kvs]
        count = sum(end - skip for skip, end in blocks)
        operands = [self.q, *(x for x, _ in kvs), *state]
        first, ahead = 1 + len(kvs), int(out is not None)
        aliases = {first + n: ahead + n for n in range(len(state))}
        kernel = functools.partial(
            attend_kernel, self.group, self.factor, self.half, ahead, keep, blocks
        )
        results = self.call(kernel, operands, self.carried, aliases, count, "attend", out)
        return results[0] if ahead else results


def per_device(queries, keys, values, positions):
    outer, inner = lax.axis_size("outer"), lax.axis_size("inner")
    tokens, heads_q, head_dim = queries.shape
    heads_kv = keys.shape[1]
    group = heads_q // heads_kv
    half = tokens // RUN * outer * inner // 2

    chips = outer // 2
    bits = inner.bit_length() - 1
    ring = [0] + list(range(1, chips, 2)) + list(range(2, chips, 2))[::-1]
    after = {ring[n]: ring[(n + 1) % chips] for n in range(chips)}

    def permute(x, to):
        pairs = []
        for z in range(chips):
            for core in range(2):
                for place in range(inner):
                    nz, ncore, nplace = to(z, core, place)
                    pairs.append(
                        (
                            (2 * z + core) * inner + place,
                            (2 * nz + ncore) * inner + nplace,
                        )
                    )
        return lax.ppermute(x, AXES, pairs)

    def along_z(x):
        return permute(x, lambda z, core, place: (after[z], core, place))

    def over_place(x, step):
        def to(z, core, place):
            return z, core, place ^ (1 << (bits - 1 - step if core else step))

        return permute(x, to)

    def other_core(x):
        return permute(x, lambda z, core, place: (z, 1 - core, place))

    def tied(x, *others):
        return lax.optimization_barrier((x, *others))[0]

    flat = jax.ShapeDtypeStruct((tokens * heads_kv, head_dim), keys.dtype)
    own = pl.pallas_call(
        pack_kernel,
        out_shape=jax.ShapeDtypeStruct(
            (2 * tokens * heads_kv + 16, head_dim), keys.dtype
        ),
        in_specs=[pl.BlockSpec(memory_space=pltpu.HBM)] * 3,
        out_specs=pl.BlockSpec(memory_space=pltpu.VMEM),
        scratch_shapes=[
            pltpu.VMEM(flat.shape, flat.dtype),
            pltpu.VMEM(flat.shape, flat.dtype),
            pltpu.VMEM((1, tokens), jnp.int32),
            pltpu.SemaphoreType.DMA((3,)),
        ],
        compiler_params=pltpu.CompilerParams(vmem_limit_bytes=60 * 1024 * 1024),
        name="pack",
    )(keys.reshape(flat.shape), values.reshape(flat.shape), positions.reshape(1, tokens))
    q = (
        queries.reshape(2, RUN, heads_kv, group, head_dim)
        .transpose(0, 2, 1, 3, 4)
        .reshape(2, heads_kv, RUN * group, head_dim)
    )

    attention = Attention(q, group, half, 2 * inner)
    state = attention.start(own)

    stage, waiting = own, None
    for n in range(chips - 1):
        following = along_z(stage)
        held = stage
        for step in range(bits):
            if n == 0 and step + 1 == bits:
                held = tied(held, state[0])
            held = jnp.concatenate([held, over_place(held, step)])
        if waiting:
            state = attention.add(state, waiting)
            held = tied(held, state[0])
        waiting = [(held, int(n == 0)), other_core(held)]
        stage = following

    found = [stage]
    for step in range(bits):
        found += [over_place(x, step) for x in found]
    *most, final = found
    most = jnp.concatenate(most)
    theirs = other_core(most)
    state = attention.add(state, waiting)
    state = attention.add(state, [most, theirs])
    final = tied(final, state[0])
    theirs = other_core(final)
    state = attention.add(state, [final], keep=1)
    out = jax.ShapeDtypeStruct(queries.shape, queries.dtype)
    return attention.add(state, [theirs], keep=1, out=out)


def solution(mesh):
    in_specs = (
        P(("outer", "inner"), None, None),
        P(("outer", "inner"), None, None),
        P(("outer", "inner"), None, None),
        P(("outer", "inner")),
    )
    out_specs = P(("outer", "inner"), None, None)
    return jax.shard_map(
        per_device, mesh=mesh, in_specs=in_specs, out_specs=out_specs, check_vma=False
    )
```

```python
import functools
import math

import jax
import jax.numpy as jnp
from jax import lax
from jax.experimental import pallas as pl
from jax.experimental.pallas import tpu as pltpu
from jax.sharding import PartitionSpec as P

RUN = 64
TILE = 8
KEEP = 4
AXES = ("outer", "inner")


def flash(score, v, state, factor, live=None):
    top, mixed = state
    keys = score.shape[1]
    if isinstance(live, int):
        lane = lax.broadcasted_iota(jnp.int32, score.shape, 1)
        keys, live = live, lane < live
    if live is not None:
        score = jnp.where(live, score, -jnp.inf)
    parts = [score[:, c : c + 128] for c in range(0, score.shape[1], 128)]
    new = jnp.max(functools.reduce(jnp.maximum, parts), axis=1, keepdims=True)
    if top is None:
        new = jnp.broadcast_to(new, parts[0].shape)
    else:
        new = jnp.maximum(top, new)
    weights = [
        jnp.exp2((part - new) * factor).astype(jnp.bfloat16) for part in parts
    ]
    weights = jnp.concatenate(weights, axis=1)
    ones = jnp.ones((keys, 128), v.dtype)
    part_mixed = jnp.dot(
        weights[:, :keys],
        jnp.concatenate([v, ones], axis=1),
        preferred_element_type=jnp.float32,
    )
    if top is None:
        return new, part_mixed
    decay = jnp.exp2((top - new) * factor)
    halves = [
        mixed[:, c : c + 128] * decay + part_mixed[:, c : c + 128]
        for c in range(0, mixed.shape[1], 128)
    ]
    return new, jnp.concatenate(halves, axis=1)


def head_tile(q_ref, state_refs, a, keys, values, factor, live=None):
    def scores(h):
        return lax.dot_general(
            q_ref[a, h],
            keys(h),
            (((1,), (1,)), ((), ())),
            preferred_element_type=jnp.float32,
        )

    heads_kv = q_ref.shape[1]
    ahead = scores(0)
    for h in range(heads_kv):
        score = ahead
        if h + 1 < heads_kv:
            ahead = scores(h + 1)
        state = (None, None)
        if live is None or isinstance(live, int):
            state = tuple(ref[a, h] for ref in state_refs)
        state = flash(score, values(h), state, factor, live)
        for ref, value in zip(state_refs, state):
            ref[a, h] = value


def own_kernel(group, factor, half, q_ref, own_ref, meta_ref, *refs):
    heads_kv, rows, head_dim = q_ref.shape[1:]
    state_refs = refs[:2]
    run_rows = 2 * heads_kv * RUN

    ids = own_ref[2 * run_rows :].astype(jnp.float32)
    lane = lax.broadcasted_iota(jnp.int32, ids.shape, 1)
    numbers = [jnp.max(jnp.where(lane // RUN == a, ids, 0.0)) for a in range(2)]
    row = lax.broadcasted_iota(jnp.int32, meta_ref.shape, 0)
    meta_ref[...] = jnp.where(
        row == 0, numbers[0], jnp.where(row == 1, numbers[1], 0.0)
    )

    row_at = lax.broadcasted_iota(jnp.int32, (rows, 2 * RUN), 0) // group
    key_at = lax.broadcasted_iota(jnp.int32, (rows, 2 * RUN), 1)
    for a in range(2):
        mine, other = numbers[a], numbers[1 - a]
        seen = (other < mine) & ((other >= half) == (mine >= half))
        reach = jnp.where(seen, RUN, 0)
        if a == 0:
            live = (key_at <= row_at) | ((key_at >= RUN) & (key_at < RUN + reach))
        else:
            live = (key_at < reach) | ((key_at >= RUN) & (key_at - RUN <= row_at))

        def own(g):
            starts = [g * RUN, run_rows + g * RUN]
            return jnp.concatenate([own_ref[n : n + RUN] for n in starts])

        head_tile(q_ref, state_refs, a, own, lambda h: own(heads_kv + h), factor, live)


def attend_kernel(group, factor, half, last, keep, blocks, q_ref, *refs):
    heads_kv, rows, head_dim = q_ref.shape[1:]
    run_rows = 2 * heads_kv * RUN
    block_rows = 2 * run_rows + 16
    kv_refs, refs = refs[: len(blocks)], refs[len(blocks) :]
    refs = refs[4:]
    if last:
        out_ref, refs = refs[0], refs[1:]
    meta_ref, *state_refs, buf = refs[:4]

    meta = meta_ref[...]
    counts = tuple(
        jnp.max(meta[2 + a : 3 + a]).astype(jnp.int32) for a in range(2)
    )
    seen_bits = []
    for ref, (skip, end) in zip(kv_refs, blocks):
        assert end - skip <= 8
        ids = jnp.concatenate(
            [ref[n * block_rows - 16 : n * block_rows] for n in range(skip + 1, end + 1)]
        ).astype(jnp.float32)
        row = lax.broadcasted_iota(jnp.int32, ids.shape, 0)
        lane = lax.broadcasted_iota(jnp.int32, ids.shape, 1)
        bit = jnp.left_shift(1, 2 * (row // 16) + lane // RUN)
        bit = jnp.where((row % 16 == 0) & (lane % RUN == 0), bit, 0).astype(jnp.float32)
        found = []
        for a in range(2):
            mine = meta[a : a + 1]
            low = jnp.where(mine >= half, float(half), 0.0)
            seen = (ids < mine) & (ids >= low)
            found.append(jnp.sum(jnp.where(seen, bit, 0.0)).astype(jnp.int32))
        seen_bits.append(found)

    for ref, (skip, end), bits in zip(kv_refs, blocks, seen_bits):

        def gather(n, counts):
            at = pl.multiple_of((skip + n // 2) * block_rows + n % 2 * run_rows, 16)
            fresh = []
            for a in range(2):
                flag = (bits[a] >> n) & 1
                count = counts[a]

                @pl.when(flag == 1)
                def _():
                    buf[a, count] = ref[pl.ds(at, run_rows), :]

                fresh.append(count + flag)
            return tuple(fresh)

        counts = lax.fori_loop(0, 2 * (end - skip), gather, counts)

    def some_runs(a, start, runs):
        def rows_of(g):
            found = buf[a, pl.ds(start, runs), g * RUN : (g + 1) * RUN, :]
            return found.reshape(runs * RUN, -1)

        def keys(h):
            if runs > 1:
                return rows_of(h)
            return jnp.concatenate([rows_of(h), jnp.zeros((RUN, head_dim), buf.dtype)])

        live = RUN if runs == 1 else None
        head_tile(
            q_ref, state_refs, a, keys, lambda h: rows_of(heads_kv + h), factor, live
        )

    whole = [count // TILE for count in counts]

    def step(item, carry):
        a = (item >= whole[0]).astype(jnp.int32)
        some_runs(a, (item - a * whole[0]) * TILE, TILE)
        return carry

    lax.fori_loop(0, whole[0] + whole[1], step, 0)

    def remainder(a, carry):
        count = jnp.where(a == 0, counts[0], counts[1])
        start = count // TILE * TILE
        runs = TILE // 2
        while runs >= keep:

            @pl.when(count & runs != 0)
            def _():
                some_runs(a, start, runs)

            start = start + (count & runs)
            runs //= 2
        return carry

    lax.fori_loop(0, 2, remainder, 0)

    if not last:
        row = lax.broadcasted_iota(jnp.int32, meta.shape, 0)
        for a in range(2):
            start = counts[a] // keep * keep
            rest = counts[a] - start
            if keep > 1:

                @pl.when((start > 0) & (rest > 0))
                def _():
                    for n in range(keep - 1):
                        buf[a, n] = buf[a, start + n]

            meta = jnp.where(row == 2 + a, rest.astype(jnp.float32), meta)
        meta_ref[...] = meta
        return

    made, sems = refs[4:]
    copies = []
    for a in range(2):
        for h in range(0, heads_kv, 2):
            done = []
            for g in (h, h + 1):
                mixed = state_refs[1][a, g]
                part = mixed[:, :head_dim] * (1.0 / mixed[:, head_dim:])
                done.append(part.reshape(RUN, group, -1))
            place = (slice(a * RUN, (a + 1) * RUN), slice(h * group, (h + 2) * group))
            made[place] = jnp.concatenate(done, axis=1).astype(out_ref.dtype)
            copy = pltpu.make_async_copy(
                made.at[place], out_ref.at[place], sems.at[len(copies)]
            )
            copy.start()
            copies.append(copy)
    for copy in copies:
        copy.wait()


def pack_kernel(k_any, v_any, positions_any, own_ref, k_ref, v_ref, positions_ref, sems):
    pairs = ((k_any, k_ref), (v_any, v_ref), (positions_any, positions_ref))
    copies = [
        pltpu.make_async_copy(source, target, sems.at[n])
        for n, (source, target) in enumerate(pairs)
    ]
    for copy in copies:
        copy.start()
    heads_kv = k_ref.shape[0] // (2 * RUN)
    rows = heads_kv * RUN
    at = lax.broadcasted_iota(jnp.int32, (rows, rows), 0)
    origin = lax.broadcasted_iota(jnp.int32, (rows, rows), 1)
    move = at % RUN * heads_kv + at // RUN == origin
    move = jnp.where(move, 1.0, 0.0).astype(k_ref.dtype)
    for n, ref in enumerate((k_ref, v_ref)):
        copies[n].wait()
        for r in range(2):
            moved = jnp.dot(
                move,
                ref[r * rows : (r + 1) * rows],
                preferred_element_type=jnp.float32,
            )
            start = (2 * r + n) * rows
            own_ref[start : start + rows] = moved.astype(own_ref.dtype)
    copies[2].wait()
    numbers = (positions_ref[...] // RUN).astype(jnp.float32)
    numbers = jnp.broadcast_to(numbers, (16, numbers.shape[1]))
    own_ref[4 * rows :] = numbers.astype(own_ref.dtype)


class Attention:
    def __init__(self, q, group, half, room):
        self.q, self.group, self.half = q, group, half
        self.factor = math.log2(math.e) / math.sqrt(q.shape[3])
        heads_kv, rows, head_dim = q.shape[1:]
        self.block_rows = 4 * heads_kv * RUN + 16
        slots = 2 * room + TILE
        self.carried = [jax.ShapeDtypeStruct((8, 128), jnp.float32)]
        self.carried += [
            jax.ShapeDtypeStruct((2, heads_kv, rows, n), jnp.float32)
            for n in (128, head_dim + 128)
        ]
        self.carried.append(
            jax.ShapeDtypeStruct((2, slots, 2 * heads_kv * RUN, head_dim), q.dtype)
        )

    def call(self, kernel, operands, shapes, aliases, count, name, out=None):
        vmem = pl.BlockSpec(memory_space=pltpu.VMEM)
        out_specs = [vmem] * len(shapes)
        scratch = []
        if out is not None:
            shapes = [out, *shapes]
            out_specs.insert(0, pl.BlockSpec(memory_space=pl.ANY))
            scratch = [pltpu.VMEM(out.shape, out.dtype), pltpu.SemaphoreType.DMA((8,))]
        return pl.pallas_call(
            kernel,
            out_shape=shapes,
            in_specs=[vmem] * len(operands),
            out_specs=out_specs,
            scratch_shapes=scratch,
            input_output_aliases=aliases,
            compiler_params=pltpu.CompilerParams(vmem_limit_bytes=28 * 1024 * 1024),
            cost_estimate=pl.CostEstimate(
                flops=count * RUN * self.q.size * 4,
                bytes_accessed=self.q.size * 8,
                transcendentals=0,
            ),
            name=name,
        )(*operands)

    def start(self, own):
        kernel = functools.partial(own_kernel, self.group, self.factor, self.half)
        return self.call(kernel, [self.q, own], self.carried, {}, 2, "attend_own")

    def add(self, state, kvs, keep=KEEP, out=None):
        kvs = [x if isinstance(x, tuple) else (x, 0) for x in kvs]
        blocks = [(skip, x.shape[0] // self.block_rows) for x, skip in kvs]
        count = sum(end - skip for skip, end in blocks)
        operands = [self.q, *(x for x, _ in kvs), *state]
        first, ahead = 1 + len(kvs), int(out is not None)
        aliases = {first + n: ahead + n for n in range(len(state))}
        kernel = functools.partial(
            attend_kernel, self.group, self.factor, self.half, ahead, keep, blocks
        )
        results = self.call(kernel, operands, self.carried, aliases, count, "attend", out)
        return results[0] if ahead else results


def per_device(queries, keys, values, positions):
    outer, inner = lax.axis_size("outer"), lax.axis_size("inner")
    tokens, heads_q, head_dim = queries.shape
    heads_kv = keys.shape[1]
    group = heads_q // heads_kv
    half = tokens // RUN * outer * inner // 2

    chips = outer // 2
    bits = inner.bit_length() - 1
    ring = [0] + list(range(1, chips, 2)) + list(range(2, chips, 2))[::-1]
    after = {ring[n]: ring[(n + 1) % chips] for n in range(chips)}

    def permute(x, to):
        pairs = []
        for z in range(chips):
            for core in range(2):
                for place in range(inner):
                    nz, ncore, nplace = to(z, core, place)
                    pairs.append(
                        (
                            (2 * z + core) * inner + place,
                            (2 * nz + ncore) * inner + nplace,
                        )
                    )
        return lax.ppermute(x, AXES, pairs)

    def along_z(x):
        return permute(x, lambda z, core, place: (after[z], core, place))

    def over_place(x, step):
        def to(z, core, place):
            return z, core, place ^ (1 << (bits - 1 - step if core else step))

        return permute(x, to)

    def other_core(x):
        return permute(x, lambda z, core, place: (z, 1 - core, place))

    def tied(x, *others):
        return lax.optimization_barrier((x, *others))[0]

    flat = jax.ShapeDtypeStruct((tokens * heads_kv, head_dim), keys.dtype)
    own = pl.pallas_call(
        pack_kernel,
        out_shape=jax.ShapeDtypeStruct(
            (2 * tokens * heads_kv + 16, head_dim), keys.dtype
        ),
        in_specs=[pl.BlockSpec(memory_space=pltpu.HBM)] * 3,
        out_specs=pl.BlockSpec(memory_space=pltpu.VMEM),
        scratch_shapes=[
            pltpu.VMEM(flat.shape, flat.dtype),
            pltpu.VMEM(flat.shape, flat.dtype),
            pltpu.VMEM((1, tokens), jnp.int32),
            pltpu.SemaphoreType.DMA((3,)),
        ],
        compiler_params=pltpu.CompilerParams(vmem_limit_bytes=60 * 1024 * 1024),
        name="pack",
    )(keys.reshape(flat.shape), values.reshape(flat.shape), positions.reshape(1, tokens))
    q = (
        queries.reshape(2, RUN, heads_kv, group, head_dim)
        .transpose(0, 2, 1, 3, 4)
        .reshape(2, heads_kv, RUN * group, head_dim)
    )

    attention = Attention(q, group, half, 2 * inner)
    state = attention.start(own)

    stage = own
    halves, theirs = [], []
    for n in range(chips - 1):
        following = along_z(stage)
        held = stage
        for step in range(bits):
            if n == 0 and step + 1 == bits:
                first = held
                held = tied(held, state[0])
            there = over_place(held, step)
            if n and step == 0:
                if n == 1:
                    kvs = [(halves[0][0], 1), theirs[0][0]]
                else:
                    kvs = [halves[n - 2][1], halves[n - 1][0], theirs[n - 2][-1]]
                state = attention.add(state, kvs)
                there = tied(there, state[0])
            if step + 1 < bits:
                held = jnp.concatenate([held, there])
        halves.append((held, there))
        if n == 0:
            theirs.append([other_core(tied(first, following)), other_core(there)])
            stage = following
            continue
        held = jnp.concatenate([held, there])
        if n + 2 == chips:
            state = attention.add(state, [halves[n - 1][1], theirs[n - 1][-1], halves[n][0]])
            held = tied(held, state[0])
        theirs.append([other_core(held)])
        stage = following

    found = [stage]
    for step in range(bits):
        found += [over_place(x, step) for x in found]
    *most, final = found
    most = jnp.concatenate(most)
    their_most = other_core(most)
    state = attention.add(state, [halves[-1][1], theirs[-1][-1]])
    state = attention.add(state, [most, their_most])
    final = tied(final, state[0])
    theirs = other_core(final)
    state = attention.add(state, [final], keep=1)
    out = jax.ShapeDtypeStruct(queries.shape, queries.dtype)
    return attention.add(state, [theirs], keep=1, out=out)


def solution(mesh):
    in_specs = (
        P(("outer", "inner"), None, None),
        P(("outer", "inner"), None, None),
        P(("outer", "inner"), None, None),
        P(("outer", "inner")),
    )
    out_specs = P(("outer", "inner"), None, None)
    return jax.shard_map(
        per_device, mesh=mesh, in_specs=in_specs, out_specs=out_specs, check_vma=False
    )
```

```python
import functools
import math

import jax
import jax.numpy as jnp
from jax import lax
from jax.experimental import pallas as pl
from jax.experimental.pallas import tpu as pltpu
from jax.sharding import PartitionSpec as P

RUN = 64
TILE = 8
KEEP = 4
AXES = ("outer", "inner")


def flash(score, v, state, factor, live=None):
    top, mixed = state
    keys = score.shape[1]
    if isinstance(live, int):
        lane = lax.broadcasted_iota(jnp.int32, score.shape, 1)
        keys, live = live, lane < live
    if live is not None:
        score = jnp.where(live, score, -jnp.inf)
    parts = [score[:, c : c + 128] for c in range(0, score.shape[1], 128)]
    new = jnp.max(functools.reduce(jnp.maximum, parts), axis=1, keepdims=True)
    if top is None:
        new = jnp.broadcast_to(new, parts[0].shape)
    else:
        new = jnp.maximum(top, new)
    weights = [
        jnp.exp2((part - new) * factor).astype(jnp.bfloat16) for part in parts
    ]
    weights = jnp.concatenate(weights, axis=1)
    ones = jnp.ones((keys, 128), v.dtype)
    part_mixed = jnp.dot(
        weights[:, :keys],
        jnp.concatenate([v, ones], axis=1),
        preferred_element_type=jnp.float32,
    )
    if top is None:
        return new, part_mixed
    decay = jnp.exp2((top - new) * factor)
    halves = [
        mixed[:, c : c + 128] * decay + part_mixed[:, c : c + 128]
        for c in range(0, mixed.shape[1], 128)
    ]
    return new, jnp.concatenate(halves, axis=1)


def head_tile(q_ref, state_refs, a, keys, values, factor, live=None):
    def scores(h):
        return lax.dot_general(
            q_ref[a, h],
            keys(h),
            (((1,), (1,)), ((), ())),
            preferred_element_type=jnp.float32,
        )

    heads_kv = q_ref.shape[1]
    ahead = scores(0)
    for h in range(heads_kv):
        score = ahead
        if h + 1 < heads_kv:
            ahead = scores(h + 1)
        state = (None, None)
        if live is None or isinstance(live, int):
            state = tuple(ref[a, h] for ref in state_refs)
        state = flash(score, values(h), state, factor, live)
        for ref, value in zip(state_refs, state):
            ref[a, h] = value


def own_kernel(group, factor, half, q_ref, own_ref, meta_ref, *refs):
    heads_kv, rows, head_dim = q_ref.shape[1:]
    state_refs = refs[:2]
    run_rows = 2 * heads_kv * RUN

    ids = own_ref[2 * run_rows :].astype(jnp.float32)
    lane = lax.broadcasted_iota(jnp.int32, ids.shape, 1)
    numbers = [jnp.max(jnp.where(lane // RUN == a, ids, 0.0)) for a in range(2)]
    row = lax.broadcasted_iota(jnp.int32, meta_ref.shape, 0)
    meta_ref[...] = jnp.where(
        row == 0, numbers[0], jnp.where(row == 1, numbers[1], 0.0)
    )

    row_at = lax.broadcasted_iota(jnp.int32, (rows, 2 * RUN), 0) // group
    key_at = lax.broadcasted_iota(jnp.int32, (rows, 2 * RUN), 1)
    for a in range(2):
        mine, other = numbers[a], numbers[1 - a]
        seen = (other < mine) & ((other >= half) == (mine >= half))
        reach = jnp.where(seen, RUN, 0)
        if a == 0:
            live = (key_at <= row_at) | ((key_at >= RUN) & (key_at < RUN + reach))
        else:
            live = (key_at < reach) | ((key_at >= RUN) & (key_at - RUN <= row_at))

        def own(g):
            starts = [g * RUN, run_rows + g * RUN]
            return jnp.concatenate([own_ref[n : n + RUN] for n in starts])

        head_tile(q_ref, state_refs, a, own, lambda h: own(heads_kv + h), factor, live)


def attend_kernel(group, factor, half, last, keep, blocks, q_ref, *refs):
    heads_kv, rows, head_dim = q_ref.shape[1:]
    run_rows = 2 * heads_kv * RUN
    block_rows = 2 * run_rows + 16
    kv_refs, refs = refs[: len(blocks)], refs[len(blocks) :]
    refs = refs[4:]
    if last:
        out_ref, refs = refs[0], refs[1:]
    meta_ref, *state_refs, buf = refs[:4]

    meta = meta_ref[...]
    counts = tuple(
        jnp.max(meta[2 + a : 3 + a]).astype(jnp.int32) for a in range(2)
    )
    seen_bits = []
    for ref, (skip, end) in zip(kv_refs, blocks):
        assert end - skip <= 8
        ids = jnp.concatenate(
            [ref[n * block_rows - 16 : n * block_rows] for n in range(skip + 1, end + 1)]
        ).astype(jnp.float32)
        row = lax.broadcasted_iota(jnp.int32, ids.shape, 0)
        lane = lax.broadcasted_iota(jnp.int32, ids.shape, 1)
        bit = jnp.left_shift(1, 2 * (row // 16) + lane // RUN)
        bit = jnp.where((row % 16 == 0) & (lane % RUN == 0), bit, 0).astype(jnp.float32)
        found = []
        for a in range(2):
            mine = meta[a : a + 1]
            low = jnp.where(mine >= half, float(half), 0.0)
            seen = (ids < mine) & (ids >= low)
            found.append(jnp.sum(jnp.where(seen, bit, 0.0)).astype(jnp.int32))
        seen_bits.append(found)

    for ref, (skip, end), bits in zip(kv_refs, blocks, seen_bits):

        def gather(n, counts):
            at = pl.multiple_of((skip + n // 2) * block_rows + n % 2 * run_rows, 16)
            fresh = []
            for a in range(2):
                flag = (bits[a] >> n) & 1
                count = counts[a]

                @pl.when(flag == 1)
                def _():
                    buf[a, count] = ref[pl.ds(at, run_rows), :]

                fresh.append(count + flag)
            return tuple(fresh)

        counts = lax.fori_loop(0, 2 * (end - skip), gather, counts)

    def some_runs(a, start, runs):
        def rows_of(g):
            found = buf[a, pl.ds(start, runs), g * RUN : (g + 1) * RUN, :]
            return found.reshape(runs * RUN, -1)

        def keys(h):
            if runs > 1:
                return rows_of(h)
            return jnp.concatenate([rows_of(h), jnp.zeros((RUN, head_dim), buf.dtype)])

        live = RUN if runs == 1 else None
        head_tile(
            q_ref, state_refs, a, keys, lambda h: rows_of(heads_kv + h), factor, live
        )

    whole = [count // TILE for count in counts]

    def step(item, carry):
        a = (item >= whole[0]).astype(jnp.int32)
        some_runs(a, (item - a * whole[0]) * TILE, TILE)
        return carry

    lax.fori_loop(0, whole[0] + whole[1], step, 0)

    def remainder(a, carry):
        count = jnp.where(a == 0, counts[0], counts[1])
        start = count // TILE * TILE
        runs = TILE // 2
        while runs >= keep:

            @pl.when(count & runs != 0)
            def _():
                some_runs(a, start, runs)

            start = start + (count & runs)
            runs //= 2
        return carry

    lax.fori_loop(0, 2, remainder, 0)

    if not last:
        row = lax.broadcasted_iota(jnp.int32, meta.shape, 0)
        for a in range(2):
            start = counts[a] // keep * keep
            rest = counts[a] - start
            if keep > 1:

                @pl.when((start > 0) & (rest > 0))
                def _():
                    for n in range(keep - 1):
                        buf[a, n] = buf[a, start + n]

            meta = jnp.where(row == 2 + a, rest.astype(jnp.float32), meta)
        meta_ref[...] = meta
        return

    made, sems = refs[4:]
    copies = []
    for a in range(2):
        for h in range(0, heads_kv, 2):
            done = []
            for g in (h, h + 1):
                mixed = state_refs[1][a, g]
                part = mixed[:, :head_dim] * (1.0 / mixed[:, head_dim:])
                done.append(part.reshape(RUN, group, -1))
            place = (slice(a * RUN, (a + 1) * RUN), slice(h * group, (h + 2) * group))
            made[place] = jnp.concatenate(done, axis=1).astype(out_ref.dtype)
            copy = pltpu.make_async_copy(
                made.at[place], out_ref.at[place], sems.at[len(copies)]
            )
            copy.start()
            copies.append(copy)
    for copy in copies:
        copy.wait()


def pack_kernel(k_any, v_any, positions_any, own_ref, k_ref, v_ref, positions_ref, sems):
    pairs = ((k_any, k_ref), (v_any, v_ref), (positions_any, positions_ref))
    copies = [
        pltpu.make_async_copy(source, target, sems.at[n])
        for n, (source, target) in enumerate(pairs)
    ]
    for copy in copies:
        copy.start()
    heads_kv = k_ref.shape[0] // (2 * RUN)
    rows = heads_kv * RUN
    at = lax.broadcasted_iota(jnp.int32, (rows, rows), 0)
    origin = lax.broadcasted_iota(jnp.int32, (rows, rows), 1)
    move = at % RUN * heads_kv + at // RUN == origin
    move = jnp.where(move, 1.0, 0.0).astype(k_ref.dtype)
    for n, ref in enumerate((k_ref, v_ref)):
        copies[n].wait()
        for r in range(2):
            moved = jnp.dot(
                move,
                ref[r * rows : (r + 1) * rows],
                preferred_element_type=jnp.float32,
            )
            start = (2 * r + n) * rows
            own_ref[start : start + rows] = moved.astype(own_ref.dtype)
    copies[2].wait()
    numbers = (positions_ref[...] // RUN).astype(jnp.float32)
    numbers = jnp.broadcast_to(numbers, (16, numbers.shape[1]))
    own_ref[4 * rows :] = numbers.astype(own_ref.dtype)


class Attention:
    def __init__(self, q, group, half, room):
        self.q, self.group, self.half = q, group, half
        self.factor = math.log2(math.e) / math.sqrt(q.shape[3])
        heads_kv, rows, head_dim = q.shape[1:]
        self.block_rows = 4 * heads_kv * RUN + 16
        slots = 2 * room + TILE
        self.carried = [jax.ShapeDtypeStruct((8, 128), jnp.float32)]
        self.carried += [
            jax.ShapeDtypeStruct((2, heads_kv, rows, n), jnp.float32)
            for n in (128, head_dim + 128)
        ]
        self.carried.append(
            jax.ShapeDtypeStruct((2, slots, 2 * heads_kv * RUN, head_dim), q.dtype)
        )

    def call(self, kernel, operands, shapes, aliases, count, name, out=None):
        vmem = pl.BlockSpec(memory_space=pltpu.VMEM)
        out_specs = [vmem] * len(shapes)
        scratch = []
        if out is not None:
            shapes = [out, *shapes]
            out_specs.insert(0, pl.BlockSpec(memory_space=pl.ANY))
            scratch = [pltpu.VMEM(out.shape, out.dtype), pltpu.SemaphoreType.DMA((8,))]
        return pl.pallas_call(
            kernel,
            out_shape=shapes,
            in_specs=[vmem] * len(operands),
            out_specs=out_specs,
            scratch_shapes=scratch,
            input_output_aliases=aliases,
            compiler_params=pltpu.CompilerParams(vmem_limit_bytes=28 * 1024 * 1024),
            cost_estimate=pl.CostEstimate(
                flops=count * RUN * self.q.size * 4,
                bytes_accessed=self.q.size * 8,
                transcendentals=0,
            ),
            name=name,
        )(*operands)

    def start(self, own):
        kernel = functools.partial(own_kernel, self.group, self.factor, self.half)
        return self.call(kernel, [self.q, own], self.carried, {}, 2, "attend_own")

    def add(self, state, kvs, keep=KEEP, out=None):
        kvs = [x if isinstance(x, tuple) else (x, 0) for x in kvs]
        blocks = [(skip, x.shape[0] // self.block_rows) for x, skip in kvs]
        count = sum(end - skip for skip, end in blocks)
        operands = [self.q, *(x for x, _ in kvs), *state]
        first, ahead = 1 + len(kvs), int(out is not None)
        aliases = {first + n: ahead + n for n in range(len(state))}
        kernel = functools.partial(
            attend_kernel, self.group, self.factor, self.half, ahead, keep, blocks
        )
        results = self.call(kernel, operands, self.carried, aliases, count, "attend", out)
        return results[0] if ahead else results


def per_device(queries, keys, values, positions):
    outer, inner = lax.axis_size("outer"), lax.axis_size("inner")
    tokens, heads_q, head_dim = queries.shape
    heads_kv = keys.shape[1]
    group = heads_q // heads_kv
    half = tokens // RUN * outer * inner // 2

    chips = outer // 2
    bits = inner.bit_length() - 1
    ring = [0] + list(range(1, chips, 2)) + list(range(2, chips, 2))[::-1]
    after = {ring[n]: ring[(n + 1) % chips] for n in range(chips)}

    def permute(x, to):
        pairs = []
        for z in range(chips):
            for core in range(2):
                for place in range(inner):
                    nz, ncore, nplace = to(z, core, place)
                    pairs.append(
                        (
                            (2 * z + core) * inner + place,
                            (2 * nz + ncore) * inner + nplace,
                        )
                    )
        return lax.ppermute(x, AXES, pairs)

    def along_z(x):
        return permute(x, lambda z, core, place: (after[z], core, place))

    def over_place(x, step, cross=0):
        def to(z, core, place):
            bit = bits - 1 - step if core else step
            return z, core ^ cross, place ^ (1 << bit)

        return permute(x, to)

    def other_core(x):
        return permute(x, lambda z, core, place: (z, 1 - core, place))

    def tied(x, *others):
        return lax.optimization_barrier((x, *others))[0]

    flat = jax.ShapeDtypeStruct((tokens * heads_kv, head_dim), keys.dtype)
    own = pl.pallas_call(
        pack_kernel,
        out_shape=jax.ShapeDtypeStruct(
            (2 * tokens * heads_kv + 16, head_dim), keys.dtype
        ),
        in_specs=[pl.BlockSpec(memory_space=pltpu.HBM)] * 3,
        out_specs=pl.BlockSpec(memory_space=pltpu.VMEM),
        scratch_shapes=[
            pltpu.VMEM(flat.shape, flat.dtype),
            pltpu.VMEM(flat.shape, flat.dtype),
            pltpu.VMEM((1, tokens), jnp.int32),
            pltpu.SemaphoreType.DMA((3,)),
        ],
        compiler_params=pltpu.CompilerParams(vmem_limit_bytes=60 * 1024 * 1024),
        name="pack",
    )(keys.reshape(flat.shape), values.reshape(flat.shape), positions.reshape(1, tokens))
    q = (
        queries.reshape(2, RUN, heads_kv, group, head_dim)
        .transpose(0, 2, 1, 3, 4)
        .reshape(2, heads_kv, RUN * group, head_dim)
    )

    attention = Attention(q, group, half, 2 * inner)
    state = attention.start(own)

    stage = own
    halves, theirs = [], []
    for n in range(chips - 1):
        following = along_z(stage)
        held = stage
        for step in range(bits):
            if n == 0 and step + 1 == bits:
                first = held
                held = tied(held, state[0])
            there = over_place(held, step)
            if n and step == 0:
                if n == 1:
                    kvs = [(halves[0][0], 1), theirs[0][0]]
                else:
                    kvs = [halves[n - 2][1], halves[n - 1][0], theirs[n - 2][-1]]
                state = attention.add(state, kvs)
                there = tied(there, state[0])
            if step + 1 < bits:
                held = jnp.concatenate([held, there])
        halves.append((held, there))
        if n == 0:
            theirs.append([other_core(tied(first, following)), other_core(there)])
            stage = following
            continue
        held = jnp.concatenate([held, there])
        if n + 2 == chips:
            state = attention.add(state, [halves[n - 1][1], theirs[n - 1][-1], halves[n][0]])
            held = tied(held, state[0])
        theirs.append([other_core(held)])
        stage = following

    found = [stage]
    for step in range(bits):
        found += [over_place(x, step) for x in found]
    *most, final = found
    crossed = over_place(found[inner // 2 - 1], bits - 1, cross=1)
    most = jnp.concatenate(most)
    their_most = other_core(most)
    state = attention.add(state, [halves[-1][1], theirs[-1][-1]])
    state = attention.add(state, [most, their_most])
    last = [tied(x, state[0]) for x in (final, crossed)]
    out = jax.ShapeDtypeStruct(queries.shape, queries.dtype)
    return attention.add(state, last, keep=1, out=out)


def solution(mesh):
    in_specs = (
        P(("outer", "inner"), None, None),
        P(("outer", "inner"), None, None),
        P(("outer", "inner"), None, None),
        P(("outer", "inner")),
    )
    out_specs = P(("outer", "inner"), None, None)
    return jax.shard_map(
        per_device, mesh=mesh, in_specs=in_specs, out_specs=out_specs, check_vma=False
    )
```

```python
import functools
import math

import jax
import jax.numpy as jnp
from jax import lax
from jax.experimental import pallas as pl
from jax.experimental.pallas import tpu as pltpu
from jax.sharding import PartitionSpec as P

RUN = 64
TILE = 8
KEEP = 4
AXES = ("outer", "inner")


def flash(score, v, state, factor, live=None):
    top, mixed = state
    keys = score.shape[1]
    if isinstance(live, int):
        lane = lax.broadcasted_iota(jnp.int32, score.shape, 1)
        keys, live = live, lane < live
    if live is not None:
        score = jnp.where(live, score, -jnp.inf)
    parts = [score[:, c : c + 128] for c in range(0, score.shape[1], 128)]
    new = jnp.max(functools.reduce(jnp.maximum, parts), axis=1, keepdims=True)
    if top is None:
        new = jnp.broadcast_to(new, parts[0].shape)
    else:
        new = jnp.maximum(top, new)
    weights = [
        jnp.exp2((part - new) * factor).astype(jnp.bfloat16) for part in parts
    ]
    weights = jnp.concatenate(weights, axis=1)
    ones = jnp.ones((keys, 128), v.dtype)
    part_mixed = jnp.dot(
        weights[:, :keys],
        jnp.concatenate([v, ones], axis=1),
        preferred_element_type=jnp.float32,
    )
    if top is None:
        return new, part_mixed
    decay = jnp.exp2((top - new) * factor)
    halves = [
        mixed[:, c : c + 128] * decay + part_mixed[:, c : c + 128]
        for c in range(0, mixed.shape[1], 128)
    ]
    return new, jnp.concatenate(halves, axis=1)


def head_tile(q_ref, state_refs, a, keys, values, factor, live=None):
    def scores(h):
        return lax.dot_general(
            q_ref[a, h],
            keys(h),
            (((1,), (1,)), ((), ())),
            preferred_element_type=jnp.float32,
        )

    heads_kv = q_ref.shape[1]
    ahead = scores(0)
    for h in range(heads_kv):
        score = ahead
        if h + 1 < heads_kv:
            ahead = scores(h + 1)
        state = (None, None)
        if live is None or isinstance(live, int):
            state = tuple(ref[a, h] for ref in state_refs)
        state = flash(score, values(h), state, factor, live)
        for ref, value in zip(state_refs, state):
            ref[a, h] = value


def own_kernel(group, factor, half, q_ref, own_ref, meta_ref, *refs):
    heads_kv, rows, head_dim = q_ref.shape[1:]
    state_refs = refs[:2]
    run_rows = 2 * heads_kv * RUN

    ids = own_ref[2 * run_rows :].astype(jnp.float32)
    lane = lax.broadcasted_iota(jnp.int32, ids.shape, 1)
    numbers = [jnp.max(jnp.where(lane // RUN == a, ids, 0.0)) for a in range(2)]
    row = lax.broadcasted_iota(jnp.int32, meta_ref.shape, 0)
    meta_ref[...] = jnp.where(
        row == 0, numbers[0], jnp.where(row == 1, numbers[1], 0.0)
    )

    row_at = lax.broadcasted_iota(jnp.int32, (rows, 2 * RUN), 0) // group
    key_at = lax.broadcasted_iota(jnp.int32, (rows, 2 * RUN), 1)
    for a in range(2):
        mine, other = numbers[a], numbers[1 - a]
        seen = (other < mine) & ((other >= half) == (mine >= half))
        reach = jnp.where(seen, RUN, 0)
        if a == 0:
            live = (key_at <= row_at) | ((key_at >= RUN) & (key_at < RUN + reach))
        else:
            live = (key_at < reach) | ((key_at >= RUN) & (key_at - RUN <= row_at))

        def own(g):
            starts = [g * RUN, run_rows + g * RUN]
            return jnp.concatenate([own_ref[n : n + RUN] for n in starts])

        head_tile(q_ref, state_refs, a, own, lambda h: own(heads_kv + h), factor, live)


def attend_kernel(group, factor, half, last, keep, blocks, q_ref, *refs):
    heads_kv, rows, head_dim = q_ref.shape[1:]
    run_rows = 2 * heads_kv * RUN
    block_rows = 2 * run_rows + 16
    kv_refs, refs = refs[: len(blocks)], refs[len(blocks) :]
    refs = refs[4:]
    if last:
        out_ref, refs = refs[0], refs[1:]
    meta_ref, *state_refs, buf = refs[:4]

    meta = meta_ref[...]
    counts = tuple(
        jnp.max(meta[2 + a : 3 + a]).astype(jnp.int32) for a in range(2)
    )
    seen_bits = []
    for ref, (skip, end) in zip(kv_refs, blocks):
        assert end - skip <= 8
        ids = jnp.concatenate(
            [ref[n * block_rows - 16 : n * block_rows] for n in range(skip + 1, end + 1)]
        ).astype(jnp.float32)
        row = lax.broadcasted_iota(jnp.int32, ids.shape, 0)
        lane = lax.broadcasted_iota(jnp.int32, ids.shape, 1)
        bit = jnp.left_shift(1, 2 * (row // 16) + lane // RUN)
        bit = jnp.where((row % 16 == 0) & (lane % RUN == 0), bit, 0).astype(jnp.float32)
        found = []
        for a in range(2):
            mine = meta[a : a + 1]
            low = jnp.where(mine >= half, float(half), 0.0)
            seen = (ids < mine) & (ids >= low)
            found.append(jnp.sum(jnp.where(seen, bit, 0.0)).astype(jnp.int32))
        seen_bits.append(found)

    for ref, (skip, end), bits in zip(kv_refs, blocks, seen_bits):

        def gather(n, counts):
            at = pl.multiple_of((skip + n // 2) * block_rows + n % 2 * run_rows, 16)
            fresh = []
            for a in range(2):
                flag = (bits[a] >> n) & 1
                count = counts[a]

                @pl.when(flag == 1)
                def _():
                    buf[a, count] = ref[pl.ds(at, run_rows), :]

                fresh.append(count + flag)
            return tuple(fresh)

        counts = lax.fori_loop(0, 2 * (end - skip), gather, counts)

    def some_runs(a, start, runs):
        def rows_of(g):
            found = buf[a, pl.ds(start, runs), g * RUN : (g + 1) * RUN, :]
            return found.reshape(runs * RUN, -1)

        def keys(h):
            if runs > 1:
                return rows_of(h)
            return jnp.concatenate([rows_of(h), jnp.zeros((RUN, head_dim), buf.dtype)])

        live = RUN if runs == 1 else None
        head_tile(
            q_ref, state_refs, a, keys, lambda h: rows_of(heads_kv + h), factor, live
        )

    whole = [count // TILE for count in counts]

    def step(item, carry):
        a = (item >= whole[0]).astype(jnp.int32)
        some_runs(a, (item - a * whole[0]) * TILE, TILE)
        return carry

    lax.fori_loop(0, whole[0] + whole[1], step, 0)

    def remainder(a, carry):
        count = jnp.where(a == 0, counts[0], counts[1])
        start = count // TILE * TILE
        runs = TILE // 2
        while runs >= keep:

            @pl.when(count & runs != 0)
            def _():
                some_runs(a, start, runs)

            start = start + (count & runs)
            runs //= 2
        return carry

    lax.fori_loop(0, 2, remainder, 0)

    if not last:
        row = lax.broadcasted_iota(jnp.int32, meta.shape, 0)
        for a in range(2):
            start = counts[a] // keep * keep
            rest = counts[a] - start
            if keep > 1:

                @pl.when((start > 0) & (rest > 0))
                def _():
                    for n in range(keep - 1):
                        buf[a, n] = buf[a, start + n]

            meta = jnp.where(row == 2 + a, rest.astype(jnp.float32), meta)
        meta_ref[...] = meta
        return

    made, sems = refs[4:]
    copies = []
    for a in range(2):
        for h in range(0, heads_kv, 2):
            done = []
            for g in (h, h + 1):
                mixed = state_refs[1][a, g]
                part = mixed[:, :head_dim] * (1.0 / mixed[:, head_dim:])
                done.append(part.reshape(RUN, group, -1))
            place = (slice(a * RUN, (a + 1) * RUN), slice(h * group, (h + 2) * group))
            made[place] = jnp.concatenate(done, axis=1).astype(out_ref.dtype)
            copy = pltpu.make_async_copy(
                made.at[place], out_ref.at[place], sems.at[len(copies)]
            )
            copy.start()
            copies.append(copy)
    for copy in copies:
        copy.wait()


def pack_kernel(k_any, v_any, positions_any, own_ref, k_ref, v_ref, positions_ref, sems):
    pairs = ((k_any, k_ref), (v_any, v_ref), (positions_any, positions_ref))
    copies = [
        pltpu.make_async_copy(source, target, sems.at[n])
        for n, (source, target) in enumerate(pairs)
    ]
    for copy in copies:
        copy.start()
    heads_kv = k_ref.shape[0] // (2 * RUN)
    rows = heads_kv * RUN
    at = lax.broadcasted_iota(jnp.int32, (rows, rows), 0)
    origin = lax.broadcasted_iota(jnp.int32, (rows, rows), 1)
    move = at % RUN * heads_kv + at // RUN == origin
    move = jnp.where(move, 1.0, 0.0).astype(k_ref.dtype)
    for n, ref in enumerate((k_ref, v_ref)):
        copies[n].wait()
        for r in range(2):
            moved = jnp.dot(
                move,
                ref[r * rows : (r + 1) * rows],
                preferred_element_type=jnp.float32,
            )
            start = (2 * r + n) * rows
            own_ref[start : start + rows] = moved.astype(own_ref.dtype)
    copies[2].wait()
    numbers = (positions_ref[...] // RUN).astype(jnp.float32)
    numbers = jnp.broadcast_to(numbers, (16, numbers.shape[1]))
    own_ref[4 * rows :] = numbers.astype(own_ref.dtype)


class Attention:
    def __init__(self, q, group, half, room):
        self.q, self.group, self.half = q, group, half
        self.factor = math.log2(math.e) / math.sqrt(q.shape[3])
        heads_kv, rows, head_dim = q.shape[1:]
        self.block_rows = 4 * heads_kv * RUN + 16
        slots = 2 * room + TILE
        self.carried = [jax.ShapeDtypeStruct((8, 128), jnp.float32)]
        self.carried += [
            jax.ShapeDtypeStruct((2, heads_kv, rows, n), jnp.float32)
            for n in (128, head_dim + 128)
        ]
        self.carried.append(
            jax.ShapeDtypeStruct((2, slots, 2 * heads_kv * RUN, head_dim), q.dtype)
        )

    def call(self, kernel, operands, shapes, aliases, count, name, out=None):
        vmem = pl.BlockSpec(memory_space=pltpu.VMEM)
        out_specs = [vmem] * len(shapes)
        scratch = []
        if out is not None:
            shapes = [out, *shapes]
            out_specs.insert(0, pl.BlockSpec(memory_space=pl.ANY))
            scratch = [pltpu.VMEM(out.shape, out.dtype), pltpu.SemaphoreType.DMA((8,))]
        return pl.pallas_call(
            kernel,
            out_shape=shapes,
            in_specs=[vmem] * len(operands),
            out_specs=out_specs,
            scratch_shapes=scratch,
            input_output_aliases=aliases,
            compiler_params=pltpu.CompilerParams(vmem_limit_bytes=28 * 1024 * 1024),
            cost_estimate=pl.CostEstimate(
                flops=count * RUN * self.q.size * 4,
                bytes_accessed=self.q.size * 8,
                transcendentals=0,
            ),
            name=name,
        )(*operands)

    def start(self, own):
        kernel = functools.partial(own_kernel, self.group, self.factor, self.half)
        return self.call(kernel, [self.q, own], self.carried, {}, 2, "attend_own")

    def add(self, state, kvs, keep=KEEP, out=None):
        kvs = [x if isinstance(x, tuple) else (x, 0) for x in kvs]
        blocks = [(skip, x.shape[0] // self.block_rows) for x, skip in kvs]
        count = sum(end - skip for skip, end in blocks)
        operands = [self.q, *(x for x, _ in kvs), *state]
        first, ahead = 1 + len(kvs), int(out is not None)
        aliases = {first + n: ahead + n for n in range(len(state))}
        kernel = functools.partial(
            attend_kernel, self.group, self.factor, self.half, ahead, keep, blocks
        )
        results = self.call(kernel, operands, self.carried, aliases, count, "attend", out)
        return results[0] if ahead else results


def per_device(queries, keys, values, positions):
    outer, inner = lax.axis_size("outer"), lax.axis_size("inner")
    tokens, heads_q, head_dim = queries.shape
    heads_kv = keys.shape[1]
    group = heads_q // heads_kv
    half = tokens // RUN * outer * inner // 2

    chips = outer // 2
    bits = inner.bit_length() - 1
    ring = [0] + list(range(1, chips, 2)) + list(range(2, chips, 2))[::-1]
    after = {ring[n]: ring[(n + 1) % chips] for n in range(chips)}

    def permute(x, to):
        pairs = []
        for z in range(chips):
            for core in range(2):
                for place in range(inner):
                    nz, ncore, nplace = to(z, core, place)
                    pairs.append(
                        (
                            (2 * z + core) * inner + place,
                            (2 * nz + ncore) * inner + nplace,
                        )
                    )
        return lax.ppermute(x, AXES, pairs)

    def along_z(x, cross=0):
        return permute(x, lambda z, core, place: (after[z], core ^ cross, place))

    def over_place(x, step):
        def to(z, core, place):
            return z, core, place ^ (1 << (bits - 1 - step if core else step))

        return permute(x, to)

    def other_core(x):
        return permute(x, lambda z, core, place: (z, 1 - core, place))

    def tied(x, *others):
        return lax.optimization_barrier((x, *others))[0]

    flat = jax.ShapeDtypeStruct((tokens * heads_kv, head_dim), keys.dtype)
    own = pl.pallas_call(
        pack_kernel,
        out_shape=jax.ShapeDtypeStruct(
            (2 * tokens * heads_kv + 16, head_dim), keys.dtype
        ),
        in_specs=[pl.BlockSpec(memory_space=pltpu.HBM)] * 3,
        out_specs=pl.BlockSpec(memory_space=pltpu.VMEM),
        scratch_shapes=[
            pltpu.VMEM(flat.shape, flat.dtype),
            pltpu.VMEM(flat.shape, flat.dtype),
            pltpu.VMEM((1, tokens), jnp.int32),
            pltpu.SemaphoreType.DMA((3,)),
        ],
        compiler_params=pltpu.CompilerParams(vmem_limit_bytes=60 * 1024 * 1024),
        name="pack",
    )(keys.reshape(flat.shape), values.reshape(flat.shape), positions.reshape(1, tokens))
    q = (
        queries.reshape(2, RUN, heads_kv, group, head_dim)
        .transpose(0, 2, 1, 3, 4)
        .reshape(2, heads_kv, RUN * group, head_dim)
    )

    attention = Attention(q, group, half, 2 * inner)
    state = attention.start(own)

    stage = own
    halves, theirs = [], []
    for n in range(chips - 1):
        following = along_z(stage)
        held = stage
        for step in range(bits):
            if n == 0 and step + 1 == bits:
                first = held
                held = tied(held, state[0])
            there = over_place(held, step)
            if n and step == 0:
                if n == 1:
                    kvs = [(halves[0][0], 1), theirs[0][0]]
                else:
                    kvs = [halves[n - 2][1], halves[n - 1][0], theirs[n - 2][-1]]
                state = attention.add(state, kvs)
                there = tied(there, state[0])
            if step + 1 < bits:
                held = jnp.concatenate([held, there])
        halves.append((held, there))
        if n == 0:
            theirs.append([other_core(tied(first, following)), other_core(there)])
            stage = following
            continue
        held = jnp.concatenate([held, there])
        if n + 2 == chips:
            state = attention.add(state, [halves[n - 1][1], theirs[n - 1][-1], halves[n][0]])
            held = tied(held, state[0])
        theirs.append([other_core(held)])
        stage = following

    found = [stage]
    for step in range(bits):
        found += [over_place(x, step) for x in found]
    *most, final = found
    crossed = along_z(halves[-1][1][-own.shape[0] :], cross=1)
    most = jnp.concatenate(most)
    their_most = other_core(most)
    state = attention.add(state, [halves[-1][1], theirs[-1][-1]])
    state = attention.add(state, [most, their_most], keep=1)
    last = [tied(x, state[0]) for x in (final, crossed)]
    out = jax.ShapeDtypeStruct(queries.shape, queries.dtype)
    return attention.add(state, last, keep=1, out=out)


def solution(mesh):
    in_specs = (
        P(("outer", "inner"), None, None),
        P(("outer", "inner"), None, None),
        P(("outer", "inner"), None, None),
        P(("outer", "inner")),
    )
    out_specs = P(("outer", "inner"), None, None)
    return jax.shard_map(
        per_device, mesh=mesh, in_specs=in_specs, out_specs=out_specs, check_vma=False
    )
```

```python
import functools
import math

import jax
import jax.numpy as jnp
from jax import lax
from jax.experimental import pallas as pl
from jax.experimental.pallas import tpu as pltpu
from jax.sharding import PartitionSpec as P

RUN = 64
TILE = 8
KEEP = 4
AXES = ("outer", "inner")


def flash(score, v, state, factor, live=None):
    top, mixed = state
    keys = score.shape[1]
    if isinstance(live, int):
        lane = lax.broadcasted_iota(jnp.int32, score.shape, 1)
        keys, live = live, lane < live
    if live is not None:
        score = jnp.where(live, score, -jnp.inf)
    parts = [score[:, c : c + 128] for c in range(0, score.shape[1], 128)]
    new = jnp.max(functools.reduce(jnp.maximum, parts), axis=1, keepdims=True)
    if top is None:
        new = jnp.broadcast_to(new, parts[0].shape)
    else:
        new = jnp.maximum(top, new)
    weights = [
        jnp.exp2((part - new) * factor).astype(jnp.bfloat16) for part in parts
    ]
    weights = jnp.concatenate(weights, axis=1)
    ones = jnp.ones((keys, 128), v.dtype)
    part_mixed = jnp.dot(
        weights[:, :keys],
        jnp.concatenate([v, ones], axis=1),
        preferred_element_type=jnp.float32,
    )
    if top is None:
        return new, part_mixed
    decay = jnp.exp2((top - new) * factor)
    halves = [
        mixed[:, c : c + 128] * decay + part_mixed[:, c : c + 128]
        for c in range(0, mixed.shape[1], 128)
    ]
    return new, jnp.concatenate(halves, axis=1)


def head_tile(q_ref, state_refs, a, keys, values, factor, live=None):
    heads_kv, rows = q_ref.shape[1:3]
    pieces = [
        (h, slice(start, start + rows // 2))
        for h in range(heads_kv)
        for start in (0, rows // 2)
    ]

    def scores(h, part):
        return lax.dot_general(
            q_ref[a, h, part],
            keys(h),
            (((1,), (1,)), ((), ())),
            preferred_element_type=jnp.float32,
        )

    ahead = scores(*pieces[0])
    for n, (h, part) in enumerate(pieces):
        score = ahead
        if n + 1 < len(pieces):
            ahead = scores(*pieces[n + 1])
        state, mask = (None, None), live
        if live is None or isinstance(live, int):
            state = tuple(ref[a, h, part] for ref in state_refs)
        else:
            mask = live[part]
        state = flash(score, values(h), state, factor, mask)
        for ref, value in zip(state_refs, state):
            ref[a, h, part] = value


def own_kernel(group, factor, half, q_ref, own_ref, meta_ref, *refs):
    heads_kv, rows, head_dim = q_ref.shape[1:]
    state_refs = refs[:2]
    run_rows = 2 * heads_kv * RUN

    ids = own_ref[2 * run_rows :].astype(jnp.float32)
    lane = lax.broadcasted_iota(jnp.int32, ids.shape, 1)
    numbers = [jnp.max(jnp.where(lane // RUN == a, ids, 0.0)) for a in range(2)]
    row = lax.broadcasted_iota(jnp.int32, meta_ref.shape, 0)
    meta_ref[...] = jnp.where(
        row == 0, numbers[0], jnp.where(row == 1, numbers[1], 0.0)
    )

    row_at = lax.broadcasted_iota(jnp.int32, (rows, 2 * RUN), 0) // group
    key_at = lax.broadcasted_iota(jnp.int32, (rows, 2 * RUN), 1)
    for a in range(2):
        mine, other = numbers[a], numbers[1 - a]
        seen = (other < mine) & ((other >= half) == (mine >= half))
        reach = jnp.where(seen, RUN, 0)
        if a == 0:
            live = (key_at <= row_at) | ((key_at >= RUN) & (key_at < RUN + reach))
        else:
            live = (key_at < reach) | ((key_at >= RUN) & (key_at - RUN <= row_at))

        def own(g):
            starts = [g * RUN, run_rows + g * RUN]
            return jnp.concatenate([own_ref[n : n + RUN] for n in starts])

        head_tile(q_ref, state_refs, a, own, lambda h: own(heads_kv + h), factor, live)


def attend_kernel(group, factor, half, last, keep, blocks, q_ref, *refs):
    heads_kv, rows, head_dim = q_ref.shape[1:]
    run_rows = 2 * heads_kv * RUN
    block_rows = 2 * run_rows + 16
    kv_refs, refs = refs[: len(blocks)], refs[len(blocks) :]
    refs = refs[4:]
    if last:
        out_ref, refs = refs[0], refs[1:]
    meta_ref, *state_refs, buf = refs[:4]

    meta = meta_ref[...]
    counts = tuple(
        jnp.max(meta[2 + a : 3 + a]).astype(jnp.int32) for a in range(2)
    )
    seen_bits = []
    for ref, (skip, end) in zip(kv_refs, blocks):
        assert end - skip <= 8
        ids = jnp.concatenate(
            [ref[n * block_rows - 16 : n * block_rows] for n in range(skip + 1, end + 1)]
        ).astype(jnp.float32)
        row = lax.broadcasted_iota(jnp.int32, ids.shape, 0)
        lane = lax.broadcasted_iota(jnp.int32, ids.shape, 1)
        bit = jnp.left_shift(1, 2 * (row // 16) + lane // RUN)
        bit = jnp.where((row % 16 == 0) & (lane % RUN == 0), bit, 0).astype(jnp.float32)
        found = []
        for a in range(2):
            mine = meta[a : a + 1]
            low = jnp.where(mine >= half, float(half), 0.0)
            seen = (ids < mine) & (ids >= low)
            found.append(jnp.sum(jnp.where(seen, bit, 0.0)).astype(jnp.int32))
        seen_bits.append(found)

    for ref, (skip, end), bits in zip(kv_refs, blocks, seen_bits):

        def gather(n, counts):
            at = pl.multiple_of((skip + n // 2) * block_rows + n % 2 * run_rows, 16)
            fresh = []
            for a in range(2):
                flag = (bits[a] >> n) & 1
                count = counts[a]

                @pl.when(flag == 1)
                def _():
                    buf[a, count] = ref[pl.ds(at, run_rows), :]

                fresh.append(count + flag)
            return tuple(fresh)

        counts = lax.fori_loop(0, 2 * (end - skip), gather, counts)

    def some_runs(a, start, runs):
        def rows_of(g):
            found = buf[a, pl.ds(start, runs), g * RUN : (g + 1) * RUN, :]
            return found.reshape(runs * RUN, -1)

        def keys(h):
            if runs > 1:
                return rows_of(h)
            return jnp.concatenate([rows_of(h), jnp.zeros((RUN, head_dim), buf.dtype)])

        live = RUN if runs == 1 else None
        head_tile(
            q_ref, state_refs, a, keys, lambda h: rows_of(heads_kv + h), factor, live
        )

    whole = [count // TILE for count in counts]

    def step(item, carry):
        a = (item >= whole[0]).astype(jnp.int32)
        some_runs(a, (item - a * whole[0]) * TILE, TILE)
        return carry

    lax.fori_loop(0, whole[0] + whole[1], step, 0)

    def remainder(a, carry):
        count = jnp.where(a == 0, counts[0], counts[1])
        start = count // TILE * TILE
        runs = TILE // 2
        while runs >= keep:

            @pl.when(count & runs != 0)
            def _():
                some_runs(a, start, runs)

            start = start + (count & runs)
            runs //= 2
        return carry

    lax.fori_loop(0, 2, remainder, 0)

    if not last:
        row = lax.broadcasted_iota(jnp.int32, meta.shape, 0)
        for a in range(2):
            start = counts[a] // keep * keep
            rest = counts[a] - start
            if keep > 1:

                @pl.when((start > 0) & (rest > 0))
                def _():
                    for n in range(keep - 1):
                        buf[a, n] = buf[a, start + n]

            meta = jnp.where(row == 2 + a, rest.astype(jnp.float32), meta)
        meta_ref[...] = meta
        return

    made, sems = refs[4:]
    copies = []
    for a in range(2):
        for h in range(0, heads_kv, 2):
            done = []
            for g in (h, h + 1):
                mixed = state_refs[1][a, g]
                part = mixed[:, :head_dim] * (1.0 / mixed[:, head_dim:])
                done.append(part.reshape(RUN, group, -1))
            place = (slice(a * RUN, (a + 1) * RUN), slice(h * group, (h + 2) * group))
            made[place] = jnp.concatenate(done, axis=1).astype(out_ref.dtype)
            copy = pltpu.make_async_copy(
                made.at[place], out_ref.at[place], sems.at[len(copies)]
            )
            copy.start()
            copies.append(copy)
    for copy in copies:
        copy.wait()


def pack_kernel(k_any, v_any, positions_any, own_ref, k_ref, v_ref, positions_ref, sems):
    pairs = ((k_any, k_ref), (v_any, v_ref), (positions_any, positions_ref))
    copies = [
        pltpu.make_async_copy(source, target, sems.at[n])
        for n, (source, target) in enumerate(pairs)
    ]
    for copy in copies:
        copy.start()
    heads_kv = k_ref.shape[0] // (2 * RUN)
    rows = heads_kv * RUN
    at = lax.broadcasted_iota(jnp.int32, (rows, rows), 0)
    origin = lax.broadcasted_iota(jnp.int32, (rows, rows), 1)
    move = at % RUN * heads_kv + at // RUN == origin
    move = jnp.where(move, 1.0, 0.0).astype(k_ref.dtype)
    for n, ref in enumerate((k_ref, v_ref)):
        copies[n].wait()
        for r in range(2):
            moved = jnp.dot(
                move,
                ref[r * rows : (r + 1) * rows],
                preferred_element_type=jnp.float32,
            )
            start = (2 * r + n) * rows
            own_ref[start : start + rows] = moved.astype(own_ref.dtype)
    copies[2].wait()
    numbers = (positions_ref[...] // RUN).astype(jnp.float32)
    numbers = jnp.broadcast_to(numbers, (16, numbers.shape[1]))
    own_ref[4 * rows :] = numbers.astype(own_ref.dtype)


class Attention:
    def __init__(self, q, group, half, room):
        self.q, self.group, self.half = q, group, half
        self.factor = math.log2(math.e) / math.sqrt(q.shape[3])
        heads_kv, rows, head_dim = q.shape[1:]
        self.block_rows = 4 * heads_kv * RUN + 16
        slots = 2 * room + TILE
        self.carried = [jax.ShapeDtypeStruct((8, 128), jnp.float32)]
        self.carried += [
            jax.ShapeDtypeStruct((2, heads_kv, rows, n), jnp.float32)
            for n in (128, head_dim + 128)
        ]
        self.carried.append(
            jax.ShapeDtypeStruct((2, slots, 2 * heads_kv * RUN, head_dim), q.dtype)
        )

    def call(self, kernel, operands, shapes, aliases, count, name, out=None):
        vmem = pl.BlockSpec(memory_space=pltpu.VMEM)
        out_specs = [vmem] * len(shapes)
        scratch = []
        if out is not None:
            shapes = [out, *shapes]
            out_specs.insert(0, pl.BlockSpec(memory_space=pl.ANY))
            scratch = [pltpu.VMEM(out.shape, out.dtype), pltpu.SemaphoreType.DMA((8,))]
        return pl.pallas_call(
            kernel,
            out_shape=shapes,
            in_specs=[vmem] * len(operands),
            out_specs=out_specs,
            scratch_shapes=scratch,
            input_output_aliases=aliases,
            compiler_params=pltpu.CompilerParams(vmem_limit_bytes=28 * 1024 * 1024),
            cost_estimate=pl.CostEstimate(
                flops=count * RUN * self.q.size * 4,
                bytes_accessed=self.q.size * 8,
                transcendentals=0,
            ),
            name=name,
        )(*operands)

    def start(self, own):
        kernel = functools.partial(own_kernel, self.group, self.factor, self.half)
        return self.call(kernel, [self.q, own], self.carried, {}, 2, "attend_own")

    def add(self, state, kvs, keep=KEEP, out=None):
        kvs = [x if isinstance(x, tuple) else (x, 0) for x in kvs]
        blocks = [(skip, x.shape[0] // self.block_rows) for x, skip in kvs]
        count = sum(end - skip for skip, end in blocks)
        operands = [self.q, *(x for x, _ in kvs), *state]
        first, ahead = 1 + len(kvs), int(out is not None)
        aliases = {first + n: ahead + n for n in range(len(state))}
        kernel = functools.partial(
            attend_kernel, self.group, self.factor, self.half, ahead, keep, blocks
        )
        results = self.call(kernel, operands, self.carried, aliases, count, "attend", out)
        return results[0] if ahead else results


def per_device(queries, keys, values, positions):
    outer, inner = lax.axis_size("outer"), lax.axis_size("inner")
    tokens, heads_q, head_dim = queries.shape
    heads_kv = keys.shape[1]
    group = heads_q // heads_kv
    half = tokens // RUN * outer * inner // 2

    chips = outer // 2
    bits = inner.bit_length() - 1
    ring = [0] + list(range(1, chips, 2)) + list(range(2, chips, 2))[::-1]
    after = {ring[n]: ring[(n + 1) % chips] for n in range(chips)}

    def permute(x, to):
        pairs = []
        for z in range(chips):
            for core in range(2):
                for place in range(inner):
                    nz, ncore, nplace = to(z, core, place)
                    pairs.append(
                        (
                            (2 * z + core) * inner + place,
                            (2 * nz + ncore) * inner + nplace,
                        )
                    )
        return lax.ppermute(x, AXES, pairs)

    def along_z(x):
        return permute(x, lambda z, core, place: (after[z], core, place))

    def over_place(x, step, cross=0):
        def to(z, core, place):
            bit = bits - 1 - step if core else step
            return z, core ^ cross, place ^ (1 << bit)

        return permute(x, to)

    def other_core(x):
        return permute(x, lambda z, core, place: (z, 1 - core, place))

    def tied(x, *others):
        return lax.optimization_barrier((x, *others))[0]

    flat = jax.ShapeDtypeStruct((tokens * heads_kv, head_dim), keys.dtype)
    own = pl.pallas_call(
        pack_kernel,
        out_shape=jax.ShapeDtypeStruct(
            (2 * tokens * heads_kv + 16, head_dim), keys.dtype
        ),
        in_specs=[pl.BlockSpec(memory_space=pltpu.HBM)] * 3,
        out_specs=pl.BlockSpec(memory_space=pltpu.VMEM),
        scratch_shapes=[
            pltpu.VMEM(flat.shape, flat.dtype),
            pltpu.VMEM(flat.shape, flat.dtype),
            pltpu.VMEM((1, tokens), jnp.int32),
            pltpu.SemaphoreType.DMA((3,)),
        ],
        compiler_params=pltpu.CompilerParams(vmem_limit_bytes=60 * 1024 * 1024),
        name="pack",
    )(keys.reshape(flat.shape), values.reshape(flat.shape), positions.reshape(1, tokens))
    q = (
        queries.reshape(2, RUN, heads_kv, group, head_dim)
        .transpose(0, 2, 1, 3, 4)
        .reshape(2, heads_kv, RUN * group, head_dim)
    )

    attention = Attention(q, group, half, 2 * inner)
    state = attention.start(own)

    stage = own
    halves, theirs = [], []
    for n in range(chips - 1):
        following = along_z(stage)
        held = stage
        for step in range(bits):
            if n == 0 and step + 1 == bits:
                first = held
                held = tied(held, state[0])
            there = over_place(held, step)
            if n and step == 0:
                if n == 1:
                    kvs = [(halves[0][0], 1), theirs[0][0]]
                else:
                    kvs = [halves[n - 2][1], halves[n - 1][0], theirs[n - 2][-1]]
                state = attention.add(state, kvs)
                there = tied(there, state[0])
            if step + 1 < bits:
                held = jnp.concatenate([held, there])
        halves.append((held, there))
        if n == 0:
            theirs.append([other_core(tied(first, following)), other_core(there)])
            stage = following
            continue
        held = jnp.concatenate([held, there])
        if n + 2 == chips:
            state = attention.add(state, [halves[n - 1][1], theirs[n - 1][-1], halves[n][0]])
            held = tied(held, state[0])
        theirs.append([other_core(held)])
        stage = following

    found = [stage]
    for step in range(bits):
        found += [over_place(x, step) for x in found]
    *most, final = found
    crossed = over_place(found[inner // 2 - 1], bits - 1, cross=1)
    most = jnp.concatenate(most)
    their_most = other_core(most)
    state = attention.add(state, [halves[-1][1], theirs[-1][-1]])
    state = attention.add(state, [most, their_most])
    last = [tied(x, state[0]) for x in (final, crossed)]
    out = jax.ShapeDtypeStruct(queries.shape, queries.dtype)
    return attention.add(state, last, keep=1, out=out)


def solution(mesh):
    in_specs = (
        P(("outer", "inner"), None, None),
        P(("outer", "inner"), None, None),
        P(("outer", "inner"), None, None),
        P(("outer", "inner")),
    )
    out_specs = P(("outer", "inner"), None, None)
    return jax.shard_map(
        per_device, mesh=mesh, in_specs=in_specs, out_specs=out_specs, check_vma=False
    )
```

```python
import functools
import math

import jax
import jax.numpy as jnp
from jax import lax
from jax.experimental import pallas as pl
from jax.experimental.pallas import tpu as pltpu
from jax.sharding import PartitionSpec as P

RUN = 64
TILE = 8
KEEP = 4
AXES = ("outer", "inner")


def flash(score, v, state, factor, live=None):
    top, mixed = state
    keys = score.shape[1]
    if isinstance(live, int):
        lane = lax.broadcasted_iota(jnp.int32, score.shape, 1)
        keys, live = live, lane < live
    if live is not None:
        score = jnp.where(live, score, -jnp.inf)
    parts = [score[:, c : c + 128] for c in range(0, score.shape[1], 128)]
    new = jnp.max(functools.reduce(jnp.maximum, parts), axis=1, keepdims=True)
    if top is None:
        new = jnp.broadcast_to(new, parts[0].shape)
    else:
        new = jnp.maximum(top, new)
    weights = [
        jnp.exp2((part - new) * factor).astype(jnp.bfloat16) for part in parts
    ]
    weights = jnp.concatenate(weights, axis=1)
    ones = jnp.ones((keys, 128), v.dtype)
    part_mixed = jnp.dot(
        weights[:, :keys],
        jnp.concatenate([v, ones], axis=1),
        preferred_element_type=jnp.float32,
    )
    if top is None:
        return new, part_mixed
    decay = jnp.exp2((top - new) * factor)
    halves = [
        mixed[:, c : c + 128] * decay + part_mixed[:, c : c + 128]
        for c in range(0, mixed.shape[1], 128)
    ]
    return new, jnp.concatenate(halves, axis=1)


def head_tile(q_ref, state_refs, a, keys, values, factor, live=None):
    def scores(h):
        return lax.dot_general(
            q_ref[a, h],
            keys(h),
            (((1,), (1,)), ((), ())),
            preferred_element_type=jnp.float32,
        )

    heads_kv = q_ref.shape[1]
    ahead = scores(0)
    for h in range(heads_kv):
        score = ahead
        if h + 1 < heads_kv:
            ahead = scores(h + 1)
        state = (None, None)
        if live is None or isinstance(live, int):
            state = tuple(ref[a, h] for ref in state_refs)
        state = flash(score, values(h), state, factor, live)
        for ref, value in zip(state_refs, state):
            ref[a, h] = value


def own_kernel(group, factor, half, q_ref, own_ref, meta_ref, *refs):
    heads_kv, rows, head_dim = q_ref.shape[1:]
    state_refs = refs[:2]
    run_rows = 2 * heads_kv * RUN

    ids = own_ref[2 * run_rows :].astype(jnp.float32)
    lane = lax.broadcasted_iota(jnp.int32, ids.shape, 1)
    numbers = [jnp.max(jnp.where(lane // RUN == a, ids, 0.0)) for a in range(2)]
    row = lax.broadcasted_iota(jnp.int32, meta_ref.shape, 0)
    meta_ref[...] = jnp.where(
        row == 0, numbers[0], jnp.where(row == 1, numbers[1], 0.0)
    )

    row_at = lax.broadcasted_iota(jnp.int32, (rows, 2 * RUN), 0) // group
    key_at = lax.broadcasted_iota(jnp.int32, (rows, 2 * RUN), 1)
    for a in range(2):
        mine, other = numbers[a], numbers[1 - a]
        seen = (other < mine) & ((other >= half) == (mine >= half))
        reach = jnp.where(seen, RUN, 0)
        if a == 0:
            live = (key_at <= row_at) | ((key_at >= RUN) & (key_at < RUN + reach))
        else:
            live = (key_at < reach) | ((key_at >= RUN) & (key_at - RUN <= row_at))

        def own(g):
            starts = [g * RUN, run_rows + g * RUN]
            return jnp.concatenate([own_ref[n : n + RUN] for n in starts])

        head_tile(q_ref, state_refs, a, own, lambda h: own(heads_kv + h), factor, live)


def attend_kernel(group, factor, half, last, keep, blocks, q_ref, *refs):
    heads_kv, rows, head_dim = q_ref.shape[1:]
    run_rows = 2 * heads_kv * RUN
    block_rows = 2 * run_rows + 16
    kv_refs, refs = refs[: len(blocks)], refs[len(blocks) :]
    refs = refs[4:]
    if last:
        out_ref, refs = refs[0], refs[1:]
    meta_ref, *state_refs, buf = refs[:4]

    meta = meta_ref[...]
    counts = tuple(
        jnp.max(meta[2 + a : 3 + a]).astype(jnp.int32) for a in range(2)
    )
    seen_bits = []
    for ref, (skip, end) in zip(kv_refs, blocks):
        assert end - skip <= 8
        ids = jnp.concatenate(
            [ref[n * block_rows - 16 : n * block_rows] for n in range(skip + 1, end + 1)]
        ).astype(jnp.float32)
        row = lax.broadcasted_iota(jnp.int32, ids.shape, 0)
        lane = lax.broadcasted_iota(jnp.int32, ids.shape, 1)
        bit = jnp.left_shift(1, 2 * (row // 16) + lane // RUN)
        bit = jnp.where((row % 16 == 0) & (lane % RUN == 0), bit, 0).astype(jnp.float32)
        found = []
        for a in range(2):
            mine = meta[a : a + 1]
            low = jnp.where(mine >= half, float(half), 0.0)
            seen = (ids < mine) & (ids >= low)
            found.append(jnp.sum(jnp.where(seen, bit, 0.0)).astype(jnp.int32))
        seen_bits.append(found)

    for ref, (skip, end), bits in zip(kv_refs, blocks, seen_bits):

        def gather(n, counts):
            at = pl.multiple_of((skip + n // 2) * block_rows + n % 2 * run_rows, 16)
            fresh = []
            for a in range(2):
                flag = (bits[a] >> n) & 1
                count = counts[a]

                @pl.when(flag == 1)
                def _():
                    buf[a, count] = ref[pl.ds(at, run_rows), :]

                fresh.append(count + flag)
            return tuple(fresh)

        counts = lax.fori_loop(0, 2 * (end - skip), gather, counts)

    def some_runs(a, start, runs):
        def rows_of(g):
            found = buf[a, pl.ds(start, runs), g * RUN : (g + 1) * RUN, :]
            return found.reshape(runs * RUN, -1)

        def keys(h):
            if runs > 1:
                return rows_of(h)
            return jnp.concatenate([rows_of(h), jnp.zeros((RUN, head_dim), buf.dtype)])

        live = RUN if runs == 1 else None
        head_tile(
            q_ref, state_refs, a, keys, lambda h: rows_of(heads_kv + h), factor, live
        )

    whole = [count // TILE for count in counts]

    def step(item, carry):
        a = (item >= whole[0]).astype(jnp.int32)
        some_runs(a, (item - a * whole[0]) * TILE, TILE)
        return carry

    lax.fori_loop(0, whole[0] + whole[1], step, 0)

    def remainder(a, carry):
        count = jnp.where(a == 0, counts[0], counts[1])
        start = count // TILE * TILE
        runs = TILE // 2
        while runs >= keep:

            @pl.when(count & runs != 0)
            def _():
                some_runs(a, start, runs)

            start = start + (count & runs)
            runs //= 2
        return carry

    lax.fori_loop(0, 2, remainder, 0)

    if not last:
        row = lax.broadcasted_iota(jnp.int32, meta.shape, 0)
        for a in range(2):
            start = counts[a] // keep * keep
            rest = counts[a] - start
            if keep > 1:

                @pl.when((start > 0) & (rest > 0))
                def _():
                    for n in range(keep - 1):
                        buf[a, n] = buf[a, start + n]

            meta = jnp.where(row == 2 + a, rest.astype(jnp.float32), meta)
        meta_ref[...] = meta
        return

    made, sems = refs[4:]
    copies = []
    for a in range(2):
        for h in range(0, heads_kv, 2):
            done = []
            for g in (h, h + 1):
                mixed = state_refs[1][a, g]
                part = mixed[:, :head_dim] * (1.0 / mixed[:, head_dim:])
                done.append(part.reshape(RUN, group, -1))
            place = (slice(a * RUN, (a + 1) * RUN), slice(h * group, (h + 2) * group))
            made[place] = jnp.concatenate(done, axis=1).astype(out_ref.dtype)
            copy = pltpu.make_async_copy(
                made.at[place], out_ref.at[place], sems.at[len(copies)]
            )
            copy.start()
            copies.append(copy)
    for copy in copies:
        copy.wait()


def pack_kernel(k_any, v_any, positions_any, own_ref, k_ref, v_ref, positions_ref, sems):
    pairs = ((k_any, k_ref), (v_any, v_ref), (positions_any, positions_ref))
    copies = [
        pltpu.make_async_copy(source, target, sems.at[n])
        for n, (source, target) in enumerate(pairs)
    ]
    for copy in copies:
        copy.start()
    heads_kv = k_ref.shape[0] // (2 * RUN)
    rows = heads_kv * RUN
    at = lax.broadcasted_iota(jnp.int32, (rows, rows), 0)
    origin = lax.broadcasted_iota(jnp.int32, (rows, rows), 1)
    move = at % RUN * heads_kv + at // RUN == origin
    move = jnp.where(move, 1.0, 0.0).astype(k_ref.dtype)
    for n, ref in enumerate((k_ref, v_ref)):
        copies[n].wait()
        for r in range(2):
            moved = jnp.dot(
                move,
                ref[r * rows : (r + 1) * rows],
                preferred_element_type=jnp.float32,
            )
            start = (2 * r + n) * rows
            own_ref[start : start + rows] = moved.astype(own_ref.dtype)
    copies[2].wait()
    numbers = (positions_ref[...] // RUN).astype(jnp.float32)
    numbers = jnp.broadcast_to(numbers, (16, numbers.shape[1]))
    own_ref[4 * rows :] = numbers.astype(own_ref.dtype)


class Attention:
    def __init__(self, q, group, half, room):
        self.q, self.group, self.half = q, group, half
        self.factor = math.log2(math.e) / math.sqrt(q.shape[3])
        heads_kv, rows, head_dim = q.shape[1:]
        self.block_rows = 4 * heads_kv * RUN + 16
        slots = 2 * room + TILE
        self.carried = [jax.ShapeDtypeStruct((8, 128), jnp.float32)]
        self.carried += [
            jax.ShapeDtypeStruct((2, heads_kv, rows, n), jnp.float32)
            for n in (128, head_dim + 128)
        ]
        self.carried.append(
            jax.ShapeDtypeStruct((2, slots, 2 * heads_kv * RUN, head_dim), q.dtype)
        )

    def call(self, kernel, operands, shapes, aliases, count, name, out=None):
        vmem = pl.BlockSpec(memory_space=pltpu.VMEM)
        out_specs = [vmem] * len(shapes)
        scratch = []
        if out is not None:
            shapes = [out, *shapes]
            out_specs.insert(0, pl.BlockSpec(memory_space=pl.ANY))
            scratch = [pltpu.VMEM(out.shape, out.dtype), pltpu.SemaphoreType.DMA((8,))]
        return pl.pallas_call(
            kernel,
            out_shape=shapes,
            in_specs=[vmem] * len(operands),
            out_specs=out_specs,
            scratch_shapes=scratch,
            input_output_aliases=aliases,
            compiler_params=pltpu.CompilerParams(vmem_limit_bytes=28 * 1024 * 1024),
            cost_estimate=pl.CostEstimate(
                flops=count * RUN * self.q.size * 4,
                bytes_accessed=self.q.size * 8,
                transcendentals=0,
            ),
            name=name,
        )(*operands)

    def start(self, own):
        kernel = functools.partial(own_kernel, self.group, self.factor, self.half)
        return self.call(kernel, [self.q, own], self.carried, {}, 2, "attend_own")

    def add(self, state, kvs, keep=KEEP, out=None):
        kvs = [x if isinstance(x, tuple) else (x, 0) for x in kvs]
        blocks = [(skip, x.shape[0] // self.block_rows) for x, skip in kvs]
        count = sum(end - skip for skip, end in blocks)
        operands = [self.q, *(x for x, _ in kvs), *state]
        first, ahead = 1 + len(kvs), int(out is not None)
        aliases = {first + n: ahead + n for n in range(len(state))}
        kernel = functools.partial(
            attend_kernel, self.group, self.factor, self.half, ahead, keep, blocks
        )
        results = self.call(kernel, operands, self.carried, aliases, count, "attend", out)
        return results[0] if ahead else results


def per_device(queries, keys, values, positions):
    outer, inner = lax.axis_size("outer"), lax.axis_size("inner")
    tokens, heads_q, head_dim = queries.shape
    heads_kv = keys.shape[1]
    group = heads_q // heads_kv
    half = tokens // RUN * outer * inner // 2

    chips = outer // 2
    bits = inner.bit_length() - 1
    ring = [0] + list(range(1, chips, 2)) + list(range(2, chips, 2))[::-1]
    after = {ring[n]: ring[(n + 1) % chips] for n in range(chips)}

    def permute(x, to):
        pairs = []
        for z in range(chips):
            for core in range(2):
                for place in range(inner):
                    nz, ncore, nplace = to(z, core, place)
                    pairs.append(
                        (
                            (2 * z + core) * inner + place,
                            (2 * nz + ncore) * inner + nplace,
                        )
                    )
        return lax.ppermute(x, AXES, pairs)

    def along_z(x):
        return permute(x, lambda z, core, place: (after[z], core, place))

    def over_place(x, step, cross=0):
        def to(z, core, place):
            bit = bits - 1 - step if core else step
            return z, core ^ cross, place ^ (1 << bit)

        return permute(x, to)

    def other_core(x):
        return permute(x, lambda z, core, place: (z, 1 - core, place))

    def tied(x, *others):
        return lax.optimization_barrier((x, *others))[0]

    flat = jax.ShapeDtypeStruct((tokens * heads_kv, head_dim), keys.dtype)
    own = pl.pallas_call(
        pack_kernel,
        out_shape=jax.ShapeDtypeStruct(
            (2 * tokens * heads_kv + 16, head_dim), keys.dtype
        ),
        in_specs=[pl.BlockSpec(memory_space=pltpu.HBM)] * 3,
        out_specs=pl.BlockSpec(memory_space=pltpu.VMEM),
        scratch_shapes=[
            pltpu.VMEM(flat.shape, flat.dtype),
            pltpu.VMEM(flat.shape, flat.dtype),
            pltpu.VMEM((1, tokens), jnp.int32),
            pltpu.SemaphoreType.DMA((3,)),
        ],
        compiler_params=pltpu.CompilerParams(vmem_limit_bytes=60 * 1024 * 1024),
        name="pack",
    )(keys.reshape(flat.shape), values.reshape(flat.shape), positions.reshape(1, tokens))
    q = (
        queries.reshape(2, RUN, heads_kv, group, head_dim)
        .transpose(0, 2, 1, 3, 4)
        .reshape(2, heads_kv, RUN * group, head_dim)
    )

    attention = Attention(q, group, half, 3 * inner if inner <= 4 else 2 * inner)
    state = attention.start(own)

    stage = own
    halves, theirs = [], []
    for n in range(chips - 1):
        following = along_z(stage)
        held = stage
        for step in range(bits):
            if n == 0 and step + 1 == bits:
                first = held
                held = tied(held, state[0])
            there = over_place(held, step)
            if n and step == 0:
                if n == 1:
                    kvs = [(halves[0][0], 1), theirs[0][0]]
                else:
                    kvs = [halves[n - 2][1], halves[n - 1][0], theirs[n - 2][-1]]
                state = attention.add(state, kvs)
                there = tied(there, state[0])
            if step + 1 < bits:
                held = jnp.concatenate([held, there])
        halves.append((held, there))
        if n == 0:
            theirs.append([other_core(tied(first, following)), other_core(there)])
            stage = following
            continue
        held = jnp.concatenate([held, there])
        if n + 2 == chips:
            state = attention.add(state, [halves[n - 1][1], theirs[n - 1][-1], halves[n][0]])
            held = tied(held, state[0])
        theirs.append([other_core(held)])
        stage = following

    found = [stage]
    for step in range(bits):
        found += [over_place(x, step) for x in found]
    *most, final = found
    crossed = over_place(found[inner // 2 - 1], bits - 1, cross=1)
    most = jnp.concatenate(most)
    their_most = other_core(most)
    rest = [halves[-1][1], theirs[-1][-1], most, their_most]
    for kvs in [rest] if inner <= 4 else [rest[:2], rest[2:]]:
        state = attention.add(state, kvs)
    last = [tied(x, state[0]) for x in (final, crossed)]
    out = jax.ShapeDtypeStruct(queries.shape, queries.dtype)
    return attention.add(state, last, keep=1, out=out)


def solution(mesh):
    in_specs = (
        P(("outer", "inner"), None, None),
        P(("outer", "inner"), None, None),
        P(("outer", "inner"), None, None),
        P(("outer", "inner")),
    )
    out_specs = P(("outer", "inner"), None, None)
    return jax.shard_map(
        per_device, mesh=mesh, in_specs=in_specs, out_specs=out_specs, check_vma=False
    )
```

```python
import functools
import math

import jax
import jax.numpy as jnp
from jax import lax
from jax.experimental import pallas as pl
from jax.experimental.pallas import tpu as pltpu
from jax.sharding import PartitionSpec as P

RUN = 64
TILE = 8
KEEP = 4
AXES = ("outer", "inner")


def flash(score, v, state, factor, live=None):
    top, mixed = state
    keys = score.shape[1]
    if isinstance(live, int):
        lane = lax.broadcasted_iota(jnp.int32, score.shape, 1)
        keys, live = live, lane < live
    if live is not None:
        score = jnp.where(live, score, -jnp.inf)
    parts = [score[:, c : c + 128] for c in range(0, score.shape[1], 128)]
    new = jnp.max(functools.reduce(jnp.maximum, parts), axis=1, keepdims=True)
    if top is None:
        new = jnp.broadcast_to(new, parts[0].shape)
    else:
        new = jnp.maximum(top, new)
    weights = [
        jnp.exp2((part - new) * factor).astype(jnp.bfloat16) for part in parts
    ]
    weights = jnp.concatenate(weights, axis=1)
    ones = jnp.ones((keys, 128), v.dtype)
    part_mixed = jnp.dot(
        weights[:, :keys],
        jnp.concatenate([v, ones], axis=1),
        preferred_element_type=jnp.float32,
    )
    if top is None:
        return new, part_mixed
    decay = jnp.exp2((top - new) * factor)
    halves = [
        mixed[:, c : c + 128] * decay + part_mixed[:, c : c + 128]
        for c in range(0, mixed.shape[1], 128)
    ]
    return new, jnp.concatenate(halves, axis=1)


def head_tile(q_ref, state_refs, a, keys, values, factor, live=None):
    def scores(h):
        return lax.dot_general(
            q_ref[a, h],
            keys(h),
            (((1,), (1,)), ((), ())),
            preferred_element_type=jnp.float32,
        )

    heads_kv = q_ref.shape[1]
    ahead = scores(0)
    for h in range(heads_kv):
        score = ahead
        if h + 1 < heads_kv:
            ahead = scores(h + 1)
        state = (None, None)
        if live is None or isinstance(live, int):
            state = tuple(ref[a, h] for ref in state_refs)
        state = flash(score, values(h), state, factor, live)
        for ref, value in zip(state_refs, state):
            ref[a, h] = value


def own_kernel(group, factor, half, q_ref, own_ref, meta_ref, *refs):
    heads_kv, rows, head_dim = q_ref.shape[1:]
    state_refs = refs[:2]
    run_rows = 2 * heads_kv * RUN

    ids = own_ref[2 * run_rows :].astype(jnp.float32)
    lane = lax.broadcasted_iota(jnp.int32, ids.shape, 1)
    numbers = [jnp.max(jnp.where(lane // RUN == a, ids, 0.0)) for a in range(2)]
    row = lax.broadcasted_iota(jnp.int32, meta_ref.shape, 0)
    meta_ref[...] = jnp.where(
        row == 0, numbers[0], jnp.where(row == 1, numbers[1], 0.0)
    )

    row_at = lax.broadcasted_iota(jnp.int32, (rows, 2 * RUN), 0) // group
    key_at = lax.broadcasted_iota(jnp.int32, (rows, 2 * RUN), 1)
    for a in range(2):
        mine, other = numbers[a], numbers[1 - a]
        seen = (other < mine) & ((other >= half) == (mine >= half))
        reach = jnp.where(seen, RUN, 0)
        if a == 0:
            live = (key_at <= row_at) | ((key_at >= RUN) & (key_at < RUN + reach))
        else:
            live = (key_at < reach) | ((key_at >= RUN) & (key_at - RUN <= row_at))

        def own(g):
            starts = [g * RUN, run_rows + g * RUN]
            return jnp.concatenate([own_ref[n : n + RUN] for n in starts])

        head_tile(q_ref, state_refs, a, own, lambda h: own(heads_kv + h), factor, live)


def attend_kernel(group, factor, half, last, keep, blocks, q_ref, *refs):
    heads_kv, rows, head_dim = q_ref.shape[1:]
    run_rows = 2 * heads_kv * RUN
    block_rows = 2 * run_rows + 16
    kv_refs, refs = refs[: len(blocks)], refs[len(blocks) :]
    refs = refs[4:]
    if last:
        out_ref, refs = refs[0], refs[1:]
    meta_ref, *state_refs, buf = refs[:4]

    meta = meta_ref[...]
    counts = tuple(
        jnp.max(meta[2 + a : 3 + a]).astype(jnp.int32) for a in range(2)
    )
    seen_bits = []
    for ref, (skip, end) in zip(kv_refs, blocks):
        assert end - skip <= 8
        ids = jnp.concatenate(
            [ref[n * block_rows - 16 : n * block_rows] for n in range(skip + 1, end + 1)]
        ).astype(jnp.float32)
        row = lax.broadcasted_iota(jnp.int32, ids.shape, 0)
        lane = lax.broadcasted_iota(jnp.int32, ids.shape, 1)
        bit = jnp.left_shift(1, 2 * (row // 16) + lane // RUN)
        bit = jnp.where((row % 16 == 0) & (lane % RUN == 0), bit, 0).astype(jnp.float32)
        found = []
        for a in range(2):
            mine = meta[a : a + 1]
            low = jnp.where(mine >= half, float(half), 0.0)
            seen = (ids < mine) & (ids >= low)
            found.append(jnp.sum(jnp.where(seen, bit, 0.0)).astype(jnp.int32))
        seen_bits.append(found)

    for ref, (skip, end), bits in zip(kv_refs, blocks, seen_bits):

        def gather(n, counts):
            at = pl.multiple_of((skip + n // 2) * block_rows + n % 2 * run_rows, 16)
            fresh = []
            for a in range(2):
                flag = (bits[a] >> n) & 1
                count = counts[a]

                @pl.when(flag == 1)
                def _():
                    buf[a, count] = ref[pl.ds(at, run_rows), :]

                fresh.append(count + flag)
            return tuple(fresh)

        counts = lax.fori_loop(0, 2 * (end - skip), gather, counts)

    def some_runs(a, start, runs):
        def rows_of(g):
            found = buf[a, pl.ds(start, runs), g * RUN : (g + 1) * RUN, :]
            return found.reshape(runs * RUN, -1)

        def keys(h):
            if runs > 1:
                return rows_of(h)
            return jnp.concatenate([rows_of(h), jnp.zeros((RUN, head_dim), buf.dtype)])

        live = RUN if runs == 1 else None
        head_tile(
            q_ref, state_refs, a, keys, lambda h: rows_of(heads_kv + h), factor, live
        )

    whole = [count // TILE for count in counts]

    def step(item, carry):
        a = (item >= whole[0]).astype(jnp.int32)
        some_runs(a, (item - a * whole[0]) * TILE, TILE)
        return carry

    lax.fori_loop(0, whole[0] + whole[1], step, 0)

    def remainder(a, carry):
        count = jnp.where(a == 0, counts[0], counts[1])
        start = count // TILE * TILE
        runs = TILE // 2
        while runs >= keep:

            @pl.when(count & runs != 0)
            def _():
                some_runs(a, start, runs)

            start = start + (count & runs)
            runs //= 2
        return carry

    lax.fori_loop(0, 2, remainder, 0)

    if not last:
        row = lax.broadcasted_iota(jnp.int32, meta.shape, 0)
        for a in range(2):
            start = counts[a] // keep * keep
            rest = counts[a] - start
            if keep > 1:

                @pl.when((start > 0) & (rest > 0))
                def _():
                    for n in range(keep - 1):
                        buf[a, n] = buf[a, start + n]

            meta = jnp.where(row == 2 + a, rest.astype(jnp.float32), meta)
        meta_ref[...] = meta
        return

    made, sems = refs[4:]
    copies = []
    for a in range(2):
        for h in range(0, heads_kv, 2):
            done = []
            for g in (h, h + 1):
                mixed = state_refs[1][a, g]
                part = mixed[:, :head_dim] * (1.0 / mixed[:, head_dim:])
                done.append(part.reshape(RUN, group, -1))
            place = (slice(a * RUN, (a + 1) * RUN), slice(h * group, (h + 2) * group))
            made[place] = jnp.concatenate(done, axis=1).astype(out_ref.dtype)
            copy = pltpu.make_async_copy(
                made.at[place], out_ref.at[place], sems.at[len(copies)]
            )
            copy.start()
            copies.append(copy)
    for copy in copies:
        copy.wait()


def pack_kernel(
    k_any, v_any, positions_any, own_any, k_ref, v_ref, positions_ref, own_ref, sems
):
    pairs = ((k_any, k_ref), (v_any, v_ref), (positions_any, positions_ref))
    copies = [
        pltpu.make_async_copy(source, target, sems.at[n])
        for n, (source, target) in enumerate(pairs)
    ]
    for copy in copies:
        copy.start()
    heads_kv = k_ref.shape[0] // (2 * RUN)
    rows = heads_kv * RUN
    at = lax.broadcasted_iota(jnp.int32, (rows, rows), 0)
    origin = lax.broadcasted_iota(jnp.int32, (rows, rows), 1)
    move = at % RUN * heads_kv + at // RUN == origin
    move = jnp.where(move, 1.0, 0.0).astype(k_ref.dtype)
    for n, ref in enumerate((k_ref, v_ref)):
        copies[n].wait()
        for r in range(2):
            moved = jnp.dot(
                move,
                ref[r * rows : (r + 1) * rows],
                preferred_element_type=jnp.float32,
            )
            start = (2 * r + n) * rows
            own_ref[start : start + rows] = moved.astype(own_ref.dtype)
            place = slice(start, start + rows)
            copy = pltpu.make_async_copy(
                own_ref.at[place], own_any.at[place], sems.at[len(copies)]
            )
            copy.start()
            copies.append(copy)
    copies[2].wait()
    numbers = (positions_ref[...] // RUN).astype(jnp.float32)
    numbers = jnp.broadcast_to(numbers, (16, numbers.shape[1]))
    own_ref[4 * rows :] = numbers.astype(own_ref.dtype)
    place = slice(4 * rows, 4 * rows + 16)
    copy = pltpu.make_async_copy(
        own_ref.at[place], own_any.at[place], sems.at[len(copies)]
    )
    copy.start()
    for copy in copies[3:] + [copy]:
        copy.wait()


class Attention:
    def __init__(self, q, group, half, room):
        self.q, self.group, self.half = q, group, half
        self.factor = math.log2(math.e) / math.sqrt(q.shape[3])
        heads_kv, rows, head_dim = q.shape[1:]
        self.block_rows = 4 * heads_kv * RUN + 16
        slots = 2 * room + TILE
        self.carried = [jax.ShapeDtypeStruct((8, 128), jnp.float32)]
        self.carried += [
            jax.ShapeDtypeStruct((2, heads_kv, rows, n), jnp.float32)
            for n in (128, head_dim + 128)
        ]
        self.carried.append(
            jax.ShapeDtypeStruct((2, slots, 2 * heads_kv * RUN, head_dim), q.dtype)
        )

    def call(self, kernel, operands, shapes, aliases, count, name, out=None):
        vmem = pl.BlockSpec(memory_space=pltpu.VMEM)
        out_specs = [vmem] * len(shapes)
        scratch = []
        if out is not None:
            shapes = [out, *shapes]
            out_specs.insert(0, pl.BlockSpec(memory_space=pl.ANY))
            scratch = [pltpu.VMEM(out.shape, out.dtype), pltpu.SemaphoreType.DMA((8,))]
        return pl.pallas_call(
            kernel,
            out_shape=shapes,
            in_specs=[vmem] * len(operands),
            out_specs=out_specs,
            scratch_shapes=scratch,
            input_output_aliases=aliases,
            compiler_params=pltpu.CompilerParams(vmem_limit_bytes=28 * 1024 * 1024),
            cost_estimate=pl.CostEstimate(
                flops=count * RUN * self.q.size * 4,
                bytes_accessed=self.q.size * 8,
                transcendentals=0,
            ),
            name=name,
        )(*operands)

    def start(self, own):
        kernel = functools.partial(own_kernel, self.group, self.factor, self.half)
        return self.call(kernel, [self.q, own], self.carried, {}, 2, "attend_own")

    def add(self, state, kvs, keep=KEEP, out=None):
        kvs = [x if isinstance(x, tuple) else (x, 0) for x in kvs]
        blocks = [(skip, x.shape[0] // self.block_rows) for x, skip in kvs]
        count = sum(end - skip for skip, end in blocks)
        operands = [self.q, *(x for x, _ in kvs), *state]
        first, ahead = 1 + len(kvs), int(out is not None)
        aliases = {first + n: ahead + n for n in range(len(state))}
        kernel = functools.partial(
            attend_kernel, self.group, self.factor, self.half, ahead, keep, blocks
        )
        results = self.call(kernel, operands, self.carried, aliases, count, "attend", out)
        return results[0] if ahead else results


def per_device(queries, keys, values, positions):
    outer, inner = lax.axis_size("outer"), lax.axis_size("inner")
    tokens, heads_q, head_dim = queries.shape
    heads_kv = keys.shape[1]
    group = heads_q // heads_kv
    half = tokens // RUN * outer * inner // 2

    chips = outer // 2
    bits = inner.bit_length() - 1
    ring = [0] + list(range(1, chips, 2)) + list(range(2, chips, 2))[::-1]
    after = {ring[n]: ring[(n + 1) % chips] for n in range(chips)}

    def permute(x, to):
        pairs = []
        for z in range(chips):
            for core in range(2):
                for place in range(inner):
                    nz, ncore, nplace = to(z, core, place)
                    pairs.append(
                        (
                            (2 * z + core) * inner + place,
                            (2 * nz + ncore) * inner + nplace,
                        )
                    )
        return lax.ppermute(x, AXES, pairs)

    def along_z(x):
        return permute(x, lambda z, core, place: (after[z], core, place))

    def over_place(x, step, cross=0):
        def to(z, core, place):
            bit = bits - 1 - step if core else step
            return z, core ^ cross, place ^ (1 << bit)

        return permute(x, to)

    def other_core(x):
        return permute(x, lambda z, core, place: (z, 1 - core, place))

    def tied(x, *others):
        return lax.optimization_barrier((x, *others))[0]

    flat = jax.ShapeDtypeStruct((tokens * heads_kv, head_dim), keys.dtype)
    own = pl.pallas_call(
        pack_kernel,
        out_shape=jax.ShapeDtypeStruct(
            (2 * tokens * heads_kv + 16, head_dim), keys.dtype
        ),
        in_specs=[pl.BlockSpec(memory_space=pltpu.HBM)] * 3,
        out_specs=pl.BlockSpec(memory_space=pltpu.HBM),
        scratch_shapes=[
            pltpu.VMEM(flat.shape, flat.dtype),
            pltpu.VMEM(flat.shape, flat.dtype),
            pltpu.VMEM((1, tokens), jnp.int32),
            pltpu.VMEM((2 * tokens * heads_kv + 16, head_dim), keys.dtype),
            pltpu.SemaphoreType.DMA((8,)),
        ],
        compiler_params=pltpu.CompilerParams(vmem_limit_bytes=60 * 1024 * 1024),
        name="pack",
    )(keys.reshape(flat.shape), values.reshape(flat.shape), positions.reshape(1, tokens))
    q = (
        queries.reshape(2, RUN, heads_kv, group, head_dim)
        .transpose(0, 2, 1, 3, 4)
        .reshape(2, heads_kv, RUN * group, head_dim)
    )

    attention = Attention(q, group, half, 3 * inner if inner <= 4 else 2 * inner)
    state = attention.start(own)

    stage = own
    halves, theirs = [], []
    for n in range(chips - 1):
        following = along_z(stage)
        held = stage
        for step in range(bits):
            if n == 0 and step + 1 == bits:
                first = held
                held = tied(held, state[0])
            there = over_place(held, step)
            if n and step == 0:
                if n == 1:
                    kvs = [(halves[0][0], 1), theirs[0][0]]
                else:
                    kvs = [halves[n - 2][1], halves[n - 1][0], theirs[n - 2][-1]]
                state = attention.add(state, kvs)
                there = tied(there, state[0])
            if step + 1 < bits:
                held = jnp.concatenate([held, there])
        halves.append((held, there))
        if n == 0:
            theirs.append([other_core(tied(first, following)), other_core(there)])
            stage = following
            continue
        held = jnp.concatenate([held, there])
        if n + 2 == chips:
            state = attention.add(state, [halves[n - 1][1], theirs[n - 1][-1], halves[n][0]])
            held = tied(held, state[0])
        theirs.append([other_core(held)])
        stage = following

    found = [stage]
    for step in range(bits):
        found += [over_place(x, step) for x in found]
    *most, final = found
    crossed = over_place(found[inner // 2 - 1], bits - 1, cross=1)
    most = jnp.concatenate(most)
    their_most = other_core(most)
    rest = [halves[-1][1], theirs[-1][-1], most, their_most]
    for kvs in [rest] if inner <= 4 else [rest[:2], rest[2:]]:
        state = attention.add(state, kvs, keep=2)
    last = [tied(x, state[0]) for x in (final, crossed)]
    out = jax.ShapeDtypeStruct(queries.shape, queries.dtype)
    return attention.add(state, last, keep=1, out=out)


def solution(mesh):
    in_specs = (
        P(("outer", "inner"), None, None),
        P(("outer", "inner"), None, None),
        P(("outer", "inner"), None, None),
        P(("outer", "inner")),
    )
    out_specs = P(("outer", "inner"), None, None)
    return jax.shard_map(
        per_device, mesh=mesh, in_specs=in_specs, out_specs=out_specs, check_vma=False
    )
```

```python
import functools
import math

import jax
import jax.numpy as jnp
from jax import lax
from jax.experimental import pallas as pl
from jax.experimental.pallas import tpu as pltpu
from jax.sharding import PartitionSpec as P

RUN = 64
TILE = 8
KEEP = 4
AXES = ("outer", "inner")


def flash(score, v, state, factor, live=None):
    top, mixed = state
    keys = score.shape[1]
    if isinstance(live, int):
        lane = lax.broadcasted_iota(jnp.int32, score.shape, 1)
        keys, live = live, lane < live
    if live is not None:
        score = jnp.where(live, score, -jnp.inf)
    parts = [score[:, c : c + 128] for c in range(0, score.shape[1], 128)]
    new = jnp.max(functools.reduce(jnp.maximum, parts), axis=1, keepdims=True)
    if top is None:
        new = jnp.broadcast_to(new, parts[0].shape)
    else:
        new = jnp.maximum(top, new)
    weights = [
        jnp.exp2((part - new) * factor).astype(jnp.bfloat16) for part in parts
    ]
    weights = jnp.concatenate(weights, axis=1)
    ones = jnp.ones((keys, 128), v.dtype)
    part_mixed = jnp.dot(
        weights[:, :keys],
        jnp.concatenate([v, ones], axis=1),
        preferred_element_type=jnp.float32,
    )
    if top is None:
        return new, part_mixed
    decay = jnp.exp2((top - new) * factor)
    halves = [
        mixed[:, c : c + 128] * decay + part_mixed[:, c : c + 128]
        for c in range(0, mixed.shape[1], 128)
    ]
    return new, jnp.concatenate(halves, axis=1)


def head_tile(q_ref, state_refs, a, keys, values, factor, live=None):
    def scores(h):
        return lax.dot_general(
            q_ref[a, h],
            keys(h),
            (((1,), (1,)), ((), ())),
            preferred_element_type=jnp.float32,
        )

    heads_kv = q_ref.shape[1]
    ahead = scores(0)
    for h in range(heads_kv):
        score = ahead
        if h + 1 < heads_kv:
            ahead = scores(h + 1)
        state = (None, None)
        if live is None or isinstance(live, int):
            state = tuple(ref[a, h] for ref in state_refs)
        state = flash(score, values(h), state, factor, live)
        for ref, value in zip(state_refs, state):
            ref[a, h] = value


def own_kernel(group, factor, half, q_ref, own_ref, meta_ref, *refs):
    heads_kv, rows, head_dim = q_ref.shape[1:]
    state_refs = refs[:2]
    run_rows = 2 * heads_kv * RUN

    ids = own_ref[2 * run_rows :].astype(jnp.float32)
    lane = lax.broadcasted_iota(jnp.int32, ids.shape, 1)
    numbers = [jnp.max(jnp.where(lane // RUN == a, ids, 0.0)) for a in range(2)]
    row = lax.broadcasted_iota(jnp.int32, meta_ref.shape, 0)
    meta_ref[...] = jnp.where(
        row == 0, numbers[0], jnp.where(row == 1, numbers[1], 0.0)
    )

    row_at = lax.broadcasted_iota(jnp.int32, (rows, 2 * RUN), 0) // group
    key_at = lax.broadcasted_iota(jnp.int32, (rows, 2 * RUN), 1)
    for a in range(2):
        mine, other = numbers[a], numbers[1 - a]
        seen = (other < mine) & ((other >= half) == (mine >= half))
        reach = jnp.where(seen, RUN, 0)
        if a == 0:
            live = (key_at <= row_at) | ((key_at >= RUN) & (key_at < RUN + reach))
        else:
            live = (key_at < reach) | ((key_at >= RUN) & (key_at - RUN <= row_at))

        def own(g):
            starts = [g * RUN, run_rows + g * RUN]
            return jnp.concatenate([own_ref[n : n + RUN] for n in starts])

        head_tile(q_ref, state_refs, a, own, lambda h: own(heads_kv + h), factor, live)


def attend_kernel(group, factor, half, last, keep, blocks, q_ref, *refs):
    heads_kv, rows, head_dim = q_ref.shape[1:]
    run_rows = 2 * heads_kv * RUN
    block_rows = 2 * run_rows + 16
    kv_refs, refs = refs[: len(blocks)], refs[len(blocks) :]
    refs = refs[4:]
    if last:
        out_ref, refs = refs[0], refs[1:]
    meta_ref, *state_refs, buf = refs[:4]

    meta = meta_ref[...]
    counts = tuple(
        jnp.max(meta[2 + a : 3 + a]).astype(jnp.int32) for a in range(2)
    )
    seen_bits = []
    for ref, (skip, end) in zip(kv_refs, blocks):
        assert end - skip <= 8
        ids = jnp.concatenate(
            [ref[n * block_rows - 16 : n * block_rows] for n in range(skip + 1, end + 1)]
        ).astype(jnp.float32)
        row = lax.broadcasted_iota(jnp.int32, ids.shape, 0)
        lane = lax.broadcasted_iota(jnp.int32, ids.shape, 1)
        bit = jnp.left_shift(1, 2 * (row // 16) + lane // RUN)
        bit = jnp.where((row % 16 == 0) & (lane % RUN == 0), bit, 0).astype(jnp.float32)
        found = []
        for a in range(2):
            mine = meta[a : a + 1]
            low = jnp.where(mine >= half, float(half), 0.0)
            seen = (ids < mine) & (ids >= low)
            found.append(jnp.sum(jnp.where(seen, bit, 0.0)).astype(jnp.int32))
        seen_bits.append(found)

    for ref, (skip, end), bits in zip(kv_refs, blocks, seen_bits):

        def gather(n, counts):
            at = pl.multiple_of((skip + n // 2) * block_rows + n % 2 * run_rows, 16)
            fresh = []
            for a in range(2):
                flag = (bits[a] >> n) & 1
                count = counts[a]

                @pl.when(flag == 1)
                def _():
                    buf[a, count] = ref[pl.ds(at, run_rows), :]

                fresh.append(count + flag)
            return tuple(fresh)

        counts = lax.fori_loop(0, 2 * (end - skip), gather, counts)

    def some_runs(a, start, runs):
        def rows_of(g):
            found = buf[a, pl.ds(start, runs), g * RUN : (g + 1) * RUN, :]
            return found.reshape(runs * RUN, -1)

        def keys(h):
            if runs > 1:
                return rows_of(h)
            return jnp.concatenate([rows_of(h), jnp.zeros((RUN, head_dim), buf.dtype)])

        live = RUN if runs == 1 else None
        head_tile(
            q_ref, state_refs, a, keys, lambda h: rows_of(heads_kv + h), factor, live
        )

    whole = [count // TILE for count in counts]

    def step(item, carry):
        a = (item >= whole[0]).astype(jnp.int32)
        some_runs(a, (item - a * whole[0]) * TILE, TILE)
        return carry

    lax.fori_loop(0, whole[0] + whole[1], step, 0)

    def remainder(a, carry):
        count = counts[a] if isinstance(a, int) else jnp.where(a == 0, *counts)
        start = count // TILE * TILE
        runs = TILE // 2
        while runs >= keep:

            @pl.when(count & runs != 0)
            def _():
                some_runs(a, start, runs)

            start = start + (count & runs)
            runs //= 2
        return carry

    if not last:
        lax.fori_loop(0, 2, remainder, 0)

    if not last:
        row = lax.broadcasted_iota(jnp.int32, meta.shape, 0)
        for a in range(2):
            start = counts[a] // keep * keep
            rest = counts[a] - start
            if keep > 1:

                @pl.when((start > 0) & (rest > 0))
                def _():
                    for n in range(keep - 1):
                        buf[a, n] = buf[a, start + n]

            meta = jnp.where(row == 2 + a, rest.astype(jnp.float32), meta)
        meta_ref[...] = meta
        return

    made, sems = refs[4:]
    copies = []
    for a in range(2):
        remainder(a, 0)
        for h in range(0, heads_kv, 2):
            done = []
            for g in (h, h + 1):
                mixed = state_refs[1][a, g]
                part = mixed[:, :head_dim] * (1.0 / mixed[:, head_dim:])
                done.append(part.reshape(RUN, group, -1))
            place = (slice(a * RUN, (a + 1) * RUN), slice(h * group, (h + 2) * group))
            made[place] = jnp.concatenate(done, axis=1).astype(out_ref.dtype)
            copy = pltpu.make_async_copy(
                made.at[place], out_ref.at[place], sems.at[len(copies)]
            )
            copy.start()
            copies.append(copy)
    for copy in copies:
        copy.wait()


def pack_kernel(
    k_any, v_any, positions_any, own_any, k_ref, v_ref, positions_ref, own_ref, sems
):
    pairs = ((k_any, k_ref), (v_any, v_ref), (positions_any, positions_ref))
    copies = [
        pltpu.make_async_copy(source, target, sems.at[n])
        for n, (source, target) in enumerate(pairs)
    ]
    for copy in copies:
        copy.start()
    heads_kv = k_ref.shape[0] // (2 * RUN)
    rows = heads_kv * RUN
    at = lax.broadcasted_iota(jnp.int32, (rows, rows), 0)
    origin = lax.broadcasted_iota(jnp.int32, (rows, rows), 1)
    move = (at & (RUN - 1)) * heads_kv + (at >> (RUN.bit_length() - 1)) == origin
    move = jnp.where(move, 1.0, 0.0).astype(k_ref.dtype)
    for n, ref in enumerate((k_ref, v_ref)):
        copies[n].wait()
        for r in range(2):
            moved = jnp.dot(
                move,
                ref[r * rows : (r + 1) * rows],
                preferred_element_type=jnp.float32,
            )
            start = (2 * r + n) * rows
            own_ref[start : start + rows] = moved.astype(own_ref.dtype)
            place = slice(start, start + rows)
            copy = pltpu.make_async_copy(
                own_ref.at[place], own_any.at[place], sems.at[len(copies)]
            )
            copy.start()
            copies.append(copy)
    copies[2].wait()
    numbers = (positions_ref[...] // RUN).astype(jnp.float32)
    numbers = jnp.broadcast_to(numbers, (16, numbers.shape[1]))
    own_ref[4 * rows :] = numbers.astype(own_ref.dtype)
    place = slice(4 * rows, 4 * rows + 16)
    copy = pltpu.make_async_copy(
        own_ref.at[place], own_any.at[place], sems.at[len(copies)]
    )
    copy.start()
    for copy in copies[3:] + [copy]:
        copy.wait()


class Attention:
    def __init__(self, q, group, half, room):
        self.q, self.group, self.half = q, group, half
        self.factor = math.log2(math.e) / math.sqrt(q.shape[3])
        heads_kv, rows, head_dim = q.shape[1:]
        self.block_rows = 4 * heads_kv * RUN + 16
        slots = 2 * room + TILE
        self.carried = [jax.ShapeDtypeStruct((8, 128), jnp.float32)]
        self.carried += [
            jax.ShapeDtypeStruct((2, heads_kv, rows, n), jnp.float32)
            for n in (128, head_dim + 128)
        ]
        self.carried.append(
            jax.ShapeDtypeStruct((2, slots, 2 * heads_kv * RUN, head_dim), q.dtype)
        )

    def call(self, kernel, operands, shapes, aliases, count, name, out=None):
        vmem = pl.BlockSpec(memory_space=pltpu.VMEM)
        out_specs = [vmem] * len(shapes)
        scratch = []
        if out is not None:
            shapes = [out, *shapes]
            out_specs.insert(0, pl.BlockSpec(memory_space=pl.ANY))
            scratch = [pltpu.VMEM(out.shape, out.dtype), pltpu.SemaphoreType.DMA((8,))]
        return pl.pallas_call(
            kernel,
            out_shape=shapes,
            in_specs=[vmem] * len(operands),
            out_specs=out_specs,
            scratch_shapes=scratch,
            input_output_aliases=aliases,
            compiler_params=pltpu.CompilerParams(vmem_limit_bytes=28 * 1024 * 1024),
            cost_estimate=pl.CostEstimate(
                flops=count * RUN * self.q.size * 4,
                bytes_accessed=self.q.size * 8,
                transcendentals=0,
            ),
            name=name,
        )(*operands)

    def start(self, own):
        kernel = functools.partial(own_kernel, self.group, self.factor, self.half)
        return self.call(kernel, [self.q, own], self.carried, {}, 2, "attend_own")

    def add(self, state, kvs, keep=KEEP, out=None):
        kvs = [x if isinstance(x, tuple) else (x, 0) for x in kvs]
        blocks = [(skip, x.shape[0] // self.block_rows) for x, skip in kvs]
        count = sum(end - skip for skip, end in blocks)
        operands = [self.q, *(x for x, _ in kvs), *state]
        first, ahead = 1 + len(kvs), int(out is not None)
        aliases = {first + n: ahead + n for n in range(len(state))}
        kernel = functools.partial(
            attend_kernel, self.group, self.factor, self.half, ahead, keep, blocks
        )
        results = self.call(kernel, operands, self.carried, aliases, count, "attend", out)
        return results[0] if ahead else results


def per_device(queries, keys, values, positions):
    outer, inner = lax.axis_size("outer"), lax.axis_size("inner")
    tokens, heads_q, head_dim = queries.shape
    heads_kv = keys.shape[1]
    group = heads_q // heads_kv
    half = tokens // RUN * outer * inner // 2

    chips = outer // 2
    bits = inner.bit_length() - 1
    ring = [0] + list(range(1, chips, 2)) + list(range(2, chips, 2))[::-1]
    after = {ring[n]: ring[(n + 1) % chips] for n in range(chips)}

    def permute(x, to):
        pairs = []
        for z in range(chips):
            for core in range(2):
                for place in range(inner):
                    nz, ncore, nplace = to(z, core, place)
                    pairs.append(
                        (
                            (2 * z + core) * inner + place,
                            (2 * nz + ncore) * inner + nplace,
                        )
                    )
        return lax.ppermute(x, AXES, pairs)

    def along_z(x):
        return permute(x, lambda z, core, place: (after[z], core, place))

    def over_place(x, step, cross=0):
        def to(z, core, place):
            bit = bits - 1 - step if core else step
            return z, core ^ cross, place ^ (1 << bit)

        return permute(x, to)

    def other_core(x):
        return permute(x, lambda z, core, place: (z, 1 - core, place))

    def tied(x, *others):
        return lax.optimization_barrier((x, *others))[0]

    flat = jax.ShapeDtypeStruct((tokens * heads_kv, head_dim), keys.dtype)
    own = pl.pallas_call(
        pack_kernel,
        out_shape=jax.ShapeDtypeStruct(
            (2 * tokens * heads_kv + 16, head_dim), keys.dtype
        ),
        in_specs=[pl.BlockSpec(memory_space=pltpu.HBM)] * 3,
        out_specs=pl.BlockSpec(memory_space=pltpu.HBM),
        scratch_shapes=[
            pltpu.VMEM(flat.shape, flat.dtype),
            pltpu.VMEM(flat.shape, flat.dtype),
            pltpu.VMEM((1, tokens), jnp.int32),
            pltpu.VMEM((2 * tokens * heads_kv + 16, head_dim), keys.dtype),
            pltpu.SemaphoreType.DMA((8,)),
        ],
        compiler_params=pltpu.CompilerParams(vmem_limit_bytes=60 * 1024 * 1024),
        name="pack",
    )(keys.reshape(flat.shape), values.reshape(flat.shape), positions.reshape(1, tokens))
    q = (
        queries.reshape(2, RUN, heads_kv, group, head_dim)
        .transpose(0, 2, 1, 3, 4)
        .reshape(2, heads_kv, RUN * group, head_dim)
    )

    attention = Attention(q, group, half, 3 * inner if inner <= 4 else 2 * inner)
    state = attention.start(own)

    stage = own
    halves, theirs = [], []
    for n in range(chips - 1):
        following = along_z(stage)
        held = stage
        for step in range(bits):
            if n == 0 and step + 1 == bits:
                first = held
                held = tied(held, state[0])
            there = over_place(held, step)
            if n and step == 0:
                if n == 1:
                    kvs = [(halves[0][0], 1), theirs[0][0]]
                else:
                    kvs = [halves[n - 2][1], halves[n - 1][0], theirs[n - 2][-1]]
                state = attention.add(state, kvs)
                there = tied(there, state[0])
            if step + 1 < bits:
                held = jnp.concatenate([held, there])
        halves.append((held, there))
        if n == 0:
            theirs.append([other_core(tied(first, following)), other_core(there)])
            stage = following
            continue
        held = jnp.concatenate([held, there])
        if n + 2 == chips:
            state = attention.add(state, [halves[n - 1][1], theirs[n - 1][-1], halves[n][0]])
            held = tied(held, state[0])
        theirs.append([other_core(held)])
        stage = following

    found = [stage]
    for step in range(bits):
        found += [over_place(x, step) for x in found]
    *most, final = found
    crossed = over_place(found[inner // 2 - 1], bits - 1, cross=1)
    most = jnp.concatenate(most)
    their_most = other_core(most)
    rest = [halves[-1][1], theirs[-1][-1], most, their_most]
    for kvs in [rest] if inner <= 4 else [rest[:2], rest[2:]]:
        state = attention.add(state, kvs, keep=2)
    last = [tied(x, state[0]) for x in (final, crossed)]
    out = jax.ShapeDtypeStruct(queries.shape, queries.dtype)
    return attention.add(state, last, keep=1, out=out)


def solution(mesh):
    in_specs = (
        P(("outer", "inner"), None, None),
        P(("outer", "inner"), None, None),
        P(("outer", "inner"), None, None),
        P(("outer", "inner")),
    )
    out_specs = P(("outer", "inner"), None, None)
    return jax.shard_map(
        per_device, mesh=mesh, in_specs=in_specs, out_specs=out_specs, check_vma=False
    )
```
